32 devices in a mesh: group: 2 (over x), tensor: 16 (over z, y, core).
Axes of the slice: x: 2, y: 2, z: 4, core: 2. Of those that a mesh axis runs over, the one named last changes fastest.
Arguments:
- hidden: bfloat16 [192, 8192], P(('group', 'tensor')), parts along dimension 0, may hold values from -6 to 6
- input_norm_scale: bfloat16 [8192], replicated, may hold values from 0.099609375 to 1.8984375
- query_key_value_weight: bfloat16 [8192, 10240], P(None, 'tensor'), may hold values from -0.0625 to 0.0625
- projection_bias: bfloat16 [10240], P('tensor'), may hold values from -4 to 4
- rotated_key_cache: bfloat16 [192, 384, 1024], P(('group', 'tensor')), parts along dimension 0, may hold values from -3000 to 3000, as said below
- past_value_cache: bfloat16 [192, 384, 1024], P(('group', 'tensor')), parts along dimension 0, may hold values from -6 to 6
- lengths: int32 [192], P(('group', 'tensor')), parts along dimension 0, may hold values from 96 to 384, as said below
- row_adapter_index: int32 [192], P(('group', 'tensor')), parts along dimension 0, may hold values from 0 to 31
- output_weight: bfloat16 [8192, 8192], P(None, 'tensor'), may hold values from -0.25 to 0.25
- adapter_down_weight: bfloat16 [32, 8192, 16], P('tensor'), may hold values from -0.0625 to 0.0625
- adapter_up_weight: bfloat16 [32, 16, 8192], P(None, None, 'tensor'), may hold values from -3 to 3
Outputs:
- projected: bfloat16 [192, 8192], P(('group', 'tensor')), parts along dimension 0
The draws below stay inside these ranges and needn't reach their ends.
There are 2 independent parts, one for each index of `group`. The reference program is written for one: setup_inputs(seed, part) draws one part's arguments, and reference() takes and returns one part's arrays. A program takes and returns all parts, laid end to end along the dimension named above; an argument that names none is the same for every part. Nothing has to cross between parts.
Inputs may be any that keep to these rules, and one draw needn't show every extreme that they name: `lengths`: every row has at least 96 cached positions, and in every draw some row's cache is full. `rotated_key_cache`: keys are finite and of moderate size in most positions.
All inputs are finite; a program needn't handle non-finite values.
Results may differ from the reference program's by a relative error of at most 0.028.
Values may be sent and summed in bfloat16 or wider, within the bound.
No kernel may reach another device: no remote copies, remote signals or barrier semaphores. Data moves between devices by JAX's collectives and lax.ppermute only.
A program may use at most 128 MiB of HBM per device.

```python
import math
import jax
import jax.numpy as jnp
import numpy as np
from jax import lax

MODEL_WIDTH = 8192
QUERY_HEADS = 64
KVH = 8
HEAD_SIZE = 128
ADAPTER_RANK = 16
CTX = 384
ADAPTER_COUNT = 32
ROWS = 96
QKV_COLS = 10240


def draw_rotated_key_cache(key, part):
    key = jax.random.fold_in(key, 11)
    first_key = jax.random.fold_in(key, 0)
    values = jax.random.truncated_normal(first_key, -6.0, 6.0, (ROWS, CTX, KVH * HEAD_SIZE), jnp.float32)
    return values.astype(jnp.bfloat16)


def draw_lengths(key, part):
    key = jax.random.fold_in(key, 23)
    spread_key, full_key = jax.random.split(key)
    counts = jax.random.randint(spread_key, (ROWS,), CTX // 4, CTX + 1)
    chosen = jax.random.randint(full_key, (), 0, ROWS)
    return jnp.where(jnp.arange(ROWS) == chosen, CTX, counts).astype(jnp.int32)


def set_ends(values, own_key, low, high):
    shape = values.shape
    index_at = [jax.random.randint(jax.random.fold_in(own_key, axis), (), 0, shape[axis]) for axis in range(len(shape))]
    values = values.at[tuple(index_at)].set(low)
    longest = shape.index(max(shape))
    index_at[longest] = (index_at[longest] + 1) % shape[longest]
    return values.at[tuple(index_at)].set(high)


def shard_levels(rng, dims, cuts, least, high):
    loudness = 1.0
    for position, shards_of in cuts:
        steps = jax.random.uniform(jax.random.fold_in(jax.random.fold_in(rng, 6), position), (shards_of,), jnp.float32, least / len(cuts), high / len(cuts))
        loudness = loudness * jnp.repeat(jnp.exp(steps), dims[position] // shards_of).reshape((-1,) + (1,) * (len(dims) - 1 - position))
    return loudness


def rank_table(amount, slope):
    weights = [(1 << 20) // math.isqrt(rank ** slope) + 1 for rank in range(1, amount + 1)]
    width = 1 + sum(weights) // (1 << 30)
    return np.cumsum(np.array([max(1, weight // width) for weight in weights]))


def skewed_ids(own_key, shape, amount, skew):
    grid = rank_table(amount, skew)
    pick = jax.random.randint(jax.random.fold_in(own_key, 1), shape, 0, int(grid[amount - 1]))
    rank = jnp.searchsorted(jnp.asarray(grid, jnp.int32), pick, side="right")
    return jax.random.permutation(jax.random.fold_in(own_key, 2), amount)[rank].astype(jnp.int32)


def scatter_about(rng, dims, spread, bound, pieces=(), kind=jnp.bfloat16):
    gain = shard_levels(rng, dims, pieces, -0.22, 0.18) if pieces else 1.0
    entries = jax.random.normal(rng, dims, jnp.float32) * spread * gain
    return jnp.minimum(jnp.maximum(entries, -bound), bound).astype(kind)


def setup_inputs(seed: int = 0, part: int = 0) -> dict:
    streams_of = jax.random.split(jax.random.key(seed), 12)
    own_keys = jax.random.split(jax.random.fold_in(streams_of[11], part), 12)
    hidden = scatter_about(own_keys[0], (ROWS, MODEL_WIDTH), 1.0, 6.0, ((0, 16),))
    input_norm_scale = jnp.clip(1.0 + 0.18 * jax.random.normal(streams_of[1], (MODEL_WIDTH,), jnp.float32), 0.099609375, 1.8984375).astype(jnp.bfloat16)
    query_key_value_weight = scatter_about(streams_of[2], (MODEL_WIDTH, QKV_COLS), MODEL_WIDTH ** -0.5, 0.0625, ((1, 16),))
    projection_bias = scatter_about(streams_of[3], (QKV_COLS,), 0.7, 4.0, ((0, 16),))
    rotated_key_cache = draw_rotated_key_cache(jax.random.fold_in(jax.random.fold_in(streams_of[11], part), 71), part)
    past_value_cache = scatter_about(own_keys[5], (ROWS, CTX, KVH * HEAD_SIZE), 1.0, 6.0, ((0, 16),))
    lengths = draw_lengths(jax.random.fold_in(jax.random.fold_in(streams_of[11], part), 71), part)
    row_adapter_index = set_ends(skewed_ids(own_keys[7], (ROWS,), ADAPTER_COUNT, 2), jax.random.fold_in(own_keys[7], 3), 0, ADAPTER_COUNT - 1).astype(jnp.int32)
    output_weight = scatter_about(streams_of[8], (QUERY_HEADS * HEAD_SIZE, MODEL_WIDTH), (MODEL_WIDTH // 16) ** -0.5, 0.25, ((1, 16),))
    adapter_down_weight = scatter_about(streams_of[9], (ADAPTER_COUNT, QUERY_HEADS * HEAD_SIZE, ADAPTER_RANK), (QUERY_HEADS * HEAD_SIZE) ** -0.5, 0.0625, ((0, 16),))
    adapter_up_weight = scatter_about(streams_of[10], (ADAPTER_COUNT, ADAPTER_RANK, MODEL_WIDTH), (ADAPTER_RANK // 4) ** -0.5, 3.0, ((2, 16),))
    return dict(hidden=hidden, input_norm_scale=input_norm_scale, query_key_value_weight=query_key_value_weight, projection_bias=projection_bias, rotated_key_cache=rotated_key_cache, past_value_cache=past_value_cache, lengths=lengths, row_adapter_index=row_adapter_index, output_weight=output_weight, adapter_down_weight=adapter_down_weight, adapter_up_weight=adapter_up_weight)


EPS = 1e-06
ROPE_BASE = 1000000.0

def rope_tables(lengths):
    half = HEAD_SIZE // 2
    inv = ROPE_BASE ** (-(jnp.arange(half, dtype=jnp.float32) * 2.0 / HEAD_SIZE))
    angle = lengths.astype(jnp.float32)[:, None] * inv[None, :]
    return (jnp.cos(angle), jnp.sin(angle))

def rotate(heads, cosine, sine):
    half = HEAD_SIZE // 2
    first = heads[..., :half]
    second = heads[..., half:]
    cosine = cosine[:, None, :]
    sine = sine[:, None, :]
    return jnp.concatenate([first * cosine - second * sine, second * cosine + first * sine], axis=-1)

def attend_one(items):
    query, new_key, new_value, keys, values, length = items
    scale = 1.0 / HEAD_SIZE ** 0.5
    query_f = query.astype(jnp.float32)
    keys_f = keys.reshape(CTX, KVH, HEAD_SIZE).astype(jnp.float32)
    values_f = values.reshape(CTX, KVH, HEAD_SIZE).astype(jnp.float32)
    scores = jnp.einsum('kgd,tkd->kgt', query_f, keys_f) * scale
    own = jnp.einsum('kgd,kd->kg', query_f, new_key.astype(jnp.float32)) * scale
    valid = jnp.arange(CTX) < length
    top = jnp.maximum(lax.optimization_barrier(jnp.max(jnp.where(valid, scores, -1e+30), axis=-1)), own)
    expo = jnp.where(valid, jnp.exp(scores - top[..., None]), 0.0)
    expo_own = jnp.exp(own - top)
    total = lax.optimization_barrier(jnp.sum(expo, axis=-1)) + expo_own
    weights = (expo / total[..., None]).astype(jnp.bfloat16)
    weight_own = (expo_own / total).astype(jnp.bfloat16)
    mixed = jnp.einsum('kgt,tkd->kgd', weights.astype(jnp.float32), values_f)
    mixed = mixed + weight_own.astype(jnp.float32)[..., None] * new_value.astype(jnp.float32)[:, None, :]
    return mixed.reshape(QUERY_HEADS * HEAD_SIZE).astype(jnp.bfloat16)

def reference(hidden, input_norm_scale, query_key_value_weight, projection_bias, rotated_key_cache, past_value_cache, lengths, row_adapter_index, output_weight, adapter_down_weight, adapter_up_weight):
    groups = QUERY_HEADS // KVH
    hidden_f = hidden.astype(jnp.float32)
    normed = (hidden_f * lax.rsqrt(lax.optimization_barrier(jnp.mean(hidden_f * hidden_f, axis=-1, keepdims=True)) + EPS) * input_norm_scale.astype(jnp.float32)).astype(jnp.bfloat16)
    qkv = (jnp.dot(normed, query_key_value_weight, preferred_element_type=jnp.float32) + projection_bias.astype(jnp.float32)).astype(jnp.bfloat16)
    query = qkv[:, :QUERY_HEADS * HEAD_SIZE].astype(jnp.float32).reshape(ROWS, QUERY_HEADS, HEAD_SIZE)
    new_key = qkv[:, QUERY_HEADS * HEAD_SIZE:(QUERY_HEADS + KVH) * HEAD_SIZE].astype(jnp.float32).reshape(ROWS, KVH, HEAD_SIZE)
    new_value = qkv[:, (QUERY_HEADS + KVH) * HEAD_SIZE:].reshape(ROWS, KVH, HEAD_SIZE)
    cosine, sine = rope_tables(lengths)
    q_rot = rotate(query, cosine, sine).astype(jnp.bfloat16).reshape(ROWS, KVH, groups, HEAD_SIZE)
    k_rot = rotate(new_key, cosine, sine).astype(jnp.bfloat16)
    attn = lax.map(attend_one, (q_rot, k_rot, new_value, rotated_key_cache, past_value_cache, lengths))
    base = jnp.dot(attn, output_weight, preferred_element_type=jnp.float32)

    def shrink_one(items):
        row, row_index = items
        down_weight = lax.dynamic_index_in_dim(adapter_down_weight, row_index.astype(jnp.int32), 0, keepdims=False)
        return jnp.dot(row[None, :], down_weight, preferred_element_type=jnp.float32)[0]
    shrunk = lax.map(shrink_one, (attn, row_adapter_index)).astype(jnp.bfloat16)

    def expand_one(items):
        row_positions, row_index = items
        up_weight = lax.dynamic_index_in_dim(adapter_up_weight, row_index.astype(jnp.int32), 0, keepdims=False)
        return jnp.dot(row_positions[None, :], up_weight, preferred_element_type=jnp.float32)[0]
    delta = lax.map(expand_one, (shrunk, row_adapter_index))
    return (base + delta).astype(jnp.bfloat16)
```

```python
import functools

import jax
import jax.numpy as jnp
from jax import lax
from jax.experimental import pallas as pl
from jax.experimental.pallas import tpu as pltpu
from jax.sharding import PartitionSpec as P

QUERY_HEADS = 64
KVH = 8
HEAD_SIZE = 128
ADAPTER_RANK = 16
GROUPS = QUERY_HEADS // KVH

EPS = 1e-06
ROPE_BASE = 1000000.0

BLOCKS = 8
LANES = 128
MIB = 1 << 20

VMEM = pl.BlockSpec(memory_space=pltpu.VMEM)
ANY = pl.BlockSpec(memory_space=pl.ANY)
SMEM = pl.BlockSpec(memory_space=pltpu.SMEM)


def params(mib):
    return pltpu.CompilerParams(vmem_limit_bytes=mib * MIB)


def factors(chips):
    inner = 1
    while inner * inner * 4 <= chips and chips % (inner * 2) == 0:
        inner *= 2
    return chips // inner, inner


def ring_order(chips):
    outer, inner = factors(chips)
    if inner < 2 or outer % 2:
        return list(range(chips))
    order = [a * inner for a in range(outer)]
    for turn, a in enumerate(reversed(range(outer))):
        steps = range(1, inner) if turn % 2 == 0 else range(inner - 1, 0, -1)
        order += [a * inner + b for b in steps]
    return order


def lookup(table, index):
    value = jnp.int32(table[0])
    for at in range(1, len(table)):
        value = jnp.where(index == at, jnp.int32(table[at]), value)
    return value


def slot_chips(devices, me):
    chips = devices // 2
    order = ring_order(chips)
    place_of = [order.index(chip) for chip in range(chips)]
    place = lookup(place_of, lax.div(me, 2))
    ahead = chips // 2
    shifts = [0] + [-j for j in range(1, ahead + 1)] + [j for j in range(1, chips - ahead)]
    return [lookup(order, lax.rem(place + shift + chips, chips)) for shift in shifts]


def gather_chunks(chunk, devices):
    chips = devices // 2
    order = ring_order(chips)
    ahead = chips // 2

    def ring(step):
        return [
            (2 * order[p] + core, 2 * order[(p + step) % chips] + core)
            for p in range(chips)
            for core in range(2)
        ]

    across = [(d, d ^ 1) for d in range(devices)]
    up, down = ring(1), ring(-1)
    from_behind, from_front = [chunk], [chunk]
    other = {("up", 0): lax.ppermute(chunk, "tensor", across)}
    for j in range(1, ahead + 1):
        from_behind.append(lax.ppermute(from_behind[-1], "tensor", up))
        if j < chips - ahead:
            from_front.append(lax.ppermute(from_front[-1], "tensor", down))
        other["up", j] = lax.ppermute(from_behind[j], "tensor", across)
        if j < chips - ahead:
            other["down", j] = lax.ppermute(from_front[j], "tensor", across)
    mine = from_behind + from_front[1:]
    theirs = [other["up", j] for j in range(ahead + 1)]
    theirs += [other["down", j] for j in range(1, chips - ahead)]
    return mine + theirs


def write_chunk(stage, ids_ref, rows, out_ref):
    width = stage.shape[1]
    for g in range(BLOCKS * rows // 8):
        out_ref[:, g * width : (g + 1) * width] = stage[8 * g : 8 * g + 8, :].astype(jnp.bfloat16)
    sub = lax.broadcasted_iota(jnp.int32, (8, LANES), 0)
    ids = jnp.zeros((8, LANES), jnp.float32)
    for r in range(rows):
        ids = jnp.where(sub == r, ids_ref[r].astype(jnp.float32), ids)
    out_ref[:, BLOCKS * rows // 8 * width :] = ids.astype(jnp.bfloat16)


def norm_kernel(ids_ref, x_ref, gain_ref, out_ref, stage):
    rows, width = x_ref.shape
    block = width // BLOCKS
    total = jnp.zeros((rows, LANES), jnp.float32)
    for c in range(width // LANES):
        x = x_ref[:, c * LANES : (c + 1) * LANES].astype(jnp.float32)
        total = total + x * x
    factor = lax.rsqrt(jnp.sum(total, axis=-1, keepdims=True) / width + EPS)
    for j in range(BLOCKS):
        cols = slice(j * block, (j + 1) * block)
        x = x_ref[:, cols].astype(jnp.float32)
        stage[j * rows : (j + 1) * rows, :] = x * factor * gain_ref[:, cols].astype(jnp.float32)
    write_chunk(stage, ids_ref, rows, out_ref)


def norm_chunk(hidden, gain, ids):
    rows, width = hidden.shape
    return pl.pallas_call(
        norm_kernel,
        out_shape=jax.ShapeDtypeStruct((8, rows * width // 8 + LANES), jnp.bfloat16),
        in_specs=[SMEM, VMEM, VMEM],
        out_specs=VMEM,
        scratch_shapes=[pltpu.VMEM((BLOCKS * rows, width // BLOCKS), jnp.float32)],
        compiler_params=params(16),
        name="norm_chunk",
    )(ids, hidden, gain.reshape(1, width))


def unpack(chunks, me, rows, stage, left):
    pairs = len(chunks) // 2
    block = stage.shape[-1]
    core = lax.rem(me, 2)
    for slot, chip in enumerate(slot_chips(2 * pairs, me)):
        turn = slot % stage.shape[0]
        for chunk, place in ((chunks[slot], core), (chunks[pairs + slot], 1 - core)):
            for g in range(BLOCKS * rows // 8):
                stage[turn, place, 8 * g : 8 * g + 8, :] = chunk[
                    :, g * block : (g + 1) * block
                ].astype(jnp.float32)
        at = pl.multiple_of(chip * 16, 16)
        for j in range(BLOCKS):
            both = [stage[turn, place, j * rows : j * rows + 8, :] for place in range(2)]
            left[j, pl.ds(at, 16), :] = jnp.concatenate(both, axis=0).astype(jnp.bfloat16)


def unpack_scratch(rows, block):
    return pltpu.VMEM((4, 2, BLOCKS * rows + 8, block), jnp.float32)


def fetch(weight, held, sems):
    block = held.shape[1]
    copies = [
        pltpu.make_async_copy(weight.at[pl.ds(j * block, block), :], held.at[j], sems.at[j])
        for j in range(BLOCKS)
    ]
    for copy in copies:
        copy.start()
    return copies


def qkv_kernel(devices, rows, *refs):
    me_ref, bias_ref, weight = refs[:3]
    chunks = refs[3 : 3 + devices]
    out_ref, held, sems, stage, left, acc = refs[3 + devices :]
    copies = fetch(weight, held, sems)
    unpack(chunks, me_ref[0], rows, stage, left)
    for j in range(BLOCKS):
        copies[j].wait()
        part = jnp.dot(left[j], held[j], preferred_element_type=jnp.float32)
        if j == 0:
            acc[...] = part + bias_ref[...].astype(jnp.float32)
        else:
            acc[...] += part
    for d in range(devices):
        out_ref[d] = acc[8 * d : 8 * d + rows, :].astype(jnp.bfloat16)


def qkv_project(me, chunks, weight, bias, rows):
    devices = len(chunks)
    width, cols = weight.shape
    block = width // BLOCKS
    return pl.pallas_call(
        functools.partial(qkv_kernel, devices, rows),
        out_shape=jax.ShapeDtypeStruct((devices, rows, cols), jnp.bfloat16),
        in_specs=[SMEM, VMEM, ANY] + [VMEM] * devices,
        out_specs=VMEM,
        scratch_shapes=[
            pltpu.VMEM((BLOCKS, block, cols), jnp.bfloat16),
            pltpu.SemaphoreType.DMA((BLOCKS,)),
            unpack_scratch(rows, block),
            pltpu.VMEM((BLOCKS, devices * 8, block), jnp.bfloat16),
            pltpu.VMEM((devices * 8, cols), jnp.float32),
        ],
        compiler_params=params(56 if devices > 16 else 32),
        cost_estimate=pl.CostEstimate(
            flops=2 * devices * rows * width * cols,
            bytes_accessed=width * cols * 2,
            transcendentals=0,
        ),
        name="qkv_project",
    )(me, bias.reshape(1, cols), weight, *chunks)


def attend_kernel(rows, len_ref, ids_ref, qkv_ref, cos_ref, sin_ref, k_ref, v_ref, out_ref, heads, mixed, stage):
    r = pl.program_id(0)
    total_heads = QUERY_HEADS + 2 * KVH
    half = HEAD_SIZE // 2

    @pl.when(r == 0)
    def _():
        for h in range(total_heads):
            tile = qkv_ref[:, h * HEAD_SIZE : (h + 1) * HEAD_SIZE].astype(jnp.float32)
            heads[pl.ds(h, rows, stride=total_heads), :] = tile

    base = pl.multiple_of(r * total_heads, 8)
    turned = heads[pl.ds(base, QUERY_HEADS + KVH), :]
    cosine = cos_ref[pl.ds(r, 1), :]
    sine = sin_ref[pl.ds(r, 1), :]
    turned = (turned * cosine + pltpu.roll(turned, half, 1) * sine).astype(jnp.bfloat16)
    query = turned[:QUERY_HEADS]
    query_f = query.astype(jnp.float32)
    new_key = turned[QUERY_HEADS:].astype(jnp.float32)
    new_value = heads[pl.ds(base + QUERY_HEADS + KVH, KVH), :]
    scale = 1.0 / HEAD_SIZE**0.5
    scores = []
    own = []
    for k in range(KVH):
        mine = slice(k * GROUPS, (k + 1) * GROUPS)
        keys = k_ref[0, :, k * HEAD_SIZE : (k + 1) * HEAD_SIZE]
        scores.append(
            lax.dot_general(
                query[mine], keys, (((1,), (1,)), ((), ())), preferred_element_type=jnp.float32
            )
        )
        own.append(jnp.sum(query_f[mine] * new_key[k : k + 1], axis=-1, keepdims=True))
    score = jnp.concatenate(scores, axis=0) * scale
    own = jnp.concatenate(own, axis=0) * scale
    valid = lax.broadcasted_iota(jnp.int32, score.shape, 1) < len_ref[r]
    top = jnp.maximum(jnp.max(jnp.where(valid, score, -1e30), axis=-1, keepdims=True), own)
    expo = jnp.where(valid, jnp.exp(score - top), 0.0)
    expo_own = jnp.exp(own - top)
    total = jnp.sum(expo, axis=-1, keepdims=True) + expo_own
    weight = (expo / total).astype(jnp.bfloat16)
    weight_own = (expo_own / total).astype(jnp.bfloat16).astype(jnp.float32)
    for k in range(KVH):
        mine = slice(k * GROUPS, (k + 1) * GROUPS)
        values = v_ref[0, :, k * HEAD_SIZE : (k + 1) * HEAD_SIZE]
        part = jnp.dot(weight[mine], values, preferred_element_type=jnp.float32)
        part = part + weight_own[mine] * new_value[k : k + 1]
        at = pl.multiple_of(r * QUERY_HEADS + k * GROUPS, 8)
        mixed[pl.ds(at, GROUPS), :] = part

    @pl.when(r == rows - 1)
    def _():
        per_block = QUERY_HEADS // BLOCKS
        for h in range(QUERY_HEADS):
            j, lane = h // per_block, h % per_block
            stage[j * rows : (j + 1) * rows, lane * HEAD_SIZE : (lane + 1) * HEAD_SIZE] = mixed[
                pl.ds(h, rows, stride=QUERY_HEADS), :
            ]
        write_chunk(stage, ids_ref, rows, out_ref)


def attend(lengths, ids, qkv, cosine, sine, keys, values):
    rows, capacity, width = keys.shape
    total_heads = QUERY_HEADS + 2 * KVH
    features = QUERY_HEADS * HEAD_SIZE
    cache = pl.BlockSpec((1, capacity, width), lambda r: (r, 0, 0))
    return pl.pallas_call(
        functools.partial(attend_kernel, rows),
        grid=(rows,),
        out_shape=jax.ShapeDtypeStruct((8, rows * features // 8 + LANES), jnp.bfloat16),
        in_specs=[SMEM, SMEM, VMEM, VMEM, VMEM, cache, cache],
        out_specs=VMEM,
        scratch_shapes=[
            pltpu.VMEM((rows * total_heads, HEAD_SIZE), jnp.float32),
            pltpu.VMEM((rows * QUERY_HEADS, HEAD_SIZE), jnp.float32),
            pltpu.VMEM((BLOCKS * rows, features // BLOCKS), jnp.float32),
        ],
        compiler_params=params(24),
        name="attend",
    )(lengths, ids, qkv, cosine, sine, keys, values)


def shrink_kernel(devices, rows, *refs):
    me_ref, down_ref = refs[:2]
    chunks = refs[2 : 2 + devices]
    left, coords_ref, stage, ids, total = refs[2 + devices :]
    me = me_ref[0]
    stored, rank, features = down_ref.shape
    block = features // BLOCKS
    unpack(chunks, me, rows, stage, left)
    for s in range(stored):
        for j in range(BLOCKS):
            part = lax.dot_general(
                down_ref[s, :, j * block : (j + 1) * block],
                left[j],
                (((1,), (1,)), ((), ())),
                preferred_element_type=jnp.float32,
            )
            if j == 0:
                total[s * rank : (s + 1) * rank, :] = part
            else:
                total[s * rank : (s + 1) * rank, :] += part
    core = lax.rem(me, 2)
    pairs = devices // 2
    for slot, chip in enumerate(slot_chips(devices, me)):
        for chunk, place in ((chunks[slot], core), (chunks[pairs + slot], 1 - core)):
            at = pl.multiple_of((2 * chip + place) * 8, 8)
            ids[pl.ds(at, 8), :] = chunk[:, features * rows // 8 :].astype(jnp.float32)
    row_ids = jnp.transpose(ids[...])[: stored * rank, :].astype(jnp.int32)
    adapter = lax.broadcasted_iota(jnp.int32, total.shape, 0) // rank + me * stored
    coords = jnp.where(row_ids == adapter, total[...], 0.0).astype(jnp.bfloat16)
    for d in range(devices):
        coords_ref[d] = coords


def shrink(me, chunks, down, rows):
    devices = len(chunks)
    stored, rank, features = down.shape
    block = features // BLOCKS
    return pl.pallas_call(
        functools.partial(shrink_kernel, devices, rows),
        out_shape=(
            jax.ShapeDtypeStruct((BLOCKS, devices * 8, block), jnp.bfloat16),
            jax.ShapeDtypeStruct((devices, stored * rank, devices * 8), jnp.bfloat16),
        ),
        in_specs=[SMEM, VMEM] + [VMEM] * devices,
        out_specs=(VMEM, VMEM),
        scratch_shapes=[
            unpack_scratch(rows, block),
            pltpu.VMEM((devices * 8, LANES), jnp.float32),
            pltpu.VMEM((stored * rank, devices * 8), jnp.float32),
        ],
        compiler_params=params(56 if devices > 16 else 24),
        name="shrink",
    )(me, down, *chunks)


def base_kernel(left, weight, out_ref, held, sems):
    copies = fetch(weight, held, sems)
    for j in range(BLOCKS):
        copies[j].wait()
        part = jnp.dot(left[j], held[j], preferred_element_type=jnp.float32)
        if j == 0:
            out_ref[...] = part
        else:
            out_ref[...] += part


def base_project(left, weight):
    width, cols = weight.shape
    block = width // BLOCKS
    rows = left.shape[1]
    return pl.pallas_call(
        base_kernel,
        out_shape=jax.ShapeDtypeStruct((rows, cols), jnp.float32),
        in_specs=[VMEM, ANY],
        out_specs=VMEM,
        scratch_shapes=[
            pltpu.VMEM((BLOCKS, block, cols), jnp.bfloat16),
            pltpu.SemaphoreType.DMA((BLOCKS,)),
        ],
        compiler_params=params(32),
        cost_estimate=pl.CostEstimate(
            flops=2 * rows * width * cols, bytes_accessed=width * cols * 2, transcendentals=0
        ),
        name="base_project",
    )(left, weight)


def add_kernel(rows, base_ref, coords_ref, up_ref, out_ref):
    delta = lax.dot_general(
        coords_ref[...], up_ref[...], (((0,), (0,)), ((), ())), preferred_element_type=jnp.float32
    )
    projected = base_ref[...] + delta
    for d in range(out_ref.shape[0]):
        out_ref[d] = projected[8 * d : 8 * d + rows, :].astype(jnp.bfloat16)


def add_delta(base, coords, up, rows):
    return pl.pallas_call(
        functools.partial(add_kernel, rows),
        out_shape=jax.ShapeDtypeStruct((base.shape[0] // 8, rows, base.shape[1]), jnp.bfloat16),
        in_specs=[VMEM, VMEM, VMEM],
        out_specs=VMEM,
        compiler_params=params(40),
        name="add_delta",
    )(base, coords, up)


def exchange(parts):
    return lax.all_to_all(parts, "tensor", split_axis=0, concat_axis=0, tiled=True)


def per_row(parts):
    devices, rows, cols = parts.shape
    return jnp.transpose(parts, (1, 0, 2)).reshape(rows, devices * cols)


def per_device(
    devices,
    hidden,
    input_norm_scale,
    query_key_value_weight,
    projection_bias,
    rotated_key_cache,
    past_value_cache,
    lengths,
    row_adapter_index,
    output_weight,
    adapter_down_weight,
    adapter_up_weight,
):
    rows = hidden.shape[0]
    me = lax.axis_index("tensor").astype(jnp.int32).reshape(1)
    half = HEAD_SIZE // 2
    inv = ROPE_BASE ** (-(jnp.arange(half, dtype=jnp.float32) * 2.0 / HEAD_SIZE))
    angle = lengths.astype(jnp.float32)[:, None] * inv[None, :]
    cosine, sine = jnp.cos(angle), jnp.sin(angle)
    cosine = jnp.concatenate([cosine, cosine], axis=1)
    sine = jnp.concatenate([-sine, sine], axis=1)
    down = jnp.transpose(adapter_down_weight, (0, 2, 1))
    up = adapter_up_weight.reshape(-1, adapter_up_weight.shape[2])

    chunk = norm_chunk(hidden, input_norm_scale, row_adapter_index)
    chunks = gather_chunks(chunk, devices)
    qkv = qkv_project(me, chunks, query_key_value_weight, projection_bias, rows)
    qkv = per_row(exchange(qkv))
    chunk = attend(
        lengths, row_adapter_index, qkv, cosine, sine, rotated_key_cache, past_value_cache
    )
    chunks = gather_chunks(chunk, devices)
    left, coords = shrink(me, chunks, down, rows)
    coords = exchange(coords)
    base = base_project(left, output_weight)
    coords = coords.reshape(-1, coords.shape[2])
    return per_row(exchange(add_delta(base, coords, up, rows)))


def solution(mesh):
    in_specs = (
        P(("group", "tensor"), None),
        P(),
        P(None, "tensor"),
        P("tensor"),
        P(("group", "tensor"), None, None),
        P(("group", "tensor"), None, None),
        P(("group", "tensor")),
        P(("group", "tensor")),
        P(None, "tensor"),
        P("tensor", None, None),
        P(None, None, "tensor"),
    )
    out_specs = P(("group", "tensor"), None)
    return jax.shard_map(
        functools.partial(per_device, mesh.shape["tensor"]),
        mesh=mesh,
        in_specs=in_specs,
        out_specs=out_specs,
        check_vma=False,
    )
```

```python
import functools

import jax
import jax.numpy as jnp
from jax import lax
from jax.experimental import pallas as pl
from jax.experimental.pallas import tpu as pltpu
from jax.sharding import PartitionSpec as P

QUERY_HEADS = 64
KVH = 8
HEAD_SIZE = 128
ADAPTER_RANK = 16
GROUPS = QUERY_HEADS // KVH

EPS = 1e-06
ROPE_BASE = 1000000.0

BLOCKS = 8
HALF = BLOCKS // 2
LANES = 128
MIB = 1 << 20

VMEM = pl.BlockSpec(memory_space=pltpu.VMEM)
HBM = pl.BlockSpec(memory_space=pltpu.HBM)
SMEM = pl.BlockSpec(memory_space=pltpu.SMEM)


def params(mib):
    return pltpu.CompilerParams(vmem_limit_bytes=mib * MIB)


def factors(chips):
    inner = 1
    while inner * inner * 4 <= chips and chips % (inner * 2) == 0:
        inner *= 2
    return chips // inner, inner


def ring_order(chips):
    outer, inner = factors(chips)
    if inner < 2 or outer % 2:
        return list(range(chips))
    order = [a * inner for a in range(outer)]
    for turn, a in enumerate(reversed(range(outer))):
        steps = range(1, inner) if turn % 2 == 0 else range(inner - 1, 0, -1)
        order += [a * inner + b for b in steps]
    return order


def lookup(table, index):
    value = jnp.int32(table[0])
    for at in range(1, len(table)):
        value = jnp.where(index == at, jnp.int32(table[at]), value)
    return value


def slot_chips(devices, me):
    chips = devices // 2
    order = ring_order(chips)
    place_of = [order.index(chip) for chip in range(chips)]
    place = lookup(place_of, lax.div(me, 2))
    ahead = chips // 2
    shifts = [-j for j in range(ahead)] + [j for j in range(1, chips - ahead + 1)]
    return [lookup(order, lax.rem(place + shift + chips, chips)) for shift in shifts]


def steps(count, unrolled, body):
    if unrolled:
        for i in range(count):
            body(i)
    else:
        lax.fori_loop(0, count, lambda i, _: (body(i), 0)[1], 0)


def gather_chunks(halves, devices):
    chips = devices // 2
    order = ring_order(chips)
    ahead = chips // 2

    def ring(step):
        return [
            (2 * order[p] + core, 2 * order[(p + step) % chips] + core)
            for p in range(chips)
            for core in range(2)
        ]

    up, down = ring(1), ring(-1)
    far = [ahead, chips - ahead - 1], [ahead - 1, chips - ahead]
    behind, front = [[half] for half in halves], [[half] for half in halves]
    for j in range(1, max(ahead, chips - ahead) + 1):
        for h in (0, 1):
            if j <= far[h][0]:
                behind[h].append(lax.ppermute(behind[h][-1], "tensor", up))
            if j <= far[h][1]:
                front[h].append(lax.ppermute(front[h][-1], "tensor", down))
    slots = []
    for h in (0, 1):
        near = behind[h][:ahead] + front[h][1 : chips - ahead]
        slots.append(near + [behind[h][ahead] if h == 0 else front[h][chips - ahead]])
    return slots


def across(x, devices):
    return lax.ppermute(x, "tensor", [(d, d ^ 1) for d in range(devices)])


def write_half(stage, h, rows, out_ref):
    block = stage.shape[1]
    for g in range(HALF * rows // 8):
        at = h * HALF * rows + 8 * g
        out_ref[:, g * block : (g + 1) * block] = stage[at : at + 8, :].astype(jnp.bfloat16)


def write_ids(ids_ref, rows, out_ref):
    sub = lax.broadcasted_iota(jnp.int32, (8, LANES), 0)
    ids = jnp.full((8, LANES), -1.0, jnp.float32)
    for r in range(rows):
        ids = jnp.where(sub == r, ids_ref[r].astype(jnp.float32), ids)
    out_ref[:, out_ref.shape[1] - LANES :] = ids.astype(jnp.bfloat16)


def norm_kernel(x_hbm, gain_hbm, first_ref, second_ref, x_ref, gain_ref, sems, stage):
    copies = [
        pltpu.make_async_copy(x_hbm, x_ref, sems.at[0]),
        pltpu.make_async_copy(gain_hbm, gain_ref, sems.at[1]),
    ]
    for copy in copies:
        copy.start()
    for copy in copies:
        copy.wait()
    rows, width = x_ref.shape
    block = width // BLOCKS
    total = jnp.zeros((rows, LANES), jnp.float32)
    for c in range(width // LANES):
        x = x_ref[:, c * LANES : (c + 1) * LANES].astype(jnp.float32)
        total = total + x * x
    factor = lax.rsqrt(jnp.sum(total, axis=-1, keepdims=True) / width + EPS)
    for c in range(width // LANES):
        x = x_ref[:, c * LANES : (c + 1) * LANES].astype(jnp.float32)
        gain = gain_ref[c : c + 1, :].astype(jnp.float32)
        j, lane = c * LANES // block, c * LANES % block
        stage[j * rows : (j + 1) * rows, lane : lane + LANES] = x * factor * gain
    write_half(stage, 0, rows, first_ref)
    write_half(stage, 1, rows, second_ref)


def norm_chunk(hidden, gain):
    rows, width = hidden.shape
    half = jax.ShapeDtypeStruct((8, rows * width // 16), jnp.bfloat16)
    return pl.pallas_call(
        norm_kernel,
        out_shape=(half, half),
        in_specs=[HBM, HBM],
        out_specs=(VMEM, VMEM),
        scratch_shapes=[
            pltpu.VMEM((rows, width), jnp.bfloat16),
            pltpu.VMEM((width // LANES, LANES), jnp.bfloat16),
            pltpu.SemaphoreType.DMA((2,)),
            pltpu.VMEM((BLOCKS * rows, width // BLOCKS), jnp.float32),
        ],
        compiler_params=params(16),
        name="norm_chunk",
    )(hidden, gain.reshape(width // LANES, LANES))


def unpack_kernel(chips, rows, with_ids, *refs):
    firsts, seconds = refs[:chips], refs[chips : 2 * chips]
    left, stage = refs[2 * chips :]
    block = stage.shape[-1]
    per_half = HALF * rows
    small = chips <= 8
    for pair in range(chips // 2):
        turn = pair % 2
        for place in range(2):
            for h, halves in ((0, firsts), (1, seconds)):
                chunk = halves[2 * pair + place]

                def widen(g, chunk=chunk, place=place, h=h):
                    lane = g * block if small else pl.multiple_of(g * block, block)
                    at = h * per_half + 8 * g
                    at = at if small else pl.multiple_of(at, 8)
                    stage[turn, place, pl.ds(at, 8), :] = chunk[:, pl.ds(lane, block)].astype(
                        jnp.float32
                    )

                steps(per_half // 8, small, widen)

        for j in range(BLOCKS):
            both = [stage[turn, place, j * rows : j * rows + 8, :] for place in range(2)]
            left[j, 16 * pair : 16 * pair + 16, :] = jnp.concatenate(both, axis=0).astype(
                jnp.bfloat16
            )
        if with_ids:
            both = [firsts[2 * pair + place][:, per_half // 8 * block :] for place in range(2)]
            both = jnp.concatenate([ids.astype(jnp.float32) for ids in both], axis=0)
            left[BLOCKS, 16 * pair : 16 * pair + 16, :LANES] = both.astype(jnp.bfloat16)


def unpack(halves, rows, width, with_ids):
    firsts, seconds = halves
    chips = len(firsts)
    block = width // BLOCKS
    return pl.pallas_call(
        functools.partial(unpack_kernel, chips, rows, with_ids),
        out_shape=jax.ShapeDtypeStruct((BLOCKS + with_ids, chips * 8, block), jnp.bfloat16),
        in_specs=[VMEM] * (2 * chips),
        out_specs=VMEM,
        scratch_shapes=[pltpu.VMEM((2, 2, BLOCKS * rows + 8, block), jnp.float32)],
        compiler_params=params(32),
        name="unpack",
    )(*firsts, *seconds)


def fetch(weight, held, sems):
    block = held.shape[1]
    copies = [
        pltpu.make_async_copy(weight.at[pl.ds(j * block, block), :], held.at[j], sems.at[j])
        for j in range(BLOCKS)
    ]
    for copy in copies:
        copy.start()
    return copies


def multiply(left, held, acc, copies=None):
    acc[...] = jnp.zeros_like(acc)
    for j in range(BLOCKS):
        if copies is not None:
            copies[j].wait()
        acc[...] += jnp.dot(left[j], held[j], preferred_element_type=jnp.float32)


def own_kernel(left, weight, held, acc, sems):
    multiply(left, held, acc, fetch(weight, held, sems))


def own_rows(left, weight, name):
    width, cols = weight.shape
    rows = left.shape[1]
    return pl.pallas_call(
        own_kernel,
        out_shape=(
            jax.ShapeDtypeStruct((BLOCKS, width // BLOCKS, cols), jnp.bfloat16),
            jax.ShapeDtypeStruct((rows, cols), jnp.float32),
        ),
        in_specs=[VMEM, HBM],
        out_specs=(VMEM, VMEM),
        scratch_shapes=[pltpu.SemaphoreType.DMA((BLOCKS,))],
        compiler_params=params(24),
        cost_estimate=pl.CostEstimate(
            flops=2 * rows * width * cols, bytes_accessed=width * cols * 2, transcendentals=0
        ),
        name=name,
    )(left, weight)


def qkv_kernel(devices, rows, me_ref, bias_ref, own_ref, left, held, out_ref, acc):
    multiply(left, held, acc)
    bias = bias_ref[...].astype(jnp.float32)
    core = lax.rem(me_ref[0], 2)
    for slot, chip in enumerate(slot_chips(devices, me_ref[0])):
        mine = slice(8 * slot, 8 * slot + rows)
        out_ref[2 * chip + core] = (own_ref[mine, :] + bias).astype(jnp.bfloat16)
        out_ref[2 * chip + 1 - core] = (acc[mine, :] + bias).astype(jnp.bfloat16)


def qkv_project(me, own, left, held, bias, devices, rows):
    cols = own.shape[1]
    return pl.pallas_call(
        functools.partial(qkv_kernel, devices, rows),
        out_shape=jax.ShapeDtypeStruct((devices, rows, cols), jnp.bfloat16),
        in_specs=[SMEM, VMEM, VMEM, VMEM, VMEM],
        out_specs=VMEM,
        scratch_shapes=[pltpu.VMEM(own.shape, jnp.float32)],
        compiler_params=params(40),
        name="qkv_project",
    )(me, bias.reshape(1, cols), own, left, held)


def attend_kernel(
    rows,
    len_ref,
    ids_ref,
    qkv_ref,
    cos_ref,
    sin_ref,
    k_hbm,
    v_hbm,
    first_ref,
    second_ref,
    keys,
    values,
    sems,
    heads,
    mixed,
    stage,
):
    total_heads = QUERY_HEADS + 2 * KVH
    half = HEAD_SIZE // 2
    for r in range(rows):
        pltpu.make_async_copy(k_hbm.at[r], keys.at[r], sems.at[0, r]).start()
        pltpu.make_async_copy(v_hbm.at[r], values.at[r], sems.at[1, r]).start()
    for h in range(total_heads):
        tile = qkv_ref[:, h * HEAD_SIZE : (h + 1) * HEAD_SIZE].astype(jnp.float32)
        heads[pl.ds(h, rows, stride=total_heads), :] = tile
    scale = 1.0 / HEAD_SIZE**0.5

    def one_row(r, carry):
        base = pl.multiple_of(r * total_heads, 8)
        turned = heads[pl.ds(base, QUERY_HEADS + KVH), :]
        cosine = cos_ref[pl.ds(r, 1), :]
        sine = sin_ref[pl.ds(r, 1), :]
        turned = (turned * cosine + pltpu.roll(turned, half, 1) * sine).astype(jnp.bfloat16)
        query = turned[:QUERY_HEADS]
        query_f = query.astype(jnp.float32)
        new_key = turned[QUERY_HEADS:].astype(jnp.float32)
        new_value = heads[pl.ds(base + QUERY_HEADS + KVH, KVH), :]
        pltpu.make_async_copy(k_hbm.at[r], keys.at[r], sems.at[0, r]).wait()
        scores = []
        own = []
        for k in range(KVH):
            mine = slice(k * GROUPS, (k + 1) * GROUPS)
            key = keys[r, :, k * HEAD_SIZE : (k + 1) * HEAD_SIZE]
            scores.append(
                lax.dot_general(
                    query[mine], key, (((1,), (1,)), ((), ())), preferred_element_type=jnp.float32
                )
            )
            own.append(jnp.sum(query_f[mine] * new_key[k : k + 1], axis=-1, keepdims=True))
        score = jnp.concatenate(scores, axis=0) * scale
        own = jnp.concatenate(own, axis=0) * scale
        valid = lax.broadcasted_iota(jnp.int32, score.shape, 1) < len_ref[r]
        top = jnp.maximum(jnp.max(jnp.where(valid, score, -1e30), axis=-1, keepdims=True), own)
        expo = jnp.where(valid, jnp.exp(score - top), 0.0)
        expo_own = jnp.exp(own - top)
        total = jnp.sum(expo, axis=-1, keepdims=True) + expo_own
        weight = (expo / total).astype(jnp.bfloat16)
        weight_own = (expo_own / total).astype(jnp.bfloat16).astype(jnp.float32)
        pltpu.make_async_copy(v_hbm.at[r], values.at[r], sems.at[1, r]).wait()
        for k in range(KVH):
            mine = slice(k * GROUPS, (k + 1) * GROUPS)
            value = values[r, :, k * HEAD_SIZE : (k + 1) * HEAD_SIZE]
            part = jnp.dot(weight[mine], value, preferred_element_type=jnp.float32)
            part = part + weight_own[mine] * new_value[k : k + 1]
            at = pl.multiple_of(r * QUERY_HEADS + k * GROUPS, 8)
            mixed[pl.ds(at, GROUPS), :] = part
        return carry

    lax.fori_loop(0, rows, one_row, 0)
    per_block = QUERY_HEADS // BLOCKS
    for h in range(QUERY_HEADS):
        j, lane = h // per_block, h % per_block
        stage[j * rows : (j + 1) * rows, lane * HEAD_SIZE : (lane + 1) * HEAD_SIZE] = mixed[
            pl.ds(h, rows, stride=QUERY_HEADS), :
        ]
    write_half(stage, 0, rows, first_ref)
    write_half(stage, 1, rows, second_ref)
    write_ids(ids_ref, rows, first_ref)


def attend(lengths, ids, qkv, cosine, sine, keys, values):
    rows, capacity, width = keys.shape
    total_heads = QUERY_HEADS + 2 * KVH
    features = QUERY_HEADS * HEAD_SIZE
    size = rows * features // 16
    return pl.pallas_call(
        functools.partial(attend_kernel, rows),
        out_shape=(
            jax.ShapeDtypeStruct((8, size + LANES), jnp.bfloat16),
            jax.ShapeDtypeStruct((8, size), jnp.bfloat16),
        ),
        in_specs=[SMEM, SMEM, VMEM, VMEM, VMEM, HBM, HBM],
        out_specs=(VMEM, VMEM),
        scratch_shapes=[
            pltpu.VMEM(keys.shape, jnp.bfloat16),
            pltpu.VMEM(keys.shape, jnp.bfloat16),
            pltpu.SemaphoreType.DMA((2, rows)),
            pltpu.VMEM((rows * total_heads, HEAD_SIZE), jnp.float32),
            pltpu.VMEM((rows * QUERY_HEADS, HEAD_SIZE), jnp.float32),
            pltpu.VMEM((BLOCKS * rows, features // BLOCKS), jnp.float32),
        ],
        compiler_params=params(24),
        name="attend",
    )(lengths, ids, qkv, cosine, sine, keys, values)


def shrink_kernel(devices, me_ref, down_ref, own, other, coords_ref, ids, place_of, total):
    me = me_ref[0]
    stored, rank, features = down_ref.shape
    block = features // BLOCKS
    rows = own.shape[1]
    for c, left in enumerate((own, other)):
        mine = slice(c * rows, (c + 1) * rows)
        for s in range(stored):
            part = jnp.zeros((rank, rows), jnp.float32)
            for j in range(BLOCKS):
                part += lax.dot_general(
                    down_ref[s, :, j * block : (j + 1) * block],
                    left[j],
                    (((1,), (1,)), ((), ())),
                    preferred_element_type=jnp.float32,
                )
            total[s * rank : (s + 1) * rank, mine] = part
        ids[mine, :] = left[BLOCKS, :, :LANES].astype(jnp.float32)
    row_ids = jnp.transpose(ids[...])[: stored * rank, :].astype(jnp.int32)
    adapter = lax.broadcasted_iota(jnp.int32, total.shape, 0) // rank + me * stored
    coords = jnp.where(row_ids == adapter, total[...], 0.0).astype(jnp.bfloat16)
    core = lax.rem(me, 2)
    sub = lax.broadcasted_iota(jnp.int32, (8, LANES), 0)
    for slot, chip in enumerate(slot_chips(devices, me)):
        for c, place in ((0, core), (1, 1 - core)):
            at = c * rows + 8 * slot
            place_of[at : at + 8, :] = sub + (2 * chip + place) * 8
    target = lax.broadcasted_iota(jnp.int32, (2 * rows, 2 * rows), 1)
    move = jnp.where(place_of[:, :1] == target, 1.0, 0.0).astype(jnp.bfloat16)
    coords = jnp.dot(coords, move, preferred_element_type=jnp.float32).astype(jnp.bfloat16)
    for d in range(devices):
        coords_ref[d] = coords


def shrink(me, own, other, down, devices):
    stored, rank, features = down.shape
    rows = devices * 8
    return pl.pallas_call(
        functools.partial(shrink_kernel, devices),
        out_shape=jax.ShapeDtypeStruct((devices, stored * rank, rows), jnp.bfloat16),
        in_specs=[SMEM, VMEM, VMEM, VMEM],
        out_specs=VMEM,
        scratch_shapes=[
            pltpu.VMEM((rows, LANES), jnp.float32),
            pltpu.VMEM((rows, LANES), jnp.int32),
            pltpu.VMEM((stored * rank, rows), jnp.float32),
        ],
        compiler_params=params(48),
        name="shrink",
    )(me, down, own, other)


def base_kernel(devices, me_ref, own_ref, left, held, out_ref, acc):
    multiply(left, held, acc)
    core = lax.rem(me_ref[0], 2)
    for slot, chip in enumerate(slot_chips(devices, me_ref[0])):
        mine = slice(8 * slot, 8 * slot + 8)
        at = pl.multiple_of((2 * chip + core) * 8, 8)
        out_ref[pl.ds(at, 8), :] = own_ref[mine, :]
        at = pl.multiple_of((2 * chip + 1 - core) * 8, 8)
        out_ref[pl.ds(at, 8), :] = acc[mine, :]


def base_project(me, own, left, held, devices):
    rows, cols = own.shape
    return pl.pallas_call(
        functools.partial(base_kernel, devices),
        out_shape=jax.ShapeDtypeStruct((2 * rows, cols), jnp.float32),
        in_specs=[SMEM, VMEM, VMEM, VMEM],
        out_specs=VMEM,
        scratch_shapes=[pltpu.VMEM(own.shape, jnp.float32)],
        compiler_params=params(40),
        cost_estimate=pl.CostEstimate(
            flops=2 * rows * held.size, bytes_accessed=2 * held.size, transcendentals=0
        ),
        name="base_project",
    )(me, own, left, held)


def add_kernel(rows, base_ref, coords_ref, up_ref, out_ref):
    delta = lax.dot_general(
        coords_ref[...], up_ref[...], (((0,), (0,)), ((), ())), preferred_element_type=jnp.float32
    )
    projected = base_ref[...] + delta
    for d in range(out_ref.shape[0]):
        out_ref[d] = projected[8 * d : 8 * d + rows, :].astype(jnp.bfloat16)


def add_delta(base, coords, up, rows):
    return pl.pallas_call(
        functools.partial(add_kernel, rows),
        out_shape=jax.ShapeDtypeStruct((base.shape[0] // 8, rows, base.shape[1]), jnp.bfloat16),
        in_specs=[VMEM, VMEM, VMEM],
        out_specs=VMEM,
        compiler_params=params(40),
        name="add_delta",
    )(base, coords, up)


def exchange(parts):
    return lax.all_to_all(parts, "tensor", split_axis=0, concat_axis=0, tiled=True)


def per_row(parts):
    devices, rows, cols = parts.shape
    return jnp.transpose(parts, (1, 0, 2)).reshape(rows, devices * cols)


def per_device(
    devices,
    hidden,
    input_norm_scale,
    query_key_value_weight,
    projection_bias,
    rotated_key_cache,
    past_value_cache,
    lengths,
    row_adapter_index,
    output_weight,
    adapter_down_weight,
    adapter_up_weight,
):
    rows = hidden.shape[0]
    me = lax.axis_index("tensor").astype(jnp.int32).reshape(1)
    half = HEAD_SIZE // 2
    inv = ROPE_BASE ** (-(jnp.arange(half, dtype=jnp.float32) * 2.0 / HEAD_SIZE))
    angle = lengths.astype(jnp.float32)[:, None] * inv[None, :]
    cosine, sine = jnp.cos(angle), jnp.sin(angle)
    cosine = jnp.concatenate([cosine, cosine], axis=1)
    sine = jnp.concatenate([-sine, sine], axis=1)
    down = jnp.transpose(adapter_down_weight, (0, 2, 1))
    up = adapter_up_weight.reshape(-1, adapter_up_weight.shape[2])

    halves = gather_chunks(norm_chunk(hidden, input_norm_scale), devices)
    mine = unpack(halves, rows, hidden.shape[1], False)
    theirs = across(mine, devices)
    held, own = own_rows(mine, query_key_value_weight, "qkv_own")
    qkv = qkv_project(me, own, theirs, held, projection_bias, devices, rows)
    qkv = per_row(exchange(qkv))
    halves = attend(
        lengths, row_adapter_index, qkv, cosine, sine, rotated_key_cache, past_value_cache
    )
    mine = unpack(gather_chunks(halves, devices), rows, QUERY_HEADS * HEAD_SIZE, True)
    theirs = across(mine, devices)
    held, own = own_rows(mine, output_weight, "base_own")
    coords = exchange(shrink(me, mine, theirs, down, devices))
    base = base_project(me, own, theirs, held, devices)
    coords = coords.reshape(-1, coords.shape[2])
    return per_row(exchange(add_delta(base, coords, up, rows)))


def solution(mesh):
    in_specs = (
        P(("group", "tensor"), None),
        P(),
        P(None, "tensor"),
        P("tensor"),
        P(("group", "tensor"), None, None),
        P(("group", "tensor"), None, None),
        P(("group", "tensor")),
        P(("group", "tensor")),
        P(None, "tensor"),
        P("tensor", None, None),
        P(None, None, "tensor"),
    )
    out_specs = P(("group", "tensor"), None)
    return jax.shard_map(
        functools.partial(per_device, mesh.shape["tensor"]),
        mesh=mesh,
        in_specs=in_specs,
        out_specs=out_specs,
        check_vma=False,
    )
```

```python
import functools

import jax
import jax.numpy as jnp
from jax import lax
from jax.experimental import pallas as pl
from jax.experimental.pallas import tpu as pltpu
from jax.sharding import PartitionSpec as P

QUERY_HEADS = 64
KVH = 8
HEAD_SIZE = 128
ADAPTER_RANK = 16
GROUPS = QUERY_HEADS // KVH

EPS = 1e-06
ROPE_BASE = 1000000.0

BLOCKS = 8
LANES = 128
MIB = 1 << 20

VMEM = pl.BlockSpec(memory_space=pltpu.VMEM)
HBM = pl.BlockSpec(memory_space=pltpu.HBM)
SMEM = pl.BlockSpec(memory_space=pltpu.SMEM)


def params(mib):
    return pltpu.CompilerParams(vmem_limit_bytes=mib * MIB)


def factors(chips):
    inner = 1
    while inner * inner * 4 <= chips and chips % (inner * 2) == 0:
        inner *= 2
    return chips // inner, inner


def slot_chips(devices, me):
    outer, inner = factors(devices // 2)
    chip = lax.div(me, 2)
    a, b = lax.div(chip, inner), lax.rem(chip, inner)
    return [
        partner(a, k, outer, -1) * inner + partner(b, m, inner, -1)
        for m in range(inner)
        for k in range(outer)
    ]


def partner(at, step, size, sign=1):
    if size & (size - 1) == 0:
        return at ^ step
    return (at + sign * step + size) % size


def steps(count, unrolled, body):
    if unrolled:
        for i in range(count):
            body(i)
    else:
        lax.fori_loop(0, count, lambda i, _: (body(i), 0)[1], 0)


def gather_chunks(chunk, devices):
    outer, inner = factors(devices // 2)

    def pairs(k, m):
        return [
            (d, 2 * (partner(d // 2 // inner, k, outer) * inner + partner(d // 2 % inner, m, inner)) + d % 2)
            for d in range(devices)
        ]

    line = [chunk] + [lax.ppermute(chunk, "tensor", pairs(k, 0)) for k in range(1, outer)]
    slots = {}
    for k in range(outer):
        for m in range(1, inner):
            slots[k, m] = lax.ppermute(line[k], "tensor", pairs(0, m))
    for k in range(outer):
        slots[k, 0] = line[k]
    return [slots[k, m] for m in range(inner) for k in range(outer)]


def across(x, devices):
    return lax.ppermute(x, "tensor", [(d, d ^ 1) for d in range(devices)])


def write_chunk(stage, rows, out_ref):
    block = stage.shape[1]
    for g in range(BLOCKS * rows // 8):
        out_ref[:, g * block : (g + 1) * block] = stage[8 * g : 8 * g + 8, :].astype(jnp.bfloat16)


def write_ids(ids_ref, rows, out_ref):
    sub = lax.broadcasted_iota(jnp.int32, (8, LANES), 0)
    ids = jnp.full((8, LANES), -1.0, jnp.float32)
    for r in range(rows):
        ids = jnp.where(sub == r, ids_ref[r].astype(jnp.float32), ids)
    out_ref[:, out_ref.shape[1] - LANES :] = ids.astype(jnp.bfloat16)


def norm_kernel(x_hbm, gain_hbm, out_ref, x_ref, gain_ref, sems, stage):
    copies = [
        pltpu.make_async_copy(x_hbm, x_ref, sems.at[0]),
        pltpu.make_async_copy(gain_hbm, gain_ref, sems.at[1]),
    ]
    for copy in copies:
        copy.start()
    for copy in copies:
        copy.wait()
    rows, width = x_ref.shape
    block = width // BLOCKS
    total = jnp.zeros((rows, LANES), jnp.float32)
    for c in range(width // LANES):
        x = x_ref[:, c * LANES : (c + 1) * LANES].astype(jnp.float32)
        total = total + x * x
    factor = lax.rsqrt(jnp.sum(total, axis=-1, keepdims=True) / width + EPS)
    for c in range(width // LANES):
        x = x_ref[:, c * LANES : (c + 1) * LANES].astype(jnp.float32)
        gain = gain_ref[c : c + 1, :].astype(jnp.float32)
        j, lane = c * LANES // block, c * LANES % block
        stage[j * rows : (j + 1) * rows, lane : lane + LANES] = x * factor * gain
    write_chunk(stage, rows, out_ref)


def norm_chunk(hidden, gain):
    rows, width = hidden.shape
    return pl.pallas_call(
        norm_kernel,
        out_shape=jax.ShapeDtypeStruct((8, rows * width // 8), jnp.bfloat16),
        in_specs=[HBM, HBM],
        out_specs=VMEM,
        scratch_shapes=[
            pltpu.VMEM((rows, width), jnp.bfloat16),
            pltpu.VMEM((width // LANES, LANES), jnp.bfloat16),
            pltpu.SemaphoreType.DMA((2,)),
            pltpu.VMEM((BLOCKS * rows, width // BLOCKS), jnp.float32),
        ],
        compiler_params=params(16),
        name="norm_chunk",
    )(hidden, gain.reshape(width // LANES, LANES))


def unpack_kernel(chips, rows, with_ids, *refs):
    chunks = refs[:chips]
    left, stage = refs[chips:]
    block = stage.shape[-1]
    small = chips <= 8
    for pair in range(chips // 2):
        turn = pair % 2
        for place in range(2):
            chunk = chunks[2 * pair + place]

            def widen(g, chunk=chunk, turn=turn, place=place):
                lane = g * block if small else pl.multiple_of(g * block, block)
                at = 8 * g if small else pl.multiple_of(8 * g, 8)
                wide = chunk[:, pl.ds(lane, block)].astype(jnp.float32)
                stage[turn, place, pl.ds(at, 8), :] = wide

            steps(BLOCKS * rows // 8, small, widen)
        for j in range(BLOCKS):
            both = [stage[turn, place, j * rows : j * rows + 8, :] for place in range(2)]
            left[j, 16 * pair : 16 * pair + 16, :] = jnp.concatenate(both, axis=0).astype(
                jnp.bfloat16
            )
        if with_ids:
            at = BLOCKS * rows // 8 * block
            both = [chunks[2 * pair + place][:, at : at + LANES] for place in range(2)]
            both = jnp.concatenate([ids.astype(jnp.float32) for ids in both], axis=0)
            left[BLOCKS, 16 * pair : 16 * pair + 16, :LANES] = both.astype(jnp.bfloat16)


def unpack(chunks, rows, width, with_ids):
    chips = len(chunks)
    block = width // BLOCKS
    return pl.pallas_call(
        functools.partial(unpack_kernel, chips, rows, with_ids),
        out_shape=jax.ShapeDtypeStruct((BLOCKS + with_ids, chips * 8, block), jnp.bfloat16),
        in_specs=[VMEM] * chips,
        out_specs=VMEM,
        scratch_shapes=[pltpu.VMEM((2, 2, BLOCKS * rows + 8, block), jnp.float32)],
        compiler_params=params(32),
        name="unpack",
    )(*chunks)


def fetch(weight, held, sems):
    block = held.shape[1]
    copies = [
        pltpu.make_async_copy(weight.at[pl.ds(j * block, block), :], held.at[j], sems.at[j])
        for j in range(BLOCKS)
    ]
    for copy in copies:
        copy.start()
    return copies


def multiply(left, held, acc, copies=None):
    acc[...] = jnp.zeros_like(acc)
    for j in range(BLOCKS):
        if copies is not None:
            copies[j].wait()
        acc[...] += jnp.dot(left[j], held[j], preferred_element_type=jnp.float32)


def own_kernel(left, weight, held, acc, sems):
    multiply(left, held, acc, fetch(weight, held, sems))


def own_rows(left, weight, mib, name):
    width, cols = weight.shape
    rows = left.shape[1]
    return pl.pallas_call(
        own_kernel,
        out_shape=(
            jax.ShapeDtypeStruct((BLOCKS, width // BLOCKS, cols), jnp.bfloat16),
            jax.ShapeDtypeStruct((rows, cols), jnp.float32),
        ),
        in_specs=[VMEM, HBM],
        out_specs=(VMEM, VMEM),
        scratch_shapes=[pltpu.SemaphoreType.DMA((BLOCKS,))],
        compiler_params=params(mib),
        cost_estimate=pl.CostEstimate(
            flops=2 * rows * width * cols, bytes_accessed=width * cols * 2, transcendentals=0
        ),
        name=name,
    )(left, weight)


def qkv_kernel(devices, rows, me_ref, bias_ref, own_ref, left, held, out_ref, acc):
    multiply(left, held, acc)
    bias = bias_ref[...].astype(jnp.float32)
    core = lax.rem(me_ref[0], 2)
    for slot, chip in enumerate(slot_chips(devices, me_ref[0])):
        mine = slice(8 * slot, 8 * slot + rows)
        out_ref[2 * chip + core] = (own_ref[mine, :] + bias).astype(jnp.bfloat16)
        out_ref[2 * chip + 1 - core] = (acc[mine, :] + bias).astype(jnp.bfloat16)


def qkv_project(me, own, left, held, bias, devices, rows):
    cols = own.shape[1]
    return pl.pallas_call(
        functools.partial(qkv_kernel, devices, rows),
        out_shape=jax.ShapeDtypeStruct((devices, rows, cols), jnp.bfloat16),
        in_specs=[SMEM, VMEM, VMEM, VMEM, VMEM],
        out_specs=VMEM,
        scratch_shapes=[pltpu.VMEM(own.shape, jnp.float32)],
        compiler_params=params(40),
        name="qkv_project",
    )(me, bias.reshape(1, cols), own, left, held)


def hold_kernel(after, k_hbm, v_hbm, keys, values, sems):
    copies = [
        pltpu.make_async_copy(k_hbm, keys, sems.at[0]),
        pltpu.make_async_copy(v_hbm, values, sems.at[1]),
    ]
    for copy in copies:
        copy.start()
    for copy in copies:
        copy.wait()


def hold_caches(after, keys, values):
    cache = jax.ShapeDtypeStruct(keys.shape, keys.dtype)
    return pl.pallas_call(
        hold_kernel,
        out_shape=(cache, cache),
        in_specs=[HBM, HBM, HBM],
        out_specs=(VMEM, VMEM),
        scratch_shapes=[pltpu.SemaphoreType.DMA((2,))],
        compiler_params=params(43),
        cost_estimate=pl.CostEstimate(flops=0, bytes_accessed=8 * keys.size, transcendentals=0),
        name="hold_caches",
    )(after, keys, values)


def attend_kernel(
    rows,
    len_ref,
    ids_ref,
    qkv_ref,
    cos_ref,
    sin_ref,
    keys,
    values,
    out_ref,
    heads,
    mixed,
    stage,
):
    total_heads = QUERY_HEADS + 2 * KVH
    half = HEAD_SIZE // 2
    for h in range(total_heads):
        tile = qkv_ref[:, h * HEAD_SIZE : (h + 1) * HEAD_SIZE].astype(jnp.float32)
        heads[pl.ds(h, rows, stride=total_heads), :] = tile
    scale = 1.0 / HEAD_SIZE**0.5

    for r in range(rows):
        base = r * total_heads
        turned = heads[base : base + QUERY_HEADS + KVH, :]
        cosine = cos_ref[r : r + 1, :]
        sine = sin_ref[r : r + 1, :]
        turned = (turned * cosine + pltpu.roll(turned, half, 1) * sine).astype(jnp.bfloat16)
        query = turned[:QUERY_HEADS]
        query_f = query.astype(jnp.float32)
        new_key = turned[QUERY_HEADS:].astype(jnp.float32)
        new_value = heads[base + QUERY_HEADS + KVH : base + total_heads, :]
        scores = []
        own = []
        for k in range(KVH):
            mine = slice(k * GROUPS, (k + 1) * GROUPS)
            key = keys[r, :, k * HEAD_SIZE : (k + 1) * HEAD_SIZE]
            scores.append(
                lax.dot_general(
                    query[mine], key, (((1,), (1,)), ((), ())), preferred_element_type=jnp.float32
                )
            )
            own.append(jnp.sum(query_f[mine] * new_key[k : k + 1], axis=-1, keepdims=True))
        score = jnp.concatenate(scores, axis=0) * scale
        own = jnp.concatenate(own, axis=0) * scale
        valid = lax.broadcasted_iota(jnp.int32, score.shape, 1) < len_ref[r]
        top = jnp.maximum(jnp.max(jnp.where(valid, score, -1e30), axis=-1, keepdims=True), own)
        expo = jnp.where(valid, jnp.exp(score - top), 0.0)
        expo_own = jnp.exp(own - top)
        total = jnp.sum(expo, axis=-1, keepdims=True) + expo_own
        weight = (expo / total).astype(jnp.bfloat16)
        weight_own = (expo_own / total).astype(jnp.bfloat16).astype(jnp.float32)
        for k in range(KVH):
            mine = slice(k * GROUPS, (k + 1) * GROUPS)
            value = values[r, :, k * HEAD_SIZE : (k + 1) * HEAD_SIZE]
            part = jnp.dot(weight[mine], value, preferred_element_type=jnp.float32)
            part = part + weight_own[mine] * new_value[k : k + 1]
            at = r * QUERY_HEADS + k * GROUPS
            mixed[at : at + GROUPS, :] = part
    per_block = QUERY_HEADS // BLOCKS
    for h in range(QUERY_HEADS):
        j, lane = h // per_block, h % per_block
        stage[j * rows : (j + 1) * rows, lane * HEAD_SIZE : (lane + 1) * HEAD_SIZE] = mixed[
            pl.ds(h, rows, stride=QUERY_HEADS), :
        ]
    write_chunk(stage, rows, out_ref)
    write_ids(ids_ref, rows, out_ref)


def attend(lengths, ids, qkv, cosine, sine, keys, values):
    rows, capacity, width = keys.shape
    total_heads = QUERY_HEADS + 2 * KVH
    features = QUERY_HEADS * HEAD_SIZE
    return pl.pallas_call(
        functools.partial(attend_kernel, rows),
        out_shape=jax.ShapeDtypeStruct((8, rows * features // 8 + LANES), jnp.bfloat16),
        in_specs=[SMEM, SMEM, VMEM, VMEM, VMEM, VMEM, VMEM],
        out_specs=VMEM,
        scratch_shapes=[
            pltpu.VMEM((rows * total_heads, HEAD_SIZE), jnp.float32),
            pltpu.VMEM((rows * QUERY_HEADS, HEAD_SIZE), jnp.float32),
            pltpu.VMEM((BLOCKS * rows, features // BLOCKS), jnp.float32),
        ],
        compiler_params=params(24),
        name="attend",
    )(lengths, ids, qkv, cosine, sine, keys, values)


def times_down(down_ref, left, write):
    stored, rank, features = down_ref.shape
    block = features // BLOCKS
    for s in range(stored):
        part = jnp.zeros((rank, left.shape[1]), jnp.float32)
        for j in range(BLOCKS):
            part += lax.dot_general(
                down_ref[s, :, j * block : (j + 1) * block],
                left[j],
                (((1,), (1,)), ((), ())),
                preferred_element_type=jnp.float32,
            )
        write(slice(s * rank, (s + 1) * rank), part)


def shrink_own_kernel(down_ref, left, out_ref):
    def write(at, part):
        out_ref[at, :] = part

    times_down(down_ref, left, write)


def shrink_own(left, down):
    stored, rank, features = down.shape
    return pl.pallas_call(
        shrink_own_kernel,
        out_shape=jax.ShapeDtypeStruct((stored * rank, left.shape[1]), jnp.float32),
        in_specs=[VMEM, VMEM],
        out_specs=VMEM,
        compiler_params=params(48),
        cost_estimate=pl.CostEstimate(
            flops=2 * left.size * stored * rank, bytes_accessed=2 * left.size, transcendentals=0
        ),
        name="shrink_own",
    )(down, left)


def shrink_kernel(
    devices, me_ref, down_ref, own_part, own, other, coords_ref, ids, place_of, total
):
    me = me_ref[0]
    stored, rank, _ = down_ref.shape
    rows = own.shape[1]
    total[:, :rows] = own_part[...]

    def write(at, part):
        total[at, rows:] = part

    times_down(down_ref, other, write)
    for c, left in enumerate((own, other)):
        ids[c * rows : (c + 1) * rows, :] = left[BLOCKS, :, :LANES].astype(jnp.float32)
    row_ids = jnp.transpose(ids[...])[: stored * rank, :].astype(jnp.int32)
    adapter = lax.broadcasted_iota(jnp.int32, total.shape, 0) // rank + me * stored
    coords = jnp.where(row_ids == adapter, total[...], 0.0).astype(jnp.bfloat16)
    core = lax.rem(me, 2)
    sub = lax.broadcasted_iota(jnp.int32, (8, LANES), 0)
    for slot, chip in enumerate(slot_chips(devices, me)):
        for c, place in ((0, core), (1, 1 - core)):
            at = c * rows + 8 * slot
            place_of[at : at + 8, :] = sub + (2 * chip + place) * 8
    target = lax.broadcasted_iota(jnp.int32, (2 * rows, 2 * rows), 1)
    move = jnp.where(place_of[:, :1] == target, 1.0, 0.0).astype(jnp.bfloat16)
    coords = jnp.dot(coords, move, preferred_element_type=jnp.float32).astype(jnp.bfloat16)
    for d in range(devices):
        coords_ref[d] = coords


def shrink(me, own_part, own, other, down, devices):
    stored, rank, features = down.shape
    rows = devices * 8
    return pl.pallas_call(
        functools.partial(shrink_kernel, devices),
        out_shape=jax.ShapeDtypeStruct((devices, stored * rank, rows), jnp.bfloat16),
        in_specs=[SMEM, VMEM, VMEM, VMEM, VMEM],
        out_specs=VMEM,
        scratch_shapes=[
            pltpu.VMEM((rows, LANES), jnp.float32),
            pltpu.VMEM((rows, LANES), jnp.int32),
            pltpu.VMEM((stored * rank, rows), jnp.float32),
        ],
        compiler_params=params(48),
        name="shrink",
    )(me, down, own_part, own, other)


def base_kernel(devices, me_ref, own_ref, left, held, out_ref, acc):
    multiply(left, held, acc)
    core = lax.rem(me_ref[0], 2)
    for slot, chip in enumerate(slot_chips(devices, me_ref[0])):
        mine = slice(8 * slot, 8 * slot + 8)
        at = pl.multiple_of((2 * chip + core) * 8, 8)
        out_ref[pl.ds(at, 8), :] = own_ref[mine, :]
        at = pl.multiple_of((2 * chip + 1 - core) * 8, 8)
        out_ref[pl.ds(at, 8), :] = acc[mine, :]


def base_project(me, own, left, held, devices):
    rows, cols = own.shape
    return pl.pallas_call(
        functools.partial(base_kernel, devices),
        out_shape=jax.ShapeDtypeStruct((2 * rows, cols), jnp.float32),
        in_specs=[SMEM, VMEM, VMEM, VMEM],
        out_specs=VMEM,
        scratch_shapes=[pltpu.VMEM(own.shape, jnp.float32)],
        compiler_params=params(40),
        cost_estimate=pl.CostEstimate(
            flops=2 * rows * held.size, bytes_accessed=2 * held.size, transcendentals=0
        ),
        name="base_project",
    )(me, own, left, held)


def add_kernel(rows, base_ref, coords_ref, up_ref, out_ref):
    delta = lax.dot_general(
        coords_ref[...], up_ref[...], (((0,), (0,)), ((), ())), preferred_element_type=jnp.float32
    )
    projected = base_ref[...] + delta
    for d in range(out_ref.shape[0]):
        out_ref[d] = projected[8 * d : 8 * d + rows, :].astype(jnp.bfloat16)


def add_delta(base, coords, up, rows):
    return pl.pallas_call(
        functools.partial(add_kernel, rows),
        out_shape=jax.ShapeDtypeStruct((base.shape[0] // 8, rows, base.shape[1]), jnp.bfloat16),
        in_specs=[VMEM, VMEM, VMEM],
        out_specs=VMEM,
        compiler_params=params(40),
        name="add_delta",
    )(base, coords, up)


def exchange(parts):
    return lax.all_to_all(parts, "tensor", split_axis=0, concat_axis=0, tiled=True)


def per_row(parts):
    devices, rows, cols = parts.shape
    return jnp.transpose(parts, (1, 0, 2)).reshape(rows, devices * cols)


def per_device(
    devices,
    hidden,
    input_norm_scale,
    query_key_value_weight,
    projection_bias,
    rotated_key_cache,
    past_value_cache,
    lengths,
    row_adapter_index,
    output_weight,
    adapter_down_weight,
    adapter_up_weight,
):
    rows = hidden.shape[0]
    me = lax.axis_index("tensor").astype(jnp.int32).reshape(1)
    half = HEAD_SIZE // 2
    inv = ROPE_BASE ** (-(jnp.arange(half, dtype=jnp.float32) * 2.0 / HEAD_SIZE))
    angle = lengths.astype(jnp.float32)[:, None] * inv[None, :]
    cosine, sine = jnp.cos(angle), jnp.sin(angle)
    cosine = jnp.concatenate([cosine, cosine], axis=1)
    sine = jnp.concatenate([-sine, sine], axis=1)
    down = jnp.transpose(adapter_down_weight, (0, 2, 1))
    up = adapter_up_weight.reshape(-1, adapter_up_weight.shape[2])

    chunks = gather_chunks(norm_chunk(hidden, input_norm_scale), devices)
    mine = unpack(chunks, rows, hidden.shape[1], False)
    theirs = across(mine, devices)
    held, own = own_rows(mine, query_key_value_weight, 40, "qkv_own")
    qkv = qkv_project(me, own, theirs, held, projection_bias, devices, rows)
    keys, values = hold_caches(qkv, rotated_key_cache, past_value_cache)
    qkv = per_row(exchange(qkv))
    chunk = attend(lengths, row_adapter_index, qkv, cosine, sine, keys, values)
    chunks = gather_chunks(chunk, devices)
    mine = unpack(chunks, rows, QUERY_HEADS * HEAD_SIZE, True)
    theirs = across(mine, devices)
    own_part = shrink_own(mine, down)
    coords = exchange(shrink(me, own_part, mine, theirs, down, devices))
    held, own = own_rows(mine, output_weight, 43, "base_own")
    base = base_project(me, own, theirs, held, devices)
    coords = coords.reshape(-1, coords.shape[2])
    return per_row(exchange(add_delta(base, coords, up, rows)))


def solution(mesh):
    in_specs = (
        P(("group", "tensor"), None),
        P(),
        P(None, "tensor"),
        P("tensor"),
        P(("group", "tensor"), None, None),
        P(("group", "tensor"), None, None),
        P(("group", "tensor")),
        P(("group", "tensor")),
        P(None, "tensor"),
        P("tensor", None, None),
        P(None, None, "tensor"),
    )
    out_specs = P(("group", "tensor"), None)
    return jax.shard_map(
        functools.partial(per_device, mesh.shape["tensor"]),
        mesh=mesh,
        in_specs=in_specs,
        out_specs=out_specs,
        check_vma=False,
    )
```

```python
import functools

import jax
import jax.numpy as jnp
from jax import lax
from jax.experimental import pallas as pl
from jax.experimental.pallas import tpu as pltpu
from jax.sharding import PartitionSpec as P

QUERY_HEADS = 64
KVH = 8
HEAD_SIZE = 128
ADAPTER_RANK = 16
GROUPS = QUERY_HEADS // KVH

EPS = 1e-06
ROPE_BASE = 1000000.0

BLOCKS = 8
LANES = 128
MIB = 1 << 20

VMEM = pl.BlockSpec(memory_space=pltpu.VMEM)
HBM = pl.BlockSpec(memory_space=pltpu.HBM)
ANY = pl.BlockSpec(memory_space=pl.ANY)
SMEM = pl.BlockSpec(memory_space=pltpu.SMEM)


def params(mib):
    return pltpu.CompilerParams(vmem_limit_bytes=mib * MIB)


def factors(chips):
    inner = 1
    while inner * inner * 4 <= chips and chips % (inner * 2) == 0:
        inner *= 2
    return chips // inner, inner


def slot_chips(devices, me):
    outer, inner = factors(devices // 2)
    chip = lax.div(me, 2)
    a, b = lax.div(chip, inner), lax.rem(chip, inner)
    return [
        partner(a, k, outer, -1) * inner + partner(b, m, inner, -1)
        for m in range(inner)
        for k in range(outer)
    ]


def partner(at, step, size, sign=1):
    if size & (size - 1) == 0:
        return at ^ step
    return (at + sign * step + size) % size


def steps(count, unrolled, body):
    if unrolled:
        for i in range(count):
            body(i)
    else:
        lax.fori_loop(0, count, lambda i, _: (body(i), 0)[1], 0)


def gather_chunks(chunk, devices, meanwhile):
    outer, inner = factors(devices // 2)

    def pairs(k, m):
        return [
            (d, 2 * (partner(d // 2 // inner, k, outer) * inner + partner(d // 2 % inner, m, inner)) + d % 2)
            for d in range(devices)
        ]

    line = [chunk] + [lax.ppermute(chunk, "tensor", pairs(k, 0)) for k in range(1, outer)]
    held, line[outer // 4] = meanwhile(line[outer // 4])
    slots = {}
    for k in range(outer):
        for m in range(1, inner):
            slots[k, m] = lax.ppermute(line[k], "tensor", pairs(0, m))
    for k in range(outer):
        slots[k, 0] = line[k]
    return [slots[k, m] for m in range(inner) for k in range(outer)], held


def across(x, devices):
    return lax.ppermute(x, "tensor", [(d, d ^ 1) for d in range(devices)])


def write_chunk(stage, rows, out_ref):
    block = stage.shape[1]
    for g in range(BLOCKS * rows // 8):
        out_ref[:, g * block : (g + 1) * block] = stage[8 * g : 8 * g + 8, :].astype(jnp.bfloat16)


def write_ids(ids_ref, rows, out_ref):
    sub = lax.broadcasted_iota(jnp.int32, (8, LANES), 0)
    ids = jnp.full((8, LANES), -1.0, jnp.float32)
    for r in range(rows):
        ids = jnp.where(sub == r, ids_ref[r].astype(jnp.float32), ids)
    out_ref[:, out_ref.shape[1] - LANES :] = ids.astype(jnp.bfloat16)


def norm_kernel(x_hbm, gain_hbm, out_ref, x_ref, gain_ref, sems, stage):
    copies = [
        pltpu.make_async_copy(x_hbm, x_ref, sems.at[0]),
        pltpu.make_async_copy(gain_hbm, gain_ref, sems.at[1]),
    ]
    for copy in copies:
        copy.start()
    for copy in copies:
        copy.wait()
    rows, width = x_ref.shape
    block = width // BLOCKS
    total = jnp.zeros((rows, LANES), jnp.float32)
    for c in range(width // LANES):
        x = x_ref[:, c * LANES : (c + 1) * LANES].astype(jnp.float32)
        total = total + x * x
    factor = lax.rsqrt(jnp.sum(total, axis=-1, keepdims=True) / width + EPS)
    for c in range(width // LANES):
        x = x_ref[:, c * LANES : (c + 1) * LANES].astype(jnp.float32)
        gain = gain_ref[c : c + 1, :].astype(jnp.float32)
        j, lane = c * LANES // block, c * LANES % block
        stage[j * rows : (j + 1) * rows, lane : lane + LANES] = x * factor * gain
    write_chunk(stage, rows, out_ref)


def norm_chunk(hidden, gain):
    rows, width = hidden.shape
    return pl.pallas_call(
        norm_kernel,
        out_shape=jax.ShapeDtypeStruct((8, rows * width // 8), jnp.bfloat16),
        in_specs=[HBM, HBM],
        out_specs=VMEM,
        scratch_shapes=[
            pltpu.VMEM((rows, width), jnp.bfloat16),
            pltpu.VMEM((width // LANES, LANES), jnp.bfloat16),
            pltpu.SemaphoreType.DMA((2,)),
            pltpu.VMEM((BLOCKS * rows, width // BLOCKS), jnp.float32),
        ],
        compiler_params=params(16),
        name="norm_chunk",
    )(hidden, gain.reshape(width // LANES, LANES))


def unpack_kernel(chips, rows, with_ids, *refs):
    chunks = refs[:chips]
    left, stage = refs[chips:]
    block = stage.shape[-1]
    small = chips <= 8
    for pair in range(chips // 2):
        turn = pair % 2
        for place in range(2):
            chunk = chunks[2 * pair + place]

            def widen(g, chunk=chunk, turn=turn, place=place):
                lane = g * block if small else pl.multiple_of(g * block, block)
                at = 8 * g if small else pl.multiple_of(8 * g, 8)
                wide = chunk[:, pl.ds(lane, block)].astype(jnp.float32)
                stage[turn, place, pl.ds(at, 8), :] = wide

            steps(BLOCKS * rows // 8, small, widen)
        for j in range(BLOCKS):
            both = [stage[turn, place, j * rows : j * rows + 8, :] for place in range(2)]
            left[j, 16 * pair : 16 * pair + 16, :] = jnp.concatenate(both, axis=0).astype(
                jnp.bfloat16
            )
        if with_ids:
            at = BLOCKS * rows // 8 * block
            both = [chunks[2 * pair + place][:, at : at + LANES] for place in range(2)]
            both = jnp.concatenate([ids.astype(jnp.float32) for ids in both], axis=0)
            left[BLOCKS, 16 * pair : 16 * pair + 16, :LANES] = both.astype(jnp.bfloat16)


def unpack(chunks, rows, width, with_ids):
    chips = len(chunks)
    block = width // BLOCKS
    return pl.pallas_call(
        functools.partial(unpack_kernel, chips, rows, with_ids),
        out_shape=jax.ShapeDtypeStruct((BLOCKS + with_ids, chips * 8, block), jnp.bfloat16),
        in_specs=[VMEM] * chips,
        out_specs=VMEM,
        scratch_shapes=[pltpu.VMEM((2, 2, BLOCKS * rows + 8, block), jnp.float32)],
        compiler_params=params(32),
        name="unpack",
    )(*chunks)


def hold_kernel(count, *refs):
    weight, held, _, sems = refs[count:]
    block = weight.shape[0] // BLOCKS
    copies = [
        pltpu.make_async_copy(
            weight.at[pl.ds(j * block, block), :], held.at[pl.ds(j * block, block), :], sems.at[j]
        )
        for j in range(BLOCKS)
    ]
    for copy in copies:
        copy.start()
    for copy in copies:
        copy.wait()


def hold(weight, chunk, after, mib, name):
    arrays = (chunk, *after)
    return pl.pallas_call(
        functools.partial(hold_kernel, len(arrays)),
        out_shape=(
            jax.ShapeDtypeStruct(weight.shape, weight.dtype),
            jax.ShapeDtypeStruct(chunk.shape, chunk.dtype),
        ),
        in_specs=[ANY] * len(arrays) + [HBM],
        out_specs=(VMEM, ANY),
        scratch_shapes=[pltpu.SemaphoreType.DMA((BLOCKS,))],
        input_output_aliases={0: 1},
        compiler_params=params(mib),
        cost_estimate=pl.CostEstimate(flops=0, bytes_accessed=4 * weight.size, transcendentals=0),
        name=name,
    )(*arrays, weight)


def multiply(left, held, acc):
    block = left.shape[2]
    acc[...] = jnp.zeros_like(acc)
    for j in range(BLOCKS):
        acc[...] += jnp.dot(
            left[j], held[j * block : (j + 1) * block, :], preferred_element_type=jnp.float32
        )


def own_rows(left, held, name):
    rows, cols = left.shape[1], held.shape[1]
    return pl.pallas_call(
        multiply,
        out_shape=jax.ShapeDtypeStruct((rows, cols), jnp.float32),
        in_specs=[VMEM, VMEM],
        out_specs=VMEM,
        compiler_params=params(40),
        cost_estimate=pl.CostEstimate(
            flops=2 * rows * held.size, bytes_accessed=2 * held.size, transcendentals=0
        ),
        name=name,
    )(left, held)


def qkv_kernel(devices, rows, me_ref, bias_ref, own_ref, left, held, out_ref, acc):
    multiply(left, held, acc)
    bias = bias_ref[...].astype(jnp.float32)
    core = lax.rem(me_ref[0], 2)
    for slot, chip in enumerate(slot_chips(devices, me_ref[0])):
        mine = slice(8 * slot, 8 * slot + rows)
        out_ref[2 * chip + core] = (own_ref[mine, :] + bias).astype(jnp.bfloat16)
        out_ref[2 * chip + 1 - core] = (acc[mine, :] + bias).astype(jnp.bfloat16)


def qkv_project(me, own, left, held, bias, devices, rows):
    cols = own.shape[1]
    return pl.pallas_call(
        functools.partial(qkv_kernel, devices, rows),
        out_shape=jax.ShapeDtypeStruct((devices, rows, cols), jnp.bfloat16),
        in_specs=[SMEM, VMEM, VMEM, VMEM, VMEM],
        out_specs=VMEM,
        scratch_shapes=[pltpu.VMEM(own.shape, jnp.float32)],
        compiler_params=params(40),
        name="qkv_project",
    )(me, bias, own, left, held)


def attend_kernel(
    rows,
    len_ref,
    ids_ref,
    qkv_ref,
    cos_ref,
    sin_ref,
    k_hbm,
    v_hbm,
    out_ref,
    keys,
    values,
    sems,
    heads,
    mixed,
    stage,
):
    copies = []
    for r in range(rows):
        copies.append(
            (
                pltpu.make_async_copy(k_hbm.at[r], keys.at[r], sems.at[0, r]),
                pltpu.make_async_copy(v_hbm.at[r], values.at[r], sems.at[1, r]),
            )
        )
    for of_row in copies:
        for copy in of_row:
            copy.start()
    total_heads = QUERY_HEADS + 2 * KVH
    half = HEAD_SIZE // 2
    for h in range(total_heads):
        tile = qkv_ref[:, h * HEAD_SIZE : (h + 1) * HEAD_SIZE].astype(jnp.float32)
        heads[pl.ds(h, rows, stride=total_heads), :] = tile
    scale = 1.0 / HEAD_SIZE**0.5

    for r in range(rows):
        for of_row in {0: copies[:1], 1: copies[1:3], 3: copies[3:]}.get(r, []):
            for copy in of_row:
                copy.wait()
        base = r * total_heads
        turned = heads[base : base + QUERY_HEADS + KVH, :]
        cosine = cos_ref[r : r + 1, :]
        sine = sin_ref[r : r + 1, :]
        turned = (turned * cosine + pltpu.roll(turned, half, 1) * sine).astype(jnp.bfloat16)
        query = turned[:QUERY_HEADS]
        query_f = query.astype(jnp.float32)
        new_key = turned[QUERY_HEADS:].astype(jnp.float32)
        new_value = heads[base + QUERY_HEADS + KVH : base + total_heads, :]
        scores = []
        own = []
        for k in range(KVH):
            mine = slice(k * GROUPS, (k + 1) * GROUPS)
            key = keys[r, :, k * HEAD_SIZE : (k + 1) * HEAD_SIZE]
            scores.append(
                lax.dot_general(
                    query[mine], key, (((1,), (1,)), ((), ())), preferred_element_type=jnp.float32
                )
            )
            own.append(jnp.sum(query_f[mine] * new_key[k : k + 1], axis=-1, keepdims=True))
        score = jnp.concatenate(scores, axis=0) * scale
        own = jnp.concatenate(own, axis=0) * scale
        valid = lax.broadcasted_iota(jnp.int32, score.shape, 1) < len_ref[r]
        top = jnp.maximum(jnp.max(jnp.where(valid, score, -1e30), axis=-1, keepdims=True), own)
        expo = jnp.where(valid, jnp.exp(score - top), 0.0)
        expo_own = jnp.exp(own - top)
        total = jnp.sum(expo, axis=-1, keepdims=True) + expo_own
        weight = (expo / total).astype(jnp.bfloat16)
        weight_own = (expo_own / total).astype(jnp.bfloat16).astype(jnp.float32)
        for k in range(KVH):
            mine = slice(k * GROUPS, (k + 1) * GROUPS)
            value = values[r, :, k * HEAD_SIZE : (k + 1) * HEAD_SIZE]
            part = jnp.dot(weight[mine], value, preferred_element_type=jnp.float32)
            part = part + weight_own[mine] * new_value[k : k + 1]
            at = r * QUERY_HEADS + k * GROUPS
            mixed[at : at + GROUPS, :] = part
    per_block = QUERY_HEADS // BLOCKS
    for h in range(QUERY_HEADS):
        j, lane = h // per_block, h % per_block
        stage[j * rows : (j + 1) * rows, lane * HEAD_SIZE : (lane + 1) * HEAD_SIZE] = mixed[
            pl.ds(h, rows, stride=QUERY_HEADS), :
        ]
    write_chunk(stage, rows, out_ref)
    write_ids(ids_ref, rows, out_ref)


def attend(lengths, ids, qkv, cosine, sine, keys, values):
    rows, capacity, width = keys.shape
    total_heads = QUERY_HEADS + 2 * KVH
    features = QUERY_HEADS * HEAD_SIZE
    return pl.pallas_call(
        functools.partial(attend_kernel, rows),
        out_shape=jax.ShapeDtypeStruct((8, rows * features // 8 + LANES), jnp.bfloat16),
        in_specs=[SMEM, SMEM, VMEM, VMEM, VMEM, HBM, HBM],
        out_specs=VMEM,
        scratch_shapes=[
            pltpu.VMEM(keys.shape, jnp.bfloat16),
            pltpu.VMEM(keys.shape, jnp.bfloat16),
            pltpu.SemaphoreType.DMA((2, rows)),
            pltpu.VMEM((rows * total_heads, HEAD_SIZE), jnp.float32),
            pltpu.VMEM((rows * QUERY_HEADS, HEAD_SIZE), jnp.float32),
            pltpu.VMEM((BLOCKS * rows, features // BLOCKS), jnp.float32),
        ],
        compiler_params=params(50),
        name="attend",
    )(lengths, ids, qkv, cosine, sine, keys, values)


def times_down(down_ref, left, write):
    stored, rank, features = down_ref.shape
    block = features // BLOCKS
    for s in range(stored):
        part = jnp.zeros((rank, left.shape[1]), jnp.float32)
        for j in range(BLOCKS):
            part += lax.dot_general(
                down_ref[s, :, j * block : (j + 1) * block],
                left[j],
                (((1,), (1,)), ((), ())),
                preferred_element_type=jnp.float32,
            )
        write(slice(s * rank, (s + 1) * rank), part)


def shrink_own_kernel(down_ref, left, out_ref):
    def write(at, part):
        out_ref[at, :] = part

    times_down(down_ref, left, write)


def shrink_own(left, down):
    stored, rank, features = down.shape
    return pl.pallas_call(
        shrink_own_kernel,
        out_shape=jax.ShapeDtypeStruct((stored * rank, left.shape[1]), jnp.float32),
        in_specs=[VMEM, VMEM],
        out_specs=VMEM,
        compiler_params=params(48),
        cost_estimate=pl.CostEstimate(
            flops=2 * left.size * stored * rank, bytes_accessed=2 * left.size, transcendentals=0
        ),
        name="shrink_own",
    )(down, left)


def shrink_kernel(
    devices, me_ref, down_ref, own_part, own, other, coords_ref, ids, place_of, total
):
    me = me_ref[0]
    stored, rank, _ = down_ref.shape
    rows = own.shape[1]
    total[:, :rows] = own_part[...]

    def write(at, part):
        total[at, rows:] = part

    times_down(down_ref, other, write)
    for c, left in enumerate((own, other)):
        ids[c * rows : (c + 1) * rows, :] = left[BLOCKS, :, :LANES].astype(jnp.float32)
    row_ids = jnp.transpose(ids[...])[: stored * rank, :].astype(jnp.int32)
    adapter = lax.broadcasted_iota(jnp.int32, total.shape, 0) // rank + me * stored
    coords = jnp.where(row_ids == adapter, total[...], 0.0).astype(jnp.bfloat16)
    core = lax.rem(me, 2)
    sub = lax.broadcasted_iota(jnp.int32, (8, LANES), 0)
    for slot, chip in enumerate(slot_chips(devices, me)):
        for c, place in ((0, core), (1, 1 - core)):
            at = c * rows + 8 * slot
            place_of[at : at + 8, :] = sub + (2 * chip + place) * 8
    target = lax.broadcasted_iota(jnp.int32, (2 * rows, 2 * rows), 1)
    move = jnp.where(place_of[:, :1] == target, 1.0, 0.0).astype(jnp.bfloat16)
    coords = jnp.dot(coords, move, preferred_element_type=jnp.float32).astype(jnp.bfloat16)
    for d in range(devices):
        coords_ref[d] = coords


def shrink(me, own_part, own, other, down, devices):
    stored, rank, features = down.shape
    rows = devices * 8
    return pl.pallas_call(
        functools.partial(shrink_kernel, devices),
        out_shape=jax.ShapeDtypeStruct((devices, stored * rank, rows), jnp.bfloat16),
        in_specs=[SMEM, VMEM, VMEM, VMEM, VMEM],
        out_specs=VMEM,
        scratch_shapes=[
            pltpu.VMEM((rows, LANES), jnp.float32),
            pltpu.VMEM((rows, LANES), jnp.int32),
            pltpu.VMEM((stored * rank, rows), jnp.float32),
        ],
        compiler_params=params(48),
        name="shrink",
    )(me, down, own_part, own, other)


def base_kernel(devices, me_ref, own_ref, left, held, out_ref, acc):
    multiply(left, held, acc)
    core = lax.rem(me_ref[0], 2)
    for slot, chip in enumerate(slot_chips(devices, me_ref[0])):
        mine = slice(8 * slot, 8 * slot + 8)
        at = pl.multiple_of((2 * chip + core) * 8, 8)
        out_ref[pl.ds(at, 8), :] = own_ref[mine, :]
        at = pl.multiple_of((2 * chip + 1 - core) * 8, 8)
        out_ref[pl.ds(at, 8), :] = acc[mine, :]


def base_project(me, own, left, held, devices):
    rows, cols = own.shape
    return pl.pallas_call(
        functools.partial(base_kernel, devices),
        out_shape=jax.ShapeDtypeStruct((2 * rows, cols), jnp.float32),
        in_specs=[SMEM, VMEM, VMEM, VMEM],
        out_specs=VMEM,
        scratch_shapes=[pltpu.VMEM(own.shape, jnp.float32)],
        compiler_params=params(40),
        cost_estimate=pl.CostEstimate(
            flops=2 * rows * held.size, bytes_accessed=2 * held.size, transcendentals=0
        ),
        name="base_project",
    )(me, own, left, held)


def add_kernel(rows, base_ref, coords_ref, up_ref, out_ref):
    delta = lax.dot_general(
        coords_ref[...], up_ref[...], (((0,), (0,)), ((), ())), preferred_element_type=jnp.float32
    )
    projected = base_ref[...] + delta
    for d in range(out_ref.shape[0]):
        out_ref[d] = projected[8 * d : 8 * d + rows, :].astype(jnp.bfloat16)


def add_delta(base, coords, up, rows):
    return pl.pallas_call(
        functools.partial(add_kernel, rows),
        out_shape=jax.ShapeDtypeStruct((base.shape[0] // 8, rows, base.shape[1]), jnp.bfloat16),
        in_specs=[VMEM, VMEM, VMEM],
        out_specs=VMEM,
        compiler_params=params(40),
        name="add_delta",
    )(base, coords, up)


def exchange(parts):
    return lax.all_to_all(parts, "tensor", split_axis=0, concat_axis=0, tiled=True)


def per_row(parts):
    devices, rows, cols = parts.shape
    return jnp.transpose(parts, (1, 0, 2)).reshape(rows, devices * cols)


def per_device(
    devices,
    hidden,
    input_norm_scale,
    query_key_value_weight,
    projection_bias,
    rotated_key_cache,
    past_value_cache,
    lengths,
    row_adapter_index,
    output_weight,
    adapter_down_weight,
    adapter_up_weight,
):
    rows = hidden.shape[0]
    me = lax.axis_index("tensor").astype(jnp.int32).reshape(1)
    half = HEAD_SIZE // 2
    inv = ROPE_BASE ** (-(jnp.arange(half, dtype=jnp.float32) * 2.0 / HEAD_SIZE))
    angle = lengths.astype(jnp.float32)[:, None] * inv[None, :]
    cosine, sine = jnp.cos(angle), jnp.sin(angle)
    cosine = jnp.concatenate([cosine, cosine], axis=1)
    sine = jnp.concatenate([-sine, sine], axis=1)
    down = jnp.transpose(adapter_down_weight, (0, 2, 1))
    up = adapter_up_weight.reshape(-1, adapter_up_weight.shape[2])

    bias = projection_bias.reshape(1, -1)
    tables = (bias, cosine, sine)
    chunks, held = gather_chunks(
        norm_chunk(hidden, input_norm_scale),
        devices,
        lambda chunk: hold(query_key_value_weight, chunk, tables, 40, "hold_qkv"),
    )
    mine = unpack(chunks, rows, hidden.shape[1], False)
    theirs = across(mine, devices)
    own = own_rows(mine, held, "qkv_own")
    qkv = qkv_project(me, own, theirs, held, bias, devices, rows)
    qkv = per_row(exchange(qkv))
    chunk = attend(
        lengths, row_adapter_index, qkv, cosine, sine, rotated_key_cache, past_value_cache
    )
    chunks, held = gather_chunks(
        chunk, devices, lambda chunk: hold(output_weight, chunk, (), 42, "hold_output")
    )
    mine = unpack(chunks, rows, QUERY_HEADS * HEAD_SIZE, True)
    theirs = across(mine, devices)
    own_part = shrink_own(mine, down)
    own = own_rows(mine, held, "base_own")
    coords = exchange(shrink(me, own_part, mine, theirs, down, devices))
    base = base_project(me, own, theirs, held, devices)
    coords = coords.reshape(-1, coords.shape[2])
    return per_row(exchange(add_delta(base, coords, up, rows)))


def solution(mesh):
    in_specs = (
        P(("group", "tensor"), None),
        P(),
        P(None, "tensor"),
        P("tensor"),
        P(("group", "tensor"), None, None),
        P(("group", "tensor"), None, None),
        P(("group", "tensor")),
        P(("group", "tensor")),
        P(None, "tensor"),
        P("tensor", None, None),
        P(None, None, "tensor"),
    )
    out_specs = P(("group", "tensor"), None)
    return jax.shard_map(
        functools.partial(per_device, mesh.shape["tensor"]),
        mesh=mesh,
        in_specs=in_specs,
        out_specs=out_specs,
        check_vma=False,
    )
```

```python
import functools

import jax
import jax.numpy as jnp
from jax import lax
from jax.experimental import pallas as pl
from jax.experimental.pallas import tpu as pltpu
from jax.sharding import PartitionSpec as P

QUERY_HEADS = 64
KVH = 8
HEAD_SIZE = 128
ADAPTER_RANK = 16
GROUPS = QUERY_HEADS // KVH

EPS = 1e-06
ROPE_BASE = 1000000.0

BLOCKS = 8
LANES = 128
MIB = 1 << 20

VMEM = pl.BlockSpec(memory_space=pltpu.VMEM)
HBM = pl.BlockSpec(memory_space=pltpu.HBM)
ANY = pl.BlockSpec(memory_space=pl.ANY)
SMEM = pl.BlockSpec(memory_space=pltpu.SMEM)


def params(mib):
    return pltpu.CompilerParams(vmem_limit_bytes=mib * MIB)


def factors(chips):
    inner = 1
    while inner * inner * 4 <= chips and chips % (inner * 2) == 0:
        inner *= 2
    return chips // inner, inner


def slot_chips(devices, me):
    outer, inner = factors(devices // 2)
    chip = lax.div(me, 2)
    a, b = lax.div(chip, inner), lax.rem(chip, inner)
    return [
        partner(a, k, outer, -1) * inner + partner(b, m, inner, -1)
        for m in range(inner)
        for k in range(outer)
    ]


def partner(at, step, size, sign=1):
    if size & (size - 1) == 0:
        return at ^ step
    return (at + sign * step + size) % size


def steps(count, unrolled, body):
    if unrolled:
        for i in range(count):
            body(i)
    else:
        lax.fori_loop(0, count, lambda i, _: (body(i), 0)[1], 0)


def gather_chunks(chunk, devices, meanwhile):
    outer, inner = factors(devices // 2)

    def pairs(k, m):
        return [
            (d, 2 * (partner(d // 2 // inner, k, outer) * inner + partner(d // 2 % inner, m, inner)) + d % 2)
            for d in range(devices)
        ]

    line = [chunk] + [lax.ppermute(chunk, "tensor", pairs(k, 0)) for k in range(1, outer)]
    held, line[outer // 4] = meanwhile(line[outer // 4])
    slots = {}
    for k in range(outer):
        for m in range(1, inner):
            slots[k, m] = lax.ppermute(line[k], "tensor", pairs(0, m))
    for k in range(outer):
        slots[k, 0] = line[k]
    return [slots[k, m] for m in range(inner) for k in range(outer)], held


def neighbours(devices):
    inner = factors(devices // 2)[1]
    return [(m, c) for m in range(inner) for c in range(2)]


def to_neighbour(x, devices, m, c):
    inner = factors(devices // 2)[1]
    return lax.ppermute(
        x,
        "tensor",
        [
            (d, 2 * (d // 2 // inner * inner + partner(d // 2 % inner, m, inner)) + (d % 2 ^ c))
            for d in range(devices)
        ],
    )


def along_line(x, devices, k):
    outer, inner = factors(devices // 2)
    return lax.ppermute(
        x,
        "tensor",
        [
            (d, 2 * (partner(d // 2 // inner, k, outer) * inner + d // 2 % inner) + d % 2)
            for d in range(devices)
        ],
    )


def source(devices, me, k, m, c):
    outer, inner = factors(devices // 2)
    chip = lax.div(me, 2)
    a, b = lax.div(chip, inner), lax.rem(chip, inner)
    chip = partner(a, k, outer, -1) * inner + partner(b, m, inner, -1)
    return 2 * chip + (lax.rem(me, 2) ^ c)


def join_kernel(*refs):
    parts, out_ref = refs[:-1], refs[-1]
    rows = parts[0].shape[0]
    for at, part in enumerate(parts):
        out_ref[at * rows : (at + 1) * rows, :] = part[...]


def gather_coords(coords, devices):
    around = [coords if mc == (0, 0) else to_neighbour(coords, devices, *mc) for mc in neighbours(devices)]
    rows, cols = coords.shape
    joined = pl.pallas_call(
        join_kernel,
        out_shape=jax.ShapeDtypeStruct((len(around) * rows, cols), coords.dtype),
        in_specs=[VMEM] * len(around),
        out_specs=VMEM,
        compiler_params=params(16),
        name="join_coords",
    )(*around)
    outer = factors(devices // 2)[0]
    return [joined] + [along_line(joined, devices, k) for k in range(1, outer)]


def across(x, devices):
    return lax.ppermute(x, "tensor", [(d, d ^ 1) for d in range(devices)])


def write_chunk(stage, rows, out_ref):
    block = stage.shape[1]
    for g in range(BLOCKS * rows // 8):
        out_ref[:, g * block : (g + 1) * block] = stage[8 * g : 8 * g + 8, :].astype(jnp.bfloat16)


def write_ids(ids_ref, rows, out_ref):
    sub = lax.broadcasted_iota(jnp.int32, (8, LANES), 0)
    ids = jnp.full((8, LANES), -1.0, jnp.float32)
    for r in range(rows):
        ids = jnp.where(sub == r, ids_ref[r].astype(jnp.float32), ids)
    out_ref[:, out_ref.shape[1] - LANES :] = ids.astype(jnp.bfloat16)


def norm_kernel(x_hbm, gain_hbm, out_ref, x_ref, gain_ref, sems, stage):
    copies = [
        pltpu.make_async_copy(x_hbm, x_ref, sems.at[0]),
        pltpu.make_async_copy(gain_hbm, gain_ref, sems.at[1]),
    ]
    for copy in copies:
        copy.start()
    for copy in copies:
        copy.wait()
    rows, width = x_ref.shape
    block = width // BLOCKS
    total = jnp.zeros((rows, LANES), jnp.float32)
    for c in range(width // LANES):
        x = x_ref[:, c * LANES : (c + 1) * LANES].astype(jnp.float32)
        total = total + x * x
    factor = lax.rsqrt(jnp.sum(total, axis=-1, keepdims=True) / width + EPS)
    for c in range(width // LANES):
        x = x_ref[:, c * LANES : (c + 1) * LANES].astype(jnp.float32)
        gain = gain_ref[c : c + 1, :].astype(jnp.float32)
        j, lane = c * LANES // block, c * LANES % block
        stage[j * rows : (j + 1) * rows, lane : lane + LANES] = x * factor * gain
    write_chunk(stage, rows, out_ref)


def norm_chunk(hidden, gain):
    rows, width = hidden.shape
    return pl.pallas_call(
        norm_kernel,
        out_shape=jax.ShapeDtypeStruct((8, rows * width // 8), jnp.bfloat16),
        in_specs=[HBM, HBM],
        out_specs=VMEM,
        scratch_shapes=[
            pltpu.VMEM((rows, width), jnp.bfloat16),
            pltpu.VMEM((width // LANES, LANES), jnp.bfloat16),
            pltpu.SemaphoreType.DMA((2,)),
            pltpu.VMEM((BLOCKS * rows, width // BLOCKS), jnp.float32),
        ],
        compiler_params=params(16),
        name="norm_chunk",
    )(hidden, gain.reshape(width // LANES, LANES))


def unpack_kernel(chips, rows, with_ids, *refs):
    chunks = refs[:chips]
    left, stage = refs[chips:]
    block = stage.shape[-1]
    small = chips <= 8
    for pair in range(chips // 2):
        turn = pair % 2
        for place in range(2):
            chunk = chunks[2 * pair + place]

            def widen(g, chunk=chunk, turn=turn, place=place):
                lane = g * block if small else pl.multiple_of(g * block, block)
                at = 8 * g if small else pl.multiple_of(8 * g, 8)
                wide = chunk[:, pl.ds(lane, block)].astype(jnp.float32)
                stage[turn, place, pl.ds(at, 8), :] = wide

            steps(BLOCKS * rows // 8, small, widen)
        for j in range(BLOCKS):
            both = [stage[turn, place, j * rows : j * rows + 8, :] for place in range(2)]
            left[j, 16 * pair : 16 * pair + 16, :] = jnp.concatenate(both, axis=0).astype(
                jnp.bfloat16
            )
        if with_ids:
            at = BLOCKS * rows // 8 * block
            both = [chunks[2 * pair + place][:, at : at + LANES] for place in range(2)]
            both = jnp.concatenate([ids.astype(jnp.float32) for ids in both], axis=0)
            left[BLOCKS, 16 * pair : 16 * pair + 16, :LANES] = both.astype(jnp.bfloat16)


def unpack(chunks, rows, width, with_ids):
    chips = len(chunks)
    block = width // BLOCKS
    return pl.pallas_call(
        functools.partial(unpack_kernel, chips, rows, with_ids),
        out_shape=jax.ShapeDtypeStruct((BLOCKS + with_ids, chips * 8, block), jnp.bfloat16),
        in_specs=[VMEM] * chips,
        out_specs=VMEM,
        scratch_shapes=[pltpu.VMEM((2, 2, BLOCKS * rows + 8, block), jnp.float32)],
        compiler_params=params(32),
        name="unpack",
    )(*chunks)


def hold_kernel(count, *refs):
    weight, held, _, sems = refs[count:]
    block = weight.shape[0] // BLOCKS
    copies = [
        pltpu.make_async_copy(
            weight.at[pl.ds(j * block, block), :], held.at[pl.ds(j * block, block), :], sems.at[j]
        )
        for j in range(BLOCKS)
    ]
    for copy in copies:
        copy.start()
    for copy in copies:
        copy.wait()


def hold(weight, chunk, after, mib, name):
    arrays = (chunk, *after)
    return pl.pallas_call(
        functools.partial(hold_kernel, len(arrays)),
        out_shape=(
            jax.ShapeDtypeStruct(weight.shape, weight.dtype),
            jax.ShapeDtypeStruct(chunk.shape, chunk.dtype),
        ),
        in_specs=[ANY] * len(arrays) + [HBM],
        out_specs=(VMEM, ANY),
        scratch_shapes=[pltpu.SemaphoreType.DMA((BLOCKS,))],
        input_output_aliases={0: 1},
        compiler_params=params(mib),
        cost_estimate=pl.CostEstimate(flops=0, bytes_accessed=4 * weight.size, transcendentals=0),
        name=name,
    )(*arrays, weight)


def multiply(left, held, acc):
    block = left.shape[2]
    acc[...] = jnp.zeros_like(acc)
    for j in range(BLOCKS):
        acc[...] += jnp.dot(
            left[j], held[j * block : (j + 1) * block, :], preferred_element_type=jnp.float32
        )


def own_rows(left, held, name):
    rows, cols = left.shape[1], held.shape[1]
    return pl.pallas_call(
        multiply,
        out_shape=jax.ShapeDtypeStruct((rows, cols), jnp.float32),
        in_specs=[VMEM, VMEM],
        out_specs=VMEM,
        compiler_params=params(40),
        cost_estimate=pl.CostEstimate(
            flops=2 * rows * held.size, bytes_accessed=2 * held.size, transcendentals=0
        ),
        name=name,
    )(left, held)


def cache_copies(cache, kept, sems):
    return [
        pltpu.make_async_copy(cache.at[r], kept.at[r], sems.at[r]) for r in range(cache.shape[0])
    ]


def qkv_own_kernel(left, held, cache, acc, kept, sems):
    copies = cache_copies(cache, kept, sems)
    for copy in copies:
        copy.start()
    multiply(left, held, acc)
    for copy in copies:
        copy.wait()


def qkv_own(left, held, cache):
    rows, cols = left.shape[1], held.shape[1]
    return pl.pallas_call(
        qkv_own_kernel,
        out_shape=(
            jax.ShapeDtypeStruct((rows, cols), jnp.float32),
            jax.ShapeDtypeStruct(cache.shape, cache.dtype),
        ),
        in_specs=[VMEM, VMEM, HBM],
        out_specs=(VMEM, VMEM),
        scratch_shapes=[pltpu.SemaphoreType.DMA((cache.shape[0],))],
        compiler_params=params(32),
        cost_estimate=pl.CostEstimate(
            flops=2 * rows * held.size, bytes_accessed=2 * held.size, transcendentals=0
        ),
        name="qkv_own",
    )(left, held, cache)


def qkv_kernel(
    devices, rows, me_ref, bias_ref, own_ref, left, held, cache, out_ref, kept, acc, sems
):
    copies = cache_copies(cache, kept, sems)
    for copy in copies:
        copy.start()
    multiply(left, held, acc)
    bias = bias_ref[...].astype(jnp.float32)
    core = lax.rem(me_ref[0], 2)
    for slot, chip in enumerate(slot_chips(devices, me_ref[0])):
        mine = slice(8 * slot, 8 * slot + rows)
        out_ref[2 * chip + core] = (own_ref[mine, :] + bias).astype(jnp.bfloat16)
        out_ref[2 * chip + 1 - core] = (acc[mine, :] + bias).astype(jnp.bfloat16)
    for copy in copies:
        copy.wait()


def qkv_project(me, own, left, held, bias, cache, devices, rows):
    cols = own.shape[1]
    return pl.pallas_call(
        functools.partial(qkv_kernel, devices, rows),
        out_shape=(
            jax.ShapeDtypeStruct((devices, rows, cols), jnp.bfloat16),
            jax.ShapeDtypeStruct(cache.shape, cache.dtype),
        ),
        in_specs=[SMEM, VMEM, VMEM, VMEM, VMEM, HBM],
        out_specs=(VMEM, VMEM),
        scratch_shapes=[
            pltpu.VMEM(own.shape, jnp.float32),
            pltpu.SemaphoreType.DMA((cache.shape[0],)),
        ],
        compiler_params=params(28),
        name="qkv_project",
    )(me, bias, own, left, held, cache)


def attend_kernel(
    rows,
    len_ref,
    ids_ref,
    qkv_ref,
    cos_ref,
    sin_ref,
    keys,
    values,
    out_ref,
    heads,
    mixed,
    stage,
):
    total_heads = QUERY_HEADS + 2 * KVH
    half = HEAD_SIZE // 2
    for h in range(total_heads):
        tile = qkv_ref[:, h * HEAD_SIZE : (h + 1) * HEAD_SIZE].astype(jnp.float32)
        heads[pl.ds(h, rows, stride=total_heads), :] = tile
    scale = 1.0 / HEAD_SIZE**0.5

    for r in range(rows):
        base = r * total_heads
        turned = heads[base : base + QUERY_HEADS + KVH, :]
        cosine = cos_ref[r : r + 1, :]
        sine = sin_ref[r : r + 1, :]
        turned = (turned * cosine + pltpu.roll(turned, half, 1) * sine).astype(jnp.bfloat16)
        query = turned[:QUERY_HEADS]
        query_f = query.astype(jnp.float32)
        new_key = turned[QUERY_HEADS:].astype(jnp.float32)
        new_value = heads[base + QUERY_HEADS + KVH : base + total_heads, :]
        scores = []
        own = []
        for k in range(KVH):
            mine = slice(k * GROUPS, (k + 1) * GROUPS)
            key = keys[r, :, k * HEAD_SIZE : (k + 1) * HEAD_SIZE]
            scores.append(
                lax.dot_general(
                    query[mine], key, (((1,), (1,)), ((), ())), preferred_element_type=jnp.float32
                )
            )
            own.append(jnp.sum(query_f[mine] * new_key[k : k + 1], axis=-1, keepdims=True))
        score = jnp.concatenate(scores, axis=0) * scale
        own = jnp.concatenate(own, axis=0) * scale
        valid = lax.broadcasted_iota(jnp.int32, score.shape, 1) < len_ref[r]
        top = jnp.maximum(jnp.max(jnp.where(valid, score, -1e30), axis=-1, keepdims=True), own)
        expo = jnp.where(valid, jnp.exp(score - top), 0.0)
        expo_own = jnp.exp(own - top)
        total = jnp.sum(expo, axis=-1, keepdims=True) + expo_own
        weight = (expo / total).astype(jnp.bfloat16)
        weight_own = (expo_own / total).astype(jnp.bfloat16).astype(jnp.float32)
        for k in range(KVH):
            mine = slice(k * GROUPS, (k + 1) * GROUPS)
            value = values[r, :, k * HEAD_SIZE : (k + 1) * HEAD_SIZE]
            part = jnp.dot(weight[mine], value, preferred_element_type=jnp.float32)
            part = part + weight_own[mine] * new_value[k : k + 1]
            at = r * QUERY_HEADS + k * GROUPS
            mixed[at : at + GROUPS, :] = part
    per_block = QUERY_HEADS // BLOCKS
    for h in range(QUERY_HEADS):
        j, lane = h // per_block, h % per_block
        stage[j * rows : (j + 1) * rows, lane * HEAD_SIZE : (lane + 1) * HEAD_SIZE] = mixed[
            pl.ds(h, rows, stride=QUERY_HEADS), :
        ]
    write_chunk(stage, rows, out_ref)
    write_ids(ids_ref, rows, out_ref)


def attend(lengths, ids, qkv, cosine, sine, keys, values):
    rows, capacity, width = keys.shape
    total_heads = QUERY_HEADS + 2 * KVH
    features = QUERY_HEADS * HEAD_SIZE
    return pl.pallas_call(
        functools.partial(attend_kernel, rows),
        out_shape=jax.ShapeDtypeStruct((8, rows * features // 8 + LANES), jnp.bfloat16),
        in_specs=[SMEM, SMEM, VMEM, VMEM, VMEM, VMEM, VMEM],
        out_specs=VMEM,
        scratch_shapes=[
            pltpu.VMEM((rows * total_heads, HEAD_SIZE), jnp.float32),
            pltpu.VMEM((rows * QUERY_HEADS, HEAD_SIZE), jnp.float32),
            pltpu.VMEM((BLOCKS * rows, features // BLOCKS), jnp.float32),
        ],
        compiler_params=params(24),
        name="attend",
    )(lengths, ids, qkv, cosine, sine, keys, values)


def times_down(down_ref, left, write):
    stored, rank, features = down_ref.shape
    block = features // BLOCKS
    for s in range(stored):
        part = jnp.zeros((rank, left.shape[1]), jnp.float32)
        for j in range(BLOCKS):
            part += lax.dot_general(
                down_ref[s, :, j * block : (j + 1) * block],
                left[j],
                (((1,), (1,)), ((), ())),
                preferred_element_type=jnp.float32,
            )
        write(slice(s * rank, (s + 1) * rank), part)


def shrink_own_kernel(down_ref, left, out_ref):
    def write(at, part):
        out_ref[at, :] = part

    times_down(down_ref, left, write)


def shrink_own(left, down):
    stored, rank, features = down.shape
    return pl.pallas_call(
        shrink_own_kernel,
        out_shape=jax.ShapeDtypeStruct((stored * rank, left.shape[1]), jnp.float32),
        in_specs=[VMEM, VMEM],
        out_specs=VMEM,
        compiler_params=params(48),
        cost_estimate=pl.CostEstimate(
            flops=2 * left.size * stored * rank, bytes_accessed=2 * left.size, transcendentals=0
        ),
        name="shrink_own",
    )(down, left)


def shrink_kernel(
    devices, me_ref, down_ref, own_part, own, other, coords_ref, ids, place_of, total
):
    me = me_ref[0]
    stored, rank, _ = down_ref.shape
    rows = own.shape[1]
    total[:, :rows] = own_part[...]

    def write(at, part):
        total[at, rows:] = part

    times_down(down_ref, other, write)
    for c, left in enumerate((own, other)):
        ids[c * rows : (c + 1) * rows, :] = left[BLOCKS, :, :LANES].astype(jnp.float32)
    row_ids = jnp.transpose(ids[...])[: stored * rank, :].astype(jnp.int32)
    adapter = lax.broadcasted_iota(jnp.int32, total.shape, 0) // rank + me * stored
    coords = jnp.where(row_ids == adapter, total[...], 0.0).astype(jnp.bfloat16)
    core = lax.rem(me, 2)
    sub = lax.broadcasted_iota(jnp.int32, (8, LANES), 0)
    for slot, chip in enumerate(slot_chips(devices, me)):
        for c, place in ((0, core), (1, 1 - core)):
            at = c * rows + 8 * slot
            place_of[at : at + 8, :] = sub + (2 * chip + place) * 8
    target = lax.broadcasted_iota(jnp.int32, (2 * rows, 2 * rows), 1)
    move = jnp.where(place_of[:, :1] == target, 1.0, 0.0).astype(jnp.bfloat16)
    coords = jnp.dot(coords, move, preferred_element_type=jnp.float32).astype(jnp.bfloat16)
    coords_ref[...] = coords


def shrink(me, own_part, own, other, down, devices):
    stored, rank, features = down.shape
    rows = devices * 8
    return pl.pallas_call(
        functools.partial(shrink_kernel, devices),
        out_shape=jax.ShapeDtypeStruct((stored * rank, rows), jnp.bfloat16),
        in_specs=[SMEM, VMEM, VMEM, VMEM, VMEM],
        out_specs=VMEM,
        scratch_shapes=[
            pltpu.VMEM((rows, LANES), jnp.float32),
            pltpu.VMEM((rows, LANES), jnp.int32),
            pltpu.VMEM((stored * rank, rows), jnp.float32),
        ],
        compiler_params=params(48),
        name="shrink",
    )(me, down, own_part, own, other)


def base_kernel(devices, me_ref, own_ref, left, held, out_ref, acc):
    multiply(left, held, acc)
    core = lax.rem(me_ref[0], 2)
    for slot, chip in enumerate(slot_chips(devices, me_ref[0])):
        mine = slice(8 * slot, 8 * slot + 8)
        at = pl.multiple_of((2 * chip + core) * 8, 8)
        out_ref[pl.ds(at, 8), :] = own_ref[mine, :]
        at = pl.multiple_of((2 * chip + 1 - core) * 8, 8)
        out_ref[pl.ds(at, 8), :] = acc[mine, :]


def base_project(me, own, left, held, devices):
    rows, cols = own.shape
    return pl.pallas_call(
        functools.partial(base_kernel, devices),
        out_shape=jax.ShapeDtypeStruct((2 * rows, cols), jnp.float32),
        in_specs=[SMEM, VMEM, VMEM, VMEM],
        out_specs=VMEM,
        scratch_shapes=[pltpu.VMEM(own.shape, jnp.float32)],
        compiler_params=params(40),
        cost_estimate=pl.CostEstimate(
            flops=2 * rows * held.size, bytes_accessed=2 * held.size, transcendentals=0
        ),
        name="base_project",
    )(me, own, left, held)


def add_kernel(devices, rows, me_ref, base_ref, up_ref, *refs):
    lines, (out_ref, coords) = refs[:-2], refs[-2:]
    part = coords.shape[1]
    for k, line in enumerate(lines):
        for at, (m, c) in enumerate(neighbours(devices)):
            coords[source(devices, me_ref[0], k, m, c)] = line[at * part : (at + 1) * part, :]
    delta = lax.dot_general(
        coords[...].reshape(devices * part, coords.shape[2]),
        up_ref[...],
        (((0,), (0,)), ((), ())),
        preferred_element_type=jnp.float32,
    )
    projected = base_ref[...] + delta
    for d in range(devices):
        out_ref[d] = projected[8 * d : 8 * d + rows, :].astype(jnp.bfloat16)


def add_delta(me, base, lines, up, devices, rows):
    part = up.shape[0] // devices
    return pl.pallas_call(
        functools.partial(add_kernel, devices, rows),
        out_shape=jax.ShapeDtypeStruct((devices, rows, base.shape[1]), jnp.bfloat16),
        in_specs=[SMEM, VMEM, VMEM] + [VMEM] * len(lines),
        out_specs=VMEM,
        scratch_shapes=[pltpu.VMEM((devices, part, lines[0].shape[1]), jnp.bfloat16)],
        compiler_params=params(48),
        name="add_delta",
    )(me, base, up, *lines)


def exchange(parts):
    return lax.all_to_all(parts, "tensor", split_axis=0, concat_axis=0, tiled=True)


def per_row(parts):
    devices, rows, cols = parts.shape
    return jnp.transpose(parts, (1, 0, 2)).reshape(rows, devices * cols)


def per_device(
    devices,
    hidden,
    input_norm_scale,
    query_key_value_weight,
    projection_bias,
    rotated_key_cache,
    past_value_cache,
    lengths,
    row_adapter_index,
    output_weight,
    adapter_down_weight,
    adapter_up_weight,
):
    rows = hidden.shape[0]
    me = lax.axis_index("tensor").astype(jnp.int32).reshape(1)
    half = HEAD_SIZE // 2
    inv = ROPE_BASE ** (-(jnp.arange(half, dtype=jnp.float32) * 2.0 / HEAD_SIZE))
    angle = lengths.astype(jnp.float32)[:, None] * inv[None, :]
    cosine, sine = jnp.cos(angle), jnp.sin(angle)
    cosine = jnp.concatenate([cosine, cosine], axis=1)
    sine = jnp.concatenate([-sine, sine], axis=1)
    down = jnp.transpose(adapter_down_weight, (0, 2, 1))
    up = adapter_up_weight.reshape(-1, adapter_up_weight.shape[2])

    bias = projection_bias.reshape(1, -1)
    chunks, held = gather_chunks(
        norm_chunk(hidden, input_norm_scale),
        devices,
        lambda chunk: hold(query_key_value_weight, chunk, (me,), 40, "hold_qkv"),
    )
    mine = unpack(chunks, rows, hidden.shape[1], False)
    theirs = across(mine, devices)
    own, keys = qkv_own(mine, held, rotated_key_cache)
    qkv, values = qkv_project(
        me, own, theirs, held, bias, past_value_cache, devices, rows
    )
    qkv = per_row(exchange(qkv))
    chunk = attend(lengths, row_adapter_index, qkv, cosine, sine, keys, values)
    chunks, held = gather_chunks(
        chunk, devices, lambda chunk: hold(output_weight, chunk, (), 42, "hold_output")
    )
    mine = unpack(chunks, rows, QUERY_HEADS * HEAD_SIZE, True)
    theirs = across(mine, devices)
    own_part = shrink_own(mine, down)
    own = own_rows(mine, held, "base_own")
    lines = gather_coords(shrink(me, own_part, mine, theirs, down, devices), devices)
    base = base_project(me, own, theirs, held, devices)
    return per_row(exchange(add_delta(me, base, lines, up, devices, rows)))


def solution(mesh):
    in_specs = (
        P(("group", "tensor"), None),
        P(),
        P(None, "tensor"),
        P("tensor"),
        P(("group", "tensor"), None, None),
        P(("group", "tensor"), None, None),
        P(("group", "tensor")),
        P(("group", "tensor")),
        P(None, "tensor"),
        P("tensor", None, None),
        P(None, None, "tensor"),
    )
    out_specs = P(("group", "tensor"), None)
    return jax.shard_map(
        functools.partial(per_device, mesh.shape["tensor"]),
        mesh=mesh,
        in_specs=in_specs,
        out_specs=out_specs,
        check_vma=False,
    )
```

```python
import functools

import jax
import jax.numpy as jnp
from jax import lax
from jax.experimental import pallas as pl
from jax.experimental.pallas import tpu as pltpu
from jax.sharding import PartitionSpec as P

QUERY_HEADS = 64
KVH = 8
HEAD_SIZE = 128
ADAPTER_RANK = 16
GROUPS = QUERY_HEADS // KVH

EPS = 1e-06
ROPE_BASE = 1000000.0

BLOCKS = 8
LANES = 128
MIB = 1 << 20

VMEM = pl.BlockSpec(memory_space=pltpu.VMEM)
HBM = pl.BlockSpec(memory_space=pltpu.HBM)
ANY = pl.BlockSpec(memory_space=pl.ANY)
SMEM = pl.BlockSpec(memory_space=pltpu.SMEM)


def params(mib):
    return pltpu.CompilerParams(vmem_limit_bytes=mib * MIB)


def factors(chips):
    inner = 1
    while inner * inner * 4 <= chips and chips % (inner * 2) == 0:
        inner *= 2
    return chips // inner, inner


def slot_chips(devices, me):
    outer, inner = factors(devices // 2)
    return [lax.div(place(devices, me, k, m, 0), 2) for m in range(inner) for k in range(outer)]


def steps(count, unrolled, body):
    if unrolled:
        for i in range(count):
            body(i)
    else:
        lax.fori_loop(0, count, lambda i, _: (body(i), 0)[1], 0)


def gather_chunks(chunk, devices, meanwhile):
    outer, inner = factors(devices // 2)

    line = [chunk] + [move(chunk, devices, k, 0, 0) for k in range(1, outer)]
    held, line[outer // 4] = meanwhile(line[outer // 4])
    slots = {}
    for k in range(outer):
        for m in range(1, inner):
            slots[k, m] = move(line[k], devices, 0, m, 0)
    for k in range(outer):
        slots[k, 0] = line[k]
    return [slots[k, m] for m in range(inner) for k in range(outer)], held


def neighbours(devices):
    return [(m, c) for m in range(factors(devices // 2)[1]) for c in range(2)]


def place(devices, d, k, m, c):
    outer, inner = factors(devices // 2)
    return 2 * ((d // 2 // inner ^ k) * inner + (d // 2 % inner ^ m)) + (d % 2 ^ c)


def move(x, devices, k, m, c):
    return lax.ppermute(
        x, "tensor", [(d, place(devices, d, k, m, c)) for d in range(devices)]
    )


def join_kernel(*refs):
    parts, out_ref = refs[:-1], refs[-1]
    rows = parts[0].shape[0]
    for at, part in enumerate(parts):
        out_ref[at * rows : (at + 1) * rows, :] = part[...]


def gather_coords(coords, devices):
    around = [coords if mc == (0, 0) else move(coords, devices, 0, *mc) for mc in neighbours(devices)]
    rows, cols = coords.shape
    joined = pl.pallas_call(
        join_kernel,
        out_shape=jax.ShapeDtypeStruct((len(around) * rows, cols), coords.dtype),
        in_specs=[VMEM] * len(around),
        out_specs=VMEM,
        compiler_params=params(16),
        name="join_coords",
    )(*around)
    outer = factors(devices // 2)[0]
    return [joined] + [move(joined, devices, k, 0, 0) for k in range(1, outer)]


def turn_kernel(devices, me_ref, *refs):
    outer, _ = factors(devices // 2)
    parts, outs = refs[:outer], refs[outer:]
    in_plane = [lax.rem(place(devices, me_ref[0], 0, m, c), len(outs)) for m, c in neighbours(devices)]
    for out_ref, at in zip(outs, in_plane):
        for k in range(outer):
            out_ref[k] = parts[k][at]


def exchange(parts, me, devices):
    outer, _ = factors(devices // 2)
    around = neighbours(devices)
    _, rows, cols = parts[0].shape
    arrived = [parts[0]] + [move(parts[k], devices, k, 0, 0) for k in range(1, outer)]
    turned = pl.pallas_call(
        functools.partial(turn_kernel, devices),
        out_shape=[jax.ShapeDtypeStruct((outer, rows, cols), parts[0].dtype) for _ in around],
        in_specs=[SMEM] + [VMEM] * outer,
        out_specs=[VMEM] * len(around),
        compiler_params=params(16),
        name="turn",
    )(me, *arrived)
    return [x if mc == (0, 0) else move(x, devices, 0, *mc) for x, mc in zip(turned, around)]


def in_order(devices, me, parts, ordered):
    for part, (m, c) in zip(parts, neighbours(devices)):
        for k in range(part.shape[0]):
            ordered[place(devices, me, k, m, c)] = part[k]


def collect_kernel(devices, me_ref, *refs):
    parts, (out_ref, ordered) = refs[:-2], refs[-2:]
    in_order(devices, me_ref[0], parts, ordered)
    cols = ordered.shape[2]
    for d in range(devices):
        out_ref[:, d * cols : (d + 1) * cols] = ordered[d]


def collect(me, parts, devices):
    _, rows, cols = parts[0].shape
    return pl.pallas_call(
        functools.partial(collect_kernel, devices),
        out_shape=jax.ShapeDtypeStruct((rows, devices * cols), parts[0].dtype),
        in_specs=[SMEM] + [VMEM] * len(parts),
        out_specs=VMEM,
        scratch_shapes=[pltpu.VMEM((devices, rows, cols), parts[0].dtype)],
        compiler_params=params(16),
        name="collect",
    )(me, *parts)


def across(x, devices):
    return lax.ppermute(x, "tensor", [(d, d ^ 1) for d in range(devices)])


def write_chunk(stage, rows, out_ref):
    block = stage.shape[1]
    for g in range(BLOCKS * rows // 8):
        out_ref[:, g * block : (g + 1) * block] = stage[8 * g : 8 * g + 8, :].astype(jnp.bfloat16)


def write_ids(ids_ref, rows, out_ref):
    sub = lax.broadcasted_iota(jnp.int32, (8, LANES), 0)
    ids = jnp.full((8, LANES), -1.0, jnp.float32)
    for r in range(rows):
        ids = jnp.where(sub == r, ids_ref[r].astype(jnp.float32), ids)
    out_ref[:, out_ref.shape[1] - LANES :] = ids.astype(jnp.bfloat16)


def norm_kernel(x_hbm, gain_hbm, out_ref, x_ref, gain_ref, sems, stage):
    copies = [
        pltpu.make_async_copy(x_hbm, x_ref, sems.at[0]),
        pltpu.make_async_copy(gain_hbm, gain_ref, sems.at[1]),
    ]
    for copy in copies:
        copy.start()
    for copy in copies:
        copy.wait()
    rows, width = x_ref.shape
    block = width // BLOCKS
    total = jnp.zeros((rows, LANES), jnp.float32)
    for c in range(width // LANES):
        x = x_ref[:, c * LANES : (c + 1) * LANES].astype(jnp.float32)
        total = total + x * x
    factor = lax.rsqrt(jnp.sum(total, axis=-1, keepdims=True) / width + EPS)
    for c in range(width // LANES):
        x = x_ref[:, c * LANES : (c + 1) * LANES].astype(jnp.float32)
        gain = gain_ref[c : c + 1, :].astype(jnp.float32)
        j, lane = c * LANES // block, c * LANES % block
        stage[j * rows : (j + 1) * rows, lane : lane + LANES] = x * factor * gain
    write_chunk(stage, rows, out_ref)


def norm_chunk(hidden, gain):
    rows, width = hidden.shape
    return pl.pallas_call(
        norm_kernel,
        out_shape=jax.ShapeDtypeStruct((8, rows * width // 8), jnp.bfloat16),
        in_specs=[HBM, HBM],
        out_specs=VMEM,
        scratch_shapes=[
            pltpu.VMEM((rows, width), jnp.bfloat16),
            pltpu.VMEM((width // LANES, LANES), jnp.bfloat16),
            pltpu.SemaphoreType.DMA((2,)),
            pltpu.VMEM((BLOCKS * rows, width // BLOCKS), jnp.float32),
        ],
        compiler_params=params(16),
        name="norm_chunk",
    )(hidden, gain.reshape(width // LANES, LANES))


def unpack_kernel(chips, rows, with_ids, *refs):
    chunks = refs[:chips]
    left, stage = refs[chips:]
    block = stage.shape[-1]
    small = chips <= 8
    for pair in range(chips // 2):
        turn = pair % 2
        for place in range(2):
            chunk = chunks[2 * pair + place]

            def widen(g, chunk=chunk, turn=turn, place=place):
                lane = g * block if small else pl.multiple_of(g * block, block)
                at = 8 * g if small else pl.multiple_of(8 * g, 8)
                wide = chunk[:, pl.ds(lane, block)].astype(jnp.float32)
                stage[turn, place, pl.ds(at, 8), :] = wide

            steps(BLOCKS * rows // 8, small, widen)
        for j in range(BLOCKS):
            both = [stage[turn, place, j * rows : j * rows + 8, :] for place in range(2)]
            left[j, 16 * pair : 16 * pair + 16, :] = jnp.concatenate(both, axis=0).astype(
                jnp.bfloat16
            )
        if with_ids:
            at = BLOCKS * rows // 8 * block
            both = [chunks[2 * pair + place][:, at : at + LANES] for place in range(2)]
            both = jnp.concatenate([ids.astype(jnp.float32) for ids in both], axis=0)
            left[BLOCKS, 16 * pair : 16 * pair + 16, :LANES] = both.astype(jnp.bfloat16)


def unpack(chunks, rows, width, with_ids):
    chips = len(chunks)
    block = width // BLOCKS
    return pl.pallas_call(
        functools.partial(unpack_kernel, chips, rows, with_ids),
        out_shape=jax.ShapeDtypeStruct((BLOCKS + with_ids, chips * 8, block), jnp.bfloat16),
        in_specs=[VMEM] * chips,
        out_specs=VMEM,
        scratch_shapes=[pltpu.VMEM((2, 2, BLOCKS * rows + 8, block), jnp.float32)],
        compiler_params=params(32),
        name="unpack",
    )(*chunks)


def hold_kernel(count, *refs):
    weight, held, _, sems = refs[count:]
    block = weight.shape[0] // BLOCKS
    copies = [
        pltpu.make_async_copy(
            weight.at[pl.ds(j * block, block), :], held.at[pl.ds(j * block, block), :], sems.at[j]
        )
        for j in range(BLOCKS)
    ]
    for copy in copies:
        copy.start()
    for copy in copies:
        copy.wait()


def hold(weight, chunk, after, mib, name):
    arrays = (chunk, *after)
    return pl.pallas_call(
        functools.partial(hold_kernel, len(arrays)),
        out_shape=(
            jax.ShapeDtypeStruct(weight.shape, weight.dtype),
            jax.ShapeDtypeStruct(chunk.shape, chunk.dtype),
        ),
        in_specs=[ANY] * len(arrays) + [HBM],
        out_specs=(VMEM, ANY),
        scratch_shapes=[pltpu.SemaphoreType.DMA((BLOCKS,))],
        input_output_aliases={0: 1},
        compiler_params=params(mib),
        cost_estimate=pl.CostEstimate(flops=0, bytes_accessed=4 * weight.size, transcendentals=0),
        name=name,
    )(*arrays, weight)


def multiply(left, held, acc):
    block = left.shape[2]
    acc[...] = jnp.zeros_like(acc)
    for j in range(BLOCKS):
        acc[...] += jnp.dot(
            left[j], held[j * block : (j + 1) * block, :], preferred_element_type=jnp.float32
        )


def own_rows(left, held, name):
    rows, cols = left.shape[1], held.shape[1]
    return pl.pallas_call(
        multiply,
        out_shape=jax.ShapeDtypeStruct((rows, cols), jnp.float32),
        in_specs=[VMEM, VMEM],
        out_specs=VMEM,
        compiler_params=params(40),
        cost_estimate=pl.CostEstimate(
            flops=2 * rows * held.size, bytes_accessed=2 * held.size, transcendentals=0
        ),
        name=name,
    )(left, held)


def cache_copies(cache, kept, sems):
    return [
        pltpu.make_async_copy(cache.at[r], kept.at[r], sems.at[r]) for r in range(cache.shape[0])
    ]


def qkv_own_kernel(left, held, cache, acc, kept, sems):
    copies = cache_copies(cache, kept, sems)
    for copy in copies:
        copy.start()
    multiply(left, held, acc)
    for copy in copies:
        copy.wait()


def qkv_own(left, held, cache):
    rows, cols = left.shape[1], held.shape[1]
    return pl.pallas_call(
        qkv_own_kernel,
        out_shape=(
            jax.ShapeDtypeStruct((rows, cols), jnp.float32),
            jax.ShapeDtypeStruct(cache.shape, cache.dtype),
        ),
        in_specs=[VMEM, VMEM, HBM],
        out_specs=(VMEM, VMEM),
        scratch_shapes=[pltpu.SemaphoreType.DMA((cache.shape[0],))],
        compiler_params=params(32),
        cost_estimate=pl.CostEstimate(
            flops=2 * rows * held.size, bytes_accessed=2 * held.size, transcendentals=0
        ),
        name="qkv_own",
    )(left, held, cache)


def qkv_kernel(devices, rows, me_ref, bias_ref, own_ref, left, held, cache, *refs):
    outer, inner = factors(devices // 2)
    outs, (kept, acc, sems) = refs[:outer], refs[outer:]
    copies = cache_copies(cache, kept, sems)
    for copy in copies:
        copy.start()
    multiply(left, held, acc)
    bias = bias_ref[...].astype(jnp.float32)
    me = me_ref[0]
    for c, product in enumerate((own_ref, acc)):
        for m in range(inner):
            at = lax.rem(place(devices, me, 0, m, c), 2 * inner)
            for k in range(outer):
                slot = m * outer + k
                mine = product[8 * slot : 8 * slot + rows, :]
                outs[k][at] = (mine + bias).astype(jnp.bfloat16)
    for copy in copies:
        copy.wait()


def qkv_project(me, own, left, held, bias, cache, devices, rows):
    outer, inner = factors(devices // 2)
    cols = own.shape[1]
    part = jax.ShapeDtypeStruct((2 * inner, rows, cols), jnp.bfloat16)
    *parts, kept = pl.pallas_call(
        functools.partial(qkv_kernel, devices, rows),
        out_shape=[part] * outer + [jax.ShapeDtypeStruct(cache.shape, cache.dtype)],
        in_specs=[SMEM, VMEM, VMEM, VMEM, VMEM, HBM],
        out_specs=[VMEM] * (outer + 1),
        scratch_shapes=[
            pltpu.VMEM(own.shape, jnp.float32),
            pltpu.SemaphoreType.DMA((cache.shape[0],)),
        ],
        compiler_params=params(28),
        name="qkv_project",
    )(me, bias, own, left, held, cache)
    return parts, kept


def head_of(ordered, h):
    cols = ordered.shape[2]
    pieces = []
    at, end = h * HEAD_SIZE, (h + 1) * HEAD_SIZE
    while at < end:
        d, lane = at // cols, at % cols
        width = min(end - at, cols - lane)
        pieces.append(ordered[d, :, lane : lane + width].astype(jnp.float32))
        at += width
    return pieces[0] if len(pieces) == 1 else jnp.concatenate(pieces, axis=1)


def attend_kernel(devices, rows, me_ref, len_ref, ids_ref, cos_ref, sin_ref, keys, values, *refs):
    parts, (out_ref, ordered, heads, mixed, stage) = refs[:-5], refs[-5:]
    total_heads = QUERY_HEADS + 2 * KVH
    half = HEAD_SIZE // 2
    in_order(devices, me_ref[0], parts, ordered)
    for h in range(total_heads):
        heads[pl.ds(h, rows, stride=total_heads), :] = head_of(ordered, h)
    scale = 1.0 / HEAD_SIZE**0.5

    for r in range(rows):
        base = r * total_heads
        turned = heads[base : base + QUERY_HEADS + KVH, :]
        cosine = cos_ref[r : r + 1, :]
        sine = sin_ref[r : r + 1, :]
        turned = (turned * cosine + pltpu.roll(turned, half, 1) * sine).astype(jnp.bfloat16)
        query = turned[:QUERY_HEADS]
        query_f = query.astype(jnp.float32)
        new_key = turned[QUERY_HEADS:].astype(jnp.float32)
        new_value = heads[base + QUERY_HEADS + KVH : base + total_heads, :]
        scores = []
        own = []
        for k in range(KVH):
            mine = slice(k * GROUPS, (k + 1) * GROUPS)
            key = keys[r, :, k * HEAD_SIZE : (k + 1) * HEAD_SIZE]
            scores.append(
                lax.dot_general(
                    query[mine], key, (((1,), (1,)), ((), ())), preferred_element_type=jnp.float32
                )
            )
            own.append(jnp.sum(query_f[mine] * new_key[k : k + 1], axis=-1, keepdims=True))
        score = jnp.concatenate(scores, axis=0) * scale
        own = jnp.concatenate(own, axis=0) * scale
        valid = lax.broadcasted_iota(jnp.int32, score.shape, 1) < len_ref[r]
        top = jnp.maximum(jnp.max(jnp.where(valid, score, -1e30), axis=-1, keepdims=True), own)
        expo = jnp.where(valid, jnp.exp(score - top), 0.0)
        expo_own = jnp.exp(own - top)
        total = jnp.sum(expo, axis=-1, keepdims=True) + expo_own
        weight = (expo / total).astype(jnp.bfloat16)
        weight_own = (expo_own / total).astype(jnp.bfloat16).astype(jnp.float32)
        for k in range(KVH):
            mine = slice(k * GROUPS, (k + 1) * GROUPS)
            value = values[r, :, k * HEAD_SIZE : (k + 1) * HEAD_SIZE]
            part = jnp.dot(weight[mine], value, preferred_element_type=jnp.float32)
            part = part + weight_own[mine] * new_value[k : k + 1]
            at = r * QUERY_HEADS + k * GROUPS
            mixed[at : at + GROUPS, :] = part
    per_block = QUERY_HEADS // BLOCKS
    for h in range(QUERY_HEADS):
        j, lane = h // per_block, h % per_block
        stage[j * rows : (j + 1) * rows, lane * HEAD_SIZE : (lane + 1) * HEAD_SIZE] = mixed[
            pl.ds(h, rows, stride=QUERY_HEADS), :
        ]
    write_chunk(stage, rows, out_ref)
    write_ids(ids_ref, rows, out_ref)


def attend(me, lengths, ids, parts, cosine, sine, keys, values, devices):
    rows, capacity, width = keys.shape
    total_heads = QUERY_HEADS + 2 * KVH
    features = QUERY_HEADS * HEAD_SIZE
    return pl.pallas_call(
        functools.partial(attend_kernel, devices, rows),
        out_shape=jax.ShapeDtypeStruct((8, rows * features // 8 + LANES), jnp.bfloat16),
        in_specs=[SMEM] * 3 + [VMEM] * (4 + len(parts)),
        out_specs=VMEM,
        scratch_shapes=[
            pltpu.VMEM((devices, rows, parts[0].shape[2]), jnp.bfloat16),
            pltpu.VMEM((rows * total_heads, HEAD_SIZE), jnp.float32),
            pltpu.VMEM((rows * QUERY_HEADS, HEAD_SIZE), jnp.float32),
            pltpu.VMEM((BLOCKS * rows, features // BLOCKS), jnp.float32),
        ],
        compiler_params=params(24),
        name="attend",
    )(me, lengths, ids, cosine, sine, keys, values, *parts)


def times_down(down_ref, left, write):
    stored, rank, features = down_ref.shape
    block = features // BLOCKS
    for s in range(stored):
        part = jnp.zeros((rank, left.shape[1]), jnp.float32)
        for j in range(BLOCKS):
            part += lax.dot_general(
                down_ref[s, :, j * block : (j + 1) * block],
                left[j],
                (((1,), (1,)), ((), ())),
                preferred_element_type=jnp.float32,
            )
        write(slice(s * rank, (s + 1) * rank), part)


def shrink_own_kernel(down_ref, left, out_ref):
    def write(at, part):
        out_ref[at, :] = part

    times_down(down_ref, left, write)


def shrink_own(left, down):
    stored, rank, features = down.shape
    return pl.pallas_call(
        shrink_own_kernel,
        out_shape=jax.ShapeDtypeStruct((stored * rank, left.shape[1]), jnp.float32),
        in_specs=[VMEM, VMEM],
        out_specs=VMEM,
        compiler_params=params(48),
        cost_estimate=pl.CostEstimate(
            flops=2 * left.size * stored * rank, bytes_accessed=2 * left.size, transcendentals=0
        ),
        name="shrink_own",
    )(down, left)


def shrink_kernel(
    devices, me_ref, down_ref, own_part, own, other, coords_ref, ids, place_of, total
):
    me = me_ref[0]
    stored, rank, _ = down_ref.shape
    rows = own.shape[1]
    total[:, :rows] = own_part[...]

    def write(at, part):
        total[at, rows:] = part

    times_down(down_ref, other, write)
    for c, left in enumerate((own, other)):
        ids[c * rows : (c + 1) * rows, :] = left[BLOCKS, :, :LANES].astype(jnp.float32)
    row_ids = jnp.transpose(ids[...])[: stored * rank, :].astype(jnp.int32)
    adapter = lax.broadcasted_iota(jnp.int32, total.shape, 0) // rank + me * stored
    coords = jnp.where(row_ids == adapter, total[...], 0.0).astype(jnp.bfloat16)
    core = lax.rem(me, 2)
    sub = lax.broadcasted_iota(jnp.int32, (8, LANES), 0)
    for slot, chip in enumerate(slot_chips(devices, me)):
        for c, place in ((0, core), (1, 1 - core)):
            at = c * rows + 8 * slot
            place_of[at : at + 8, :] = sub + (2 * chip + place) * 8
    target = lax.broadcasted_iota(jnp.int32, (2 * rows, 2 * rows), 1)
    move = jnp.where(place_of[:, :1] == target, 1.0, 0.0).astype(jnp.bfloat16)
    coords = jnp.dot(coords, move, preferred_element_type=jnp.float32).astype(jnp.bfloat16)
    coords_ref[...] = coords


def shrink(me, own_part, own, other, down, devices):
    stored, rank, features = down.shape
    rows = devices * 8
    return pl.pallas_call(
        functools.partial(shrink_kernel, devices),
        out_shape=jax.ShapeDtypeStruct((stored * rank, rows), jnp.bfloat16),
        in_specs=[SMEM, VMEM, VMEM, VMEM, VMEM],
        out_specs=VMEM,
        scratch_shapes=[
            pltpu.VMEM((rows, LANES), jnp.float32),
            pltpu.VMEM((rows, LANES), jnp.int32),
            pltpu.VMEM((stored * rank, rows), jnp.float32),
        ],
        compiler_params=params(48),
        name="shrink",
    )(me, down, own_part, own, other)


def base_kernel(devices, me_ref, own_ref, left, held, out_ref, acc):
    multiply(left, held, acc)
    core = lax.rem(me_ref[0], 2)
    for slot, chip in enumerate(slot_chips(devices, me_ref[0])):
        mine = slice(8 * slot, 8 * slot + 8)
        at = pl.multiple_of((2 * chip + core) * 8, 8)
        out_ref[pl.ds(at, 8), :] = own_ref[mine, :]
        at = pl.multiple_of((2 * chip + 1 - core) * 8, 8)
        out_ref[pl.ds(at, 8), :] = acc[mine, :]


def base_project(me, own, left, held, devices):
    rows, cols = own.shape
    return pl.pallas_call(
        functools.partial(base_kernel, devices),
        out_shape=jax.ShapeDtypeStruct((2 * rows, cols), jnp.float32),
        in_specs=[SMEM, VMEM, VMEM, VMEM],
        out_specs=VMEM,
        scratch_shapes=[pltpu.VMEM(own.shape, jnp.float32)],
        compiler_params=params(40),
        cost_estimate=pl.CostEstimate(
            flops=2 * rows * held.size, bytes_accessed=2 * held.size, transcendentals=0
        ),
        name="base_project",
    )(me, own, left, held)


def add_kernel(devices, rows, me_ref, base_ref, up_ref, *refs):
    outer, inner = factors(devices // 2)
    lines, outs, (coords, projected) = refs[:outer], refs[outer : 2 * outer], refs[2 * outer :]
    part = coords.shape[1]
    me = me_ref[0]
    for k, line in enumerate(lines):
        for at, (m, c) in enumerate(neighbours(devices)):
            coords[place(devices, me, k, m, c)] = line[at * part : (at + 1) * part, :]
    delta = lax.dot_general(
        coords[...].reshape(devices * part, coords.shape[2]),
        up_ref[...],
        (((0,), (0,)), ((), ())),
        preferred_element_type=jnp.float32,
    )
    projected[...] = base_ref[...] + delta
    for k, out_ref in enumerate(outs):
        for m, c in neighbours(devices):
            d = place(devices, me, k, m, c)
            row = projected[pl.ds(pl.multiple_of(8 * d, 8), 8), :]
            out_ref[lax.rem(d, 2 * inner)] = row[:rows].astype(jnp.bfloat16)


def add_delta(me, base, lines, up, devices, rows):
    outer, inner = factors(devices // 2)
    part = up.shape[0] // devices
    out = jax.ShapeDtypeStruct((2 * inner, rows, base.shape[1]), jnp.bfloat16)
    return pl.pallas_call(
        functools.partial(add_kernel, devices, rows),
        out_shape=[out] * outer,
        in_specs=[SMEM, VMEM, VMEM] + [VMEM] * outer,
        out_specs=[VMEM] * outer,
        scratch_shapes=[
            pltpu.VMEM((devices, part, lines[0].shape[1]), jnp.bfloat16),
            pltpu.VMEM(base.shape, jnp.float32),
        ],
        compiler_params=params(48),
        name="add_delta",
    )(me, base, up, *lines)


def per_device(
    devices,
    hidden,
    input_norm_scale,
    query_key_value_weight,
    projection_bias,
    rotated_key_cache,
    past_value_cache,
    lengths,
    row_adapter_index,
    output_weight,
    adapter_down_weight,
    adapter_up_weight,
):
    rows = hidden.shape[0]
    me = lax.axis_index("tensor").astype(jnp.int32).reshape(1)
    half = HEAD_SIZE // 2
    inv = ROPE_BASE ** (-(jnp.arange(half, dtype=jnp.float32) * 2.0 / HEAD_SIZE))
    angle = lengths.astype(jnp.float32)[:, None] * inv[None, :]
    cosine, sine = jnp.cos(angle), jnp.sin(angle)
    cosine = jnp.concatenate([cosine, cosine], axis=1)
    sine = jnp.concatenate([-sine, sine], axis=1)
    down = jnp.transpose(adapter_down_weight, (0, 2, 1))
    up = adapter_up_weight.reshape(-1, adapter_up_weight.shape[2])

    bias = projection_bias.reshape(1, -1)
    chunks, held = gather_chunks(
        norm_chunk(hidden, input_norm_scale),
        devices,
        lambda chunk: hold(query_key_value_weight, chunk, (me,), 40, "hold_qkv"),
    )
    mine = unpack(chunks, rows, hidden.shape[1], False)
    theirs = across(mine, devices)
    own, keys = qkv_own(mine, held, rotated_key_cache)
    parts, values = qkv_project(me, own, theirs, held, bias, past_value_cache, devices, rows)
    parts = exchange(parts, me, devices)
    chunk = attend(
        me, lengths, row_adapter_index, parts, cosine, sine, keys, values, devices
    )
    chunks, held = gather_chunks(
        chunk, devices, lambda chunk: hold(output_weight, chunk, (), 42, "hold_output")
    )
    mine = unpack(chunks, rows, QUERY_HEADS * HEAD_SIZE, True)
    theirs = across(mine, devices)
    own_part = shrink_own(mine, down)
    own = own_rows(mine, held, "base_own")
    lines = gather_coords(shrink(me, own_part, mine, theirs, down, devices), devices)
    base = base_project(me, own, theirs, held, devices)
    parts = exchange(add_delta(me, base, lines, up, devices, rows), me, devices)
    return collect(me, parts, devices)


def solution(mesh):
    in_specs = (
        P(("group", "tensor"), None),
        P(),
        P(None, "tensor"),
        P("tensor"),
        P(("group", "tensor"), None, None),
        P(("group", "tensor"), None, None),
        P(("group", "tensor")),
        P(("group", "tensor")),
        P(None, "tensor"),
        P("tensor", None, None),
        P(None, None, "tensor"),
    )
    out_specs = P(("group", "tensor"), None)
    return jax.shard_map(
        functools.partial(per_device, mesh.shape["tensor"]),
        mesh=mesh,
        in_specs=in_specs,
        out_specs=out_specs,
        check_vma=False,
    )
```

```python
import functools

import jax
import jax.numpy as jnp
from jax import lax
from jax.experimental import pallas as pl
from jax.experimental.pallas import tpu as pltpu
from jax.sharding import PartitionSpec as P

QUERY_HEADS = 64
KVH = 8
HEAD_SIZE = 128
ADAPTER_RANK = 16
GROUPS = QUERY_HEADS // KVH

EPS = 1e-06
ROPE_BASE = 1000000.0

BLOCKS = 8
LANES = 128
MIB = 1 << 20

VMEM = pl.BlockSpec(memory_space=pltpu.VMEM)
HBM = pl.BlockSpec(memory_space=pltpu.HBM)
ANY = pl.BlockSpec(memory_space=pl.ANY)
SMEM = pl.BlockSpec(memory_space=pltpu.SMEM)


def params(mib):
    return pltpu.CompilerParams(vmem_limit_bytes=mib * MIB)


def factors(chips):
    inner = 1
    while inner * inner * 4 <= chips and chips % (inner * 2) == 0:
        inner *= 2
    return chips // inner, inner


def slot_chips(devices, me):
    outer, inner = factors(devices // 2)
    return [lax.div(place(devices, me, k, m, 0), 2) for m in range(inner) for k in range(outer)]


def steps(count, unrolled, body):
    if unrolled:
        for i in range(count):
            body(i)
    else:
        lax.fori_loop(0, count, lambda i, _: (body(i), 0)[1], 0)


def gather_chunks(chunk, devices, meanwhile):
    outer, inner = factors(devices // 2)

    line = [chunk] + [move(chunk, devices, k, 0, 0) for k in range(1, outer)]
    held, line[outer // 4] = meanwhile(line[outer // 4])
    slots = {}
    for k in range(outer):
        for m in range(1, inner):
            slots[k, m] = move(line[k], devices, 0, m, 0)
    for k in range(outer):
        slots[k, 0] = line[k]
    return [slots[k, m] for m in range(inner) for k in range(outer)], held


def neighbours(devices):
    return [(m, c) for m in range(factors(devices // 2)[1]) for c in range(2)]


def place(devices, d, k, m, c):
    outer, inner = factors(devices // 2)
    return 2 * ((d // 2 // inner ^ k) * inner + (d // 2 % inner ^ m)) + (d % 2 ^ c)


def move(x, devices, k, m, c):
    return lax.ppermute(
        x, "tensor", [(d, place(devices, d, k, m, c)) for d in range(devices)]
    )


def join_kernel(*refs):
    parts, out_ref = refs[:-1], refs[-1]
    rows = parts[0].shape[0]
    for at, part in enumerate(parts):
        out_ref[at * rows : (at + 1) * rows, :] = part[...]


def gather_coords(coords, devices):
    around = [coords if mc == (0, 0) else move(coords, devices, 0, *mc) for mc in neighbours(devices)]
    rows, cols = coords.shape
    joined = pl.pallas_call(
        join_kernel,
        out_shape=jax.ShapeDtypeStruct((len(around) * rows, cols), coords.dtype),
        in_specs=[VMEM] * len(around),
        out_specs=VMEM,
        compiler_params=params(16),
        name="join_coords",
    )(*around)
    outer = factors(devices // 2)[0]
    return [joined] + [move(joined, devices, k, 0, 0) for k in range(1, outer)]


def turn_kernel(rows, *refs):
    wide, stage = refs[-2:]
    outer = wide.shape[0]
    parts, outs = refs[:outer], refs[outer:-2]
    for k, part in enumerate(parts):
        wide[k] = part[...].astype(jnp.float32)
    for at, out_ref in enumerate(outs):
        for k in range(outer):
            stage[k * rows : (k + 1) * rows, :] = wide[k, at * rows : (at + 1) * rows, :]
        out_ref[...] = stage[...].astype(jnp.bfloat16)


def exchange(parts, rows, devices):
    outer, _ = factors(devices // 2)
    around = neighbours(devices)
    cols = parts[0].shape[1]
    arrived = [parts[0]] + [move(parts[k], devices, k, 0, 0) for k in range(1, outer)]
    turned = pl.pallas_call(
        functools.partial(turn_kernel, rows),
        out_shape=[jax.ShapeDtypeStruct((outer * rows, cols), parts[0].dtype) for _ in around],
        in_specs=[VMEM] * outer,
        out_specs=[VMEM] * len(around),
        scratch_shapes=[
            pltpu.VMEM((outer, *parts[0].shape), jnp.float32),
            pltpu.VMEM((outer * rows, cols), jnp.float32),
        ],
        compiler_params=params(16),
        name="turn",
    )(*arrived)
    return [x if mc == (0, 0) else move(x, devices, 0, *mc) for x, mc in zip(turned, around)]


def across(x, devices):
    return move(x, devices, 0, 0, 1)


def write_chunk(stage, rows, out_ref):
    block = stage.shape[1]
    for g in range(BLOCKS * rows // 8):
        out_ref[:, g * block : (g + 1) * block] = stage[8 * g : 8 * g + 8, :].astype(jnp.bfloat16)


def write_ids(ids_ref, rows, out_ref):
    sub = lax.broadcasted_iota(jnp.int32, (8, LANES), 0)
    ids = jnp.full((8, LANES), -1.0, jnp.float32)
    for r in range(rows):
        ids = jnp.where(sub == r, ids_ref[r].astype(jnp.float32), ids)
    out_ref[:, out_ref.shape[1] - LANES :] = ids.astype(jnp.bfloat16)


def norm_kernel(x_hbm, gain_hbm, out_ref, x_ref, gain_ref, sems, stage):
    copies = [
        pltpu.make_async_copy(x_hbm, x_ref, sems.at[0]),
        pltpu.make_async_copy(gain_hbm, gain_ref, sems.at[1]),
    ]
    for copy in copies:
        copy.start()
    for copy in copies:
        copy.wait()
    rows, width = x_ref.shape
    block = width // BLOCKS
    total = jnp.zeros((rows, LANES), jnp.float32)
    for c in range(width // LANES):
        x = x_ref[:, c * LANES : (c + 1) * LANES].astype(jnp.float32)
        total = total + x * x
    factor = lax.rsqrt(jnp.sum(total, axis=-1, keepdims=True) / width + EPS)
    for c in range(width // LANES):
        x = x_ref[:, c * LANES : (c + 1) * LANES].astype(jnp.float32)
        gain = gain_ref[c : c + 1, :].astype(jnp.float32)
        j, lane = c * LANES // block, c * LANES % block
        stage[j * rows : (j + 1) * rows, lane : lane + LANES] = x * factor * gain
    write_chunk(stage, rows, out_ref)


def norm_chunk(hidden, gain):
    rows, width = hidden.shape
    return pl.pallas_call(
        norm_kernel,
        out_shape=jax.ShapeDtypeStruct((8, rows * width // 8), jnp.bfloat16),
        in_specs=[HBM, HBM],
        out_specs=VMEM,
        scratch_shapes=[
            pltpu.VMEM((rows, width), jnp.bfloat16),
            pltpu.VMEM((width // LANES, LANES), jnp.bfloat16),
            pltpu.SemaphoreType.DMA((2,)),
            pltpu.VMEM((BLOCKS * rows, width // BLOCKS), jnp.float32),
        ],
        compiler_params=params(16),
        name="norm_chunk",
    )(hidden, gain.reshape(width // LANES, LANES))


def unpack_kernel(chips, rows, with_ids, *refs):
    chunks = refs[:chips]
    left, stage = refs[chips:]
    block = stage.shape[-1]
    small = chips <= 8
    for pair in range(chips // 2):
        turn = pair % 2
        for place in range(2):
            chunk = chunks[2 * pair + place]

            def widen(g, chunk=chunk, turn=turn, place=place):
                lane = g * block if small else pl.multiple_of(g * block, block)
                at = 8 * g if small else pl.multiple_of(8 * g, 8)
                wide = chunk[:, pl.ds(lane, block)].astype(jnp.float32)
                stage[turn, place, pl.ds(at, 8), :] = wide

            steps(BLOCKS * rows // 8, small, widen)
        for j in range(BLOCKS):
            both = [stage[turn, place, j * rows : j * rows + 8, :] for place in range(2)]
            left[j, 16 * pair : 16 * pair + 16, :] = jnp.concatenate(both, axis=0).astype(
                jnp.bfloat16
            )
        if with_ids:
            at = BLOCKS * rows // 8 * block
            both = [chunks[2 * pair + place][:, at : at + LANES] for place in range(2)]
            both = jnp.concatenate([ids.astype(jnp.float32) for ids in both], axis=0)
            left[BLOCKS, 16 * pair : 16 * pair + 16, :LANES] = both.astype(jnp.bfloat16)


def unpack(chunks, rows, width, with_ids):
    chips = len(chunks)
    block = width // BLOCKS
    return pl.pallas_call(
        functools.partial(unpack_kernel, chips, rows, with_ids),
        out_shape=jax.ShapeDtypeStruct((BLOCKS + with_ids, chips * 8, block), jnp.bfloat16),
        in_specs=[VMEM] * chips,
        out_specs=VMEM,
        scratch_shapes=[pltpu.VMEM((2, 2, BLOCKS * rows + 8, block), jnp.float32)],
        compiler_params=params(32),
        name="unpack",
    )(*chunks)


def hold_kernel(count, *refs):
    weight, held, _, sems = refs[count:]
    block = weight.shape[0] // BLOCKS
    copies = [
        pltpu.make_async_copy(
            weight.at[pl.ds(j * block, block), :], held.at[pl.ds(j * block, block), :], sems.at[j]
        )
        for j in range(BLOCKS)
    ]
    for copy in copies:
        copy.start()
    for copy in copies:
        copy.wait()


def hold(weight, chunk, after, mib, name):
    arrays = (chunk, *after)
    return pl.pallas_call(
        functools.partial(hold_kernel, len(arrays)),
        out_shape=(
            jax.ShapeDtypeStruct(weight.shape, weight.dtype),
            jax.ShapeDtypeStruct(chunk.shape, chunk.dtype),
        ),
        in_specs=[ANY] * len(arrays) + [HBM],
        out_specs=(VMEM, ANY),
        scratch_shapes=[pltpu.SemaphoreType.DMA((BLOCKS,))],
        input_output_aliases={0: 1},
        compiler_params=params(mib),
        cost_estimate=pl.CostEstimate(flops=0, bytes_accessed=4 * weight.size, transcendentals=0),
        name=name,
    )(*arrays, weight)


def multiply(left, held, acc):
    block = left.shape[2]
    acc[...] = jnp.zeros_like(acc)
    for j in range(BLOCKS):
        acc[...] += jnp.dot(
            left[j], held[j * block : (j + 1) * block, :], preferred_element_type=jnp.float32
        )


def own_rows(left, held, name):
    rows, cols = left.shape[1], held.shape[1]
    return pl.pallas_call(
        multiply,
        out_shape=jax.ShapeDtypeStruct((rows, cols), jnp.float32),
        in_specs=[VMEM, VMEM],
        out_specs=VMEM,
        compiler_params=params(40),
        cost_estimate=pl.CostEstimate(
            flops=2 * rows * held.size, bytes_accessed=2 * held.size, transcendentals=0
        ),
        name=name,
    )(left, held)


def cache_copies(cache, kept, sems):
    return [
        pltpu.make_async_copy(cache.at[r], kept.at[r], sems.at[r]) for r in range(cache.shape[0])
    ]


def qkv_own_kernel(left, held, cache, acc, kept, sems):
    copies = cache_copies(cache, kept, sems)
    for copy in copies:
        copy.start()
    multiply(left, held, acc)
    for copy in copies:
        copy.wait()


def qkv_own(left, held, cache):
    rows, cols = left.shape[1], held.shape[1]
    return pl.pallas_call(
        qkv_own_kernel,
        out_shape=(
            jax.ShapeDtypeStruct((rows, cols), jnp.float32),
            jax.ShapeDtypeStruct(cache.shape, cache.dtype),
        ),
        in_specs=[VMEM, VMEM, HBM],
        out_specs=(VMEM, VMEM),
        scratch_shapes=[pltpu.SemaphoreType.DMA((cache.shape[0],))],
        compiler_params=params(32),
        cost_estimate=pl.CostEstimate(
            flops=2 * rows * held.size, bytes_accessed=2 * held.size, transcendentals=0
        ),
        name="qkv_own",
    )(left, held, cache)


def qkv_kernel(devices, rows, bias_ref, own_ref, left, held, cache, *refs):
    outer, inner = factors(devices // 2)
    outs, (kept, acc, stage, sems) = refs[:outer], refs[outer:]
    copies = cache_copies(cache, kept, sems)
    for copy in copies:
        copy.start()
    multiply(left, held, acc)
    bias = bias_ref[...].astype(jnp.float32)
    products = own_ref, acc
    for k in range(outer):
        for at, (m, c) in enumerate(neighbours(devices)):
            slot = m * outer + k
            mine = products[c][8 * slot : 8 * slot + rows, :]
            stage[at * rows : (at + 1) * rows, :] = mine + bias
        outs[k][...] = stage[...].astype(jnp.bfloat16)
    for copy in copies:
        copy.wait()


def qkv_project(own, left, held, bias, cache, devices, rows):
    outer, inner = factors(devices // 2)
    cols = own.shape[1]
    part = jax.ShapeDtypeStruct((2 * inner * rows, cols), jnp.bfloat16)
    *parts, kept = pl.pallas_call(
        functools.partial(qkv_kernel, devices, rows),
        out_shape=[part] * outer + [jax.ShapeDtypeStruct(cache.shape, cache.dtype)],
        in_specs=[VMEM, VMEM, VMEM, VMEM, HBM],
        out_specs=[VMEM] * (outer + 1),
        scratch_shapes=[
            pltpu.VMEM(own.shape, jnp.float32),
            pltpu.VMEM((2 * inner * rows, cols), jnp.float32),
            pltpu.SemaphoreType.DMA((cache.shape[0],)),
        ],
        compiler_params=params(28),
        name="qkv_project",
    )(bias, own, left, held, cache)
    return parts, kept


def head_of(ordered, h):
    cols = ordered.shape[2]
    pieces = []
    at, end = h * HEAD_SIZE, (h + 1) * HEAD_SIZE
    while at < end:
        d, lane = at // cols, at % cols
        width = min(end - at, cols - lane)
        pieces.append(ordered[d, :, lane : lane + width])
        at += width
    return pieces[0] if len(pieces) == 1 else jnp.concatenate(pieces, axis=1)


def in_order(devices, me, parts, wide, ordered):
    rows = ordered.shape[1]
    for at, (m, c) in enumerate(neighbours(devices)):
        wide[at] = parts[at][...].astype(jnp.float32)
        for k in range(wide.shape[1] // rows):
            ordered[place(devices, me, k, m, c)] = wide[at, k * rows : (k + 1) * rows, :]


def attend_kernel(devices, rows, me_ref, len_ref, ids_ref, cos_ref, sin_ref, keys, values, *refs):
    parts, (out_ref, wide, ordered, heads, mixed, stage) = refs[:-6], refs[-6:]
    total_heads = QUERY_HEADS + 2 * KVH
    half = HEAD_SIZE // 2
    in_order(devices, me_ref[0], parts, wide, ordered)
    for h in range(total_heads):
        heads[pl.ds(h, rows, stride=total_heads), :] = head_of(ordered, h)
    scale = 1.0 / HEAD_SIZE**0.5
    upper = lax.broadcasted_iota(jnp.int32, (2 * GROUPS, HEAD_SIZE), 0) < GROUPS
    for r in range(rows):
        base = r * total_heads
        turned = heads[base : base + QUERY_HEADS + KVH, :]
        cosine = cos_ref[r : r + 1, :]
        sine = sin_ref[r : r + 1, :]
        turned = (turned * cosine + pltpu.roll(turned, half, 1) * sine).astype(jnp.bfloat16)
        query = turned[:QUERY_HEADS]
        query_f = query.astype(jnp.float32)
        new_key = turned[QUERY_HEADS:].astype(jnp.float32)
        new_value = heads[base + QUERY_HEADS + KVH : base + total_heads, :]
        scores = []
        own = []
        for k in range(0, KVH, 2):
            mine = slice(k * GROUPS, (k + 2) * GROUPS)
            both = query_f[mine]
            wide_query = jnp.concatenate(
                [jnp.where(upper, both, 0.0), jnp.where(upper, 0.0, both)], axis=1
            ).astype(jnp.bfloat16)
            scores.append(
                lax.dot_general(
                    wide_query,
                    keys[r, :, k * HEAD_SIZE : (k + 2) * HEAD_SIZE],
                    (((1,), (1,)), ((), ())),
                    preferred_element_type=jnp.float32,
                )
            )
        for k in range(KVH):
            mine = slice(k * GROUPS, (k + 1) * GROUPS)
            own.append(jnp.sum(query_f[mine] * new_key[k : k + 1], axis=-1, keepdims=True))
        score = jnp.concatenate(scores, axis=0) * scale
        own = jnp.concatenate(own, axis=0) * scale
        valid = lax.broadcasted_iota(jnp.int32, score.shape, 1) < len_ref[r]
        top = jnp.maximum(jnp.max(jnp.where(valid, score, -1e30), axis=-1, keepdims=True), own)
        expo = jnp.where(valid, jnp.exp(score - top), 0.0)
        expo_own = jnp.exp(own - top)
        total = jnp.sum(expo, axis=-1, keepdims=True) + expo_own
        weight = (expo / total).astype(jnp.bfloat16)
        weight_own = (expo_own / total).astype(jnp.bfloat16).astype(jnp.float32)
        for k in range(0, KVH, 2):
            both = jnp.dot(
                weight[k * GROUPS : (k + 2) * GROUPS],
                values[r, :, k * HEAD_SIZE : (k + 2) * HEAD_SIZE],
                preferred_element_type=jnp.float32,
            )
            for i in range(2):
                mine = slice((k + i) * GROUPS, (k + i + 1) * GROUPS)
                part = both[i * GROUPS : (i + 1) * GROUPS, i * HEAD_SIZE : (i + 1) * HEAD_SIZE]
                part = part + weight_own[mine] * new_value[k + i : k + i + 1]
                at = r * QUERY_HEADS + (k + i) * GROUPS
                mixed[at : at + GROUPS, :] = part
    per_block = QUERY_HEADS // BLOCKS
    for h in range(QUERY_HEADS):
        j, lane = h // per_block, h % per_block
        stage[j * rows : (j + 1) * rows, lane * HEAD_SIZE : (lane + 1) * HEAD_SIZE] = mixed[
            pl.ds(h, rows, stride=QUERY_HEADS), :
        ]
    write_chunk(stage, rows, out_ref)
    write_ids(ids_ref, rows, out_ref)


def attend(me, lengths, ids, parts, cosine, sine, keys, values, devices):
    rows, capacity, width = keys.shape
    total_heads = QUERY_HEADS + 2 * KVH
    features = QUERY_HEADS * HEAD_SIZE
    return pl.pallas_call(
        functools.partial(attend_kernel, devices, rows),
        out_shape=jax.ShapeDtypeStruct((8, rows * features // 8 + LANES), jnp.bfloat16),
        in_specs=[SMEM] * 3 + [VMEM] * (4 + len(parts)),
        out_specs=VMEM,
        scratch_shapes=[
            pltpu.VMEM((len(parts), *parts[0].shape), jnp.float32),
            pltpu.VMEM((devices, rows, parts[0].shape[1]), jnp.float32),
            pltpu.VMEM((rows * total_heads, HEAD_SIZE), jnp.float32),
            pltpu.VMEM((rows * QUERY_HEADS, HEAD_SIZE), jnp.float32),
            pltpu.VMEM((BLOCKS * rows, features // BLOCKS), jnp.float32),
        ],
        compiler_params=params(24),
        name="attend",
    )(me, lengths, ids, cosine, sine, keys, values, *parts)


def times_down(down_ref, left, write):
    stored, rank, features = down_ref.shape
    block = features // BLOCKS
    for s in range(stored):
        part = jnp.zeros((rank, left.shape[1]), jnp.float32)
        for j in range(BLOCKS):
            part += lax.dot_general(
                down_ref[s, :, j * block : (j + 1) * block],
                left[j],
                (((1,), (1,)), ((), ())),
                preferred_element_type=jnp.float32,
            )
        write(slice(s * rank, (s + 1) * rank), part)


def shrink_own_kernel(down_ref, left, out_ref):
    def write(at, part):
        out_ref[at, :] = part

    times_down(down_ref, left, write)


def shrink_own(left, down):
    stored, rank, features = down.shape
    return pl.pallas_call(
        shrink_own_kernel,
        out_shape=jax.ShapeDtypeStruct((stored * rank, left.shape[1]), jnp.float32),
        in_specs=[VMEM, VMEM],
        out_specs=VMEM,
        compiler_params=params(48),
        cost_estimate=pl.CostEstimate(
            flops=2 * left.size * stored * rank, bytes_accessed=2 * left.size, transcendentals=0
        ),
        name="shrink_own",
    )(down, left)


def shrink_kernel(
    devices, me_ref, down_ref, own_part, own, other, after, coords_ref, ids, place_of, total
):
    me = me_ref[0]
    stored, rank, _ = down_ref.shape
    rows = own.shape[1]
    total[:, :rows] = own_part[...]

    def write(at, part):
        total[at, rows:] = part

    times_down(down_ref, other, write)
    for c, left in enumerate((own, other)):
        ids[c * rows : (c + 1) * rows, :] = left[BLOCKS, :, :LANES].astype(jnp.float32)
    row_ids = jnp.transpose(ids[...])[: stored * rank, :].astype(jnp.int32)
    adapter = lax.broadcasted_iota(jnp.int32, total.shape, 0) // rank + me * stored
    coords = jnp.where(row_ids == adapter, total[...], 0.0).astype(jnp.bfloat16)
    core = lax.rem(me, 2)
    sub = lax.broadcasted_iota(jnp.int32, (8, LANES), 0)
    for slot, chip in enumerate(slot_chips(devices, me)):
        for c, place in ((0, core), (1, 1 - core)):
            at = c * rows + 8 * slot
            place_of[at : at + 8, :] = sub + (2 * chip + place) * 8
    target = lax.broadcasted_iota(jnp.int32, (2 * rows, 2 * rows), 1)
    move = jnp.where(place_of[:, :1] == target, 1.0, 0.0).astype(jnp.bfloat16)
    coords = jnp.dot(coords, move, preferred_element_type=jnp.float32).astype(jnp.bfloat16)
    coords_ref[...] = coords


def shrink(me, own_part, own, other, down, after, devices):
    stored, rank, features = down.shape
    rows = devices * 8
    return pl.pallas_call(
        functools.partial(shrink_kernel, devices),
        out_shape=jax.ShapeDtypeStruct((stored * rank, rows), jnp.bfloat16),
        in_specs=[SMEM, VMEM, VMEM, VMEM, VMEM, ANY],
        out_specs=VMEM,
        scratch_shapes=[
            pltpu.VMEM((rows, LANES), jnp.float32),
            pltpu.VMEM((rows, LANES), jnp.int32),
            pltpu.VMEM((stored * rank, rows), jnp.float32),
        ],
        compiler_params=params(48),
        name="shrink",
    )(me, down, own_part, own, other, after)


def base_kernel(devices, me_ref, own_ref, left, held, out_ref, acc):
    multiply(left, held, acc)
    core = lax.rem(me_ref[0], 2)
    for slot, chip in enumerate(slot_chips(devices, me_ref[0])):
        mine = slice(8 * slot, 8 * slot + 8)
        at = pl.multiple_of((2 * chip + core) * 8, 8)
        out_ref[pl.ds(at, 8), :] = own_ref[mine, :]
        at = pl.multiple_of((2 * chip + 1 - core) * 8, 8)
        out_ref[pl.ds(at, 8), :] = acc[mine, :]


def base_project(me, own, left, held, devices):
    rows, cols = own.shape
    return pl.pallas_call(
        functools.partial(base_kernel, devices),
        out_shape=jax.ShapeDtypeStruct((2 * rows, cols), jnp.float32),
        in_specs=[SMEM, VMEM, VMEM, VMEM],
        out_specs=VMEM,
        scratch_shapes=[pltpu.VMEM(own.shape, jnp.float32)],
        compiler_params=params(40),
        cost_estimate=pl.CostEstimate(
            flops=2 * rows * held.size, bytes_accessed=2 * held.size, transcendentals=0
        ),
        name="base_project",
    )(me, own, left, held)


def add_kernel(devices, rows, me_ref, base_ref, up_ref, *refs):
    lines, (out_ref, coords) = refs[:-2], refs[-2:]
    part = coords.shape[1]
    for k, line in enumerate(lines):
        for at, (m, c) in enumerate(neighbours(devices)):
            coords[place(devices, me_ref[0], k, m, c)] = line[at * part : (at + 1) * part, :]
    delta = lax.dot_general(
        coords[...].reshape(devices * part, coords.shape[2]),
        up_ref[...],
        (((0,), (0,)), ((), ())),
        preferred_element_type=jnp.float32,
    )
    projected = base_ref[...] + delta
    for d in range(devices):
        out_ref[d] = projected[8 * d : 8 * d + rows, :].astype(jnp.bfloat16)


def add_delta(me, base, lines, up, devices, rows):
    part = up.shape[0] // devices
    return pl.pallas_call(
        functools.partial(add_kernel, devices, rows),
        out_shape=jax.ShapeDtypeStruct((devices, rows, base.shape[1]), jnp.bfloat16),
        in_specs=[SMEM, VMEM, VMEM] + [VMEM] * len(lines),
        out_specs=VMEM,
        scratch_shapes=[pltpu.VMEM((devices, part, lines[0].shape[1]), jnp.bfloat16)],
        compiler_params=params(48),
        name="add_delta",
    )(me, base, up, *lines)


def per_device(
    devices,
    hidden,
    input_norm_scale,
    query_key_value_weight,
    projection_bias,
    rotated_key_cache,
    past_value_cache,
    lengths,
    row_adapter_index,
    output_weight,
    adapter_down_weight,
    adapter_up_weight,
):
    rows = hidden.shape[0]
    me = lax.axis_index("tensor").astype(jnp.int32).reshape(1)
    half = HEAD_SIZE // 2
    inv = ROPE_BASE ** (-(jnp.arange(half, dtype=jnp.float32) * 2.0 / HEAD_SIZE))
    angle = lengths.astype(jnp.float32)[:, None] * inv[None, :]
    cosine, sine = jnp.cos(angle), jnp.sin(angle)
    cosine = jnp.concatenate([cosine, cosine], axis=1)
    sine = jnp.concatenate([-sine, sine], axis=1)
    down = jnp.transpose(adapter_down_weight, (0, 2, 1))
    up = adapter_up_weight.reshape(-1, adapter_up_weight.shape[2])

    bias = projection_bias.reshape(1, -1)
    chunks, held = gather_chunks(
        norm_chunk(hidden, input_norm_scale),
        devices,
        lambda chunk: hold(query_key_value_weight, chunk, (me,), 40, "hold_qkv"),
    )
    mine = unpack(chunks, rows, hidden.shape[1], False)
    theirs = across(mine, devices)
    own, keys = qkv_own(mine, held, rotated_key_cache)
    parts, values = qkv_project(own, theirs, held, bias, past_value_cache, devices, rows)
    parts = exchange(parts, rows, devices)
    chunk = attend(
        me, lengths, row_adapter_index, parts, cosine, sine, keys, values, devices
    )
    chunks, held = gather_chunks(
        chunk, devices, lambda chunk: hold(output_weight, chunk, (), 42, "hold_output")
    )
    mine = unpack(chunks, rows, QUERY_HEADS * HEAD_SIZE, True)
    theirs = across(mine, devices)
    own_part = shrink_own(mine, down)
    own = own_rows(mine, held, "base_own")
    coords = shrink(me, own_part, mine, theirs, down, own, devices)
    lines = gather_coords(coords, devices)
    base = base_project(me, own, theirs, held, devices)
    projected = add_delta(me, base, lines, up, devices, rows)
    projected = lax.all_to_all(projected, "tensor", split_axis=0, concat_axis=0, tiled=True)
    return jnp.transpose(projected, (1, 0, 2)).reshape(rows, -1)


def solution(mesh):
    in_specs = (
        P(("group", "tensor"), None),
        P(),
        P(None, "tensor"),
        P("tensor"),
        P(("group", "tensor"), None, None),
        P(("group", "tensor"), None, None),
        P(("group", "tensor")),
        P(("group", "tensor")),
        P(None, "tensor"),
        P("tensor", None, None),
        P(None, None, "tensor"),
    )
    out_specs = P(("group", "tensor"), None)
    return jax.shard_map(
        functools.partial(per_device, mesh.shape["tensor"]),
        mesh=mesh,
        in_specs=in_specs,
        out_specs=out_specs,
        check_vma=False,
    )
```

```python
import functools

import jax
import jax.numpy as jnp
from jax import lax
from jax.experimental import pallas as pl
from jax.experimental.pallas import tpu as pltpu
from jax.sharding import PartitionSpec as P

QUERY_HEADS = 64
KVH = 8
HEAD_SIZE = 128
ADAPTER_RANK = 16
GROUPS = QUERY_HEADS // KVH

EPS = 1e-06
ROPE_BASE = 1000000.0

BLOCKS = 8
LANES = 128
MIB = 1 << 20

VMEM = pl.BlockSpec(memory_space=pltpu.VMEM)
HBM = pl.BlockSpec(memory_space=pltpu.HBM)
ANY = pl.BlockSpec(memory_space=pl.ANY)
SMEM = pl.BlockSpec(memory_space=pltpu.SMEM)


def params(mib):
    return pltpu.CompilerParams(vmem_limit_bytes=mib * MIB)


def factors(chips):
    inner = 1
    while inner * inner * 4 <= chips and chips % (inner * 2) == 0:
        inner *= 2
    return chips // inner, inner


def slot_chips(devices, me):
    outer, inner = factors(devices // 2)
    return [lax.div(place(devices, me, k, m, 0), 2) for m in range(inner) for k in range(outer)]


def steps(count, unrolled, body):
    if unrolled:
        for i in range(count):
            body(i)
    else:
        lax.fori_loop(0, count, lambda i, _: (body(i), 0)[1], 0)


def gather_chunks(chunk, devices, meanwhile):
    outer, inner = factors(devices // 2)

    line = [chunk] + [move(chunk, devices, k, 0, 0) for k in range(1, outer)]
    held, line[outer // 4] = meanwhile(line[outer // 4])
    slots = {}
    for k in range(outer):
        for m in range(1, inner):
            slots[k, m] = move(line[k], devices, 0, m, 0)
    for k in range(outer):
        slots[k, 0] = line[k]
    return [slots[k, m] for m in range(inner) for k in range(outer)], held


def neighbours(devices):
    return [(m, c) for m in range(factors(devices // 2)[1]) for c in range(2)]


def place(devices, d, k, m, c):
    outer, inner = factors(devices // 2)
    return 2 * ((d // 2 // inner ^ k) * inner + (d // 2 % inner ^ m)) + (d % 2 ^ c)


def move(x, devices, k, m, c):
    return lax.ppermute(
        x, "tensor", [(d, place(devices, d, k, m, c)) for d in range(devices)]
    )


def join_kernel(*refs):
    parts, out_ref = refs[:-1], refs[-1]
    rows = parts[0].shape[0]
    for at, part in enumerate(parts):
        out_ref[at * rows : (at + 1) * rows, :] = part[...]


def gather_coords(coords, devices):
    around = [coords if mc == (0, 0) else move(coords, devices, 0, *mc) for mc in neighbours(devices)]
    rows, cols = coords.shape
    joined = pl.pallas_call(
        join_kernel,
        out_shape=jax.ShapeDtypeStruct((len(around) * rows, cols), coords.dtype),
        in_specs=[VMEM] * len(around),
        out_specs=VMEM,
        compiler_params=params(16),
        name="join_coords",
    )(*around)
    outer = factors(devices // 2)[0]
    return [joined] + [move(joined, devices, k, 0, 0) for k in range(1, outer)]


def turn_kernel(rows, *refs):
    wide, stage = refs[-2:]
    outer = wide.shape[0]
    parts, outs = refs[:outer], refs[outer:-2]
    for k, part in enumerate(parts):
        wide[k] = part[...].astype(jnp.float32)
    for at, out_ref in enumerate(outs):
        for k in range(outer):
            stage[k * rows : (k + 1) * rows, :] = wide[k, at * rows : (at + 1) * rows, :]
        out_ref[...] = stage[...].astype(jnp.bfloat16)


def exchange(parts, rows, devices):
    outer, _ = factors(devices // 2)
    around = neighbours(devices)
    cols = parts[0].shape[1]
    arrived = [parts[0]] + [move(parts[k], devices, k, 0, 0) for k in range(1, outer)]
    turned = pl.pallas_call(
        functools.partial(turn_kernel, rows),
        out_shape=[jax.ShapeDtypeStruct((outer * rows, cols), parts[0].dtype) for _ in around],
        in_specs=[VMEM] * outer,
        out_specs=[VMEM] * len(around),
        scratch_shapes=[
            pltpu.VMEM((outer, *parts[0].shape), jnp.float32),
            pltpu.VMEM((outer * rows, cols), jnp.float32),
        ],
        compiler_params=params(16),
        name="turn",
    )(*arrived)
    return [x if mc == (0, 0) else move(x, devices, 0, *mc) for x, mc in zip(turned, around)]


def across(x, devices):
    return move(x, devices, 0, 0, 1)


def write_chunk(stage, rows, out_ref):
    block = stage.shape[1]
    for g in range(BLOCKS * rows // 8):
        out_ref[:, g * block : (g + 1) * block] = stage[8 * g : 8 * g + 8, :].astype(jnp.bfloat16)


def write_ids(ids_ref, rows, out_ref):
    sub = lax.broadcasted_iota(jnp.int32, (8, LANES), 0)
    ids = jnp.full((8, LANES), -1.0, jnp.float32)
    for r in range(rows):
        ids = jnp.where(sub == r, ids_ref[r].astype(jnp.float32), ids)
    out_ref[:, out_ref.shape[1] - LANES :] = ids.astype(jnp.bfloat16)


def norm_kernel(x_hbm, gain_hbm, out_ref, x_ref, gain_ref, sems, stage):
    copies = [
        pltpu.make_async_copy(x_hbm, x_ref, sems.at[0]),
        pltpu.make_async_copy(gain_hbm, gain_ref, sems.at[1]),
    ]
    for copy in copies:
        copy.start()
    for copy in copies:
        copy.wait()
    rows, width = x_ref.shape
    block = width // BLOCKS
    total = jnp.zeros((rows, LANES), jnp.float32)
    for c in range(width // LANES):
        x = x_ref[:, c * LANES : (c + 1) * LANES].astype(jnp.float32)
        total = total + x * x
    factor = lax.rsqrt(jnp.sum(total, axis=-1, keepdims=True) / width + EPS)
    for c in range(width // LANES):
        x = x_ref[:, c * LANES : (c + 1) * LANES].astype(jnp.float32)
        gain = gain_ref[c : c + 1, :].astype(jnp.float32)
        j, lane = c * LANES // block, c * LANES % block
        stage[j * rows : (j + 1) * rows, lane : lane + LANES] = x * factor * gain
    write_chunk(stage, rows, out_ref)


def norm_chunk(hidden, gain):
    rows, width = hidden.shape
    return pl.pallas_call(
        norm_kernel,
        out_shape=jax.ShapeDtypeStruct((8, rows * width // 8), jnp.bfloat16),
        in_specs=[HBM, HBM],
        out_specs=VMEM,
        scratch_shapes=[
            pltpu.VMEM((rows, width), jnp.bfloat16),
            pltpu.VMEM((width // LANES, LANES), jnp.bfloat16),
            pltpu.SemaphoreType.DMA((2,)),
            pltpu.VMEM((BLOCKS * rows, width // BLOCKS), jnp.float32),
        ],
        compiler_params=params(16),
        name="norm_chunk",
    )(hidden, gain.reshape(width // LANES, LANES))


def unpack_kernel(chips, rows, with_ids, *refs):
    chunks = refs[:chips]
    left, stage = refs[chips:]
    block = stage.shape[-1]
    small = chips <= 8
    for pair in range(chips // 2):
        turn = pair % 2
        for place in range(2):
            chunk = chunks[2 * pair + place]

            def widen(g, chunk=chunk, turn=turn, place=place):
                lane = g * block if small else pl.multiple_of(g * block, block)
                at = 8 * g if small else pl.multiple_of(8 * g, 8)
                wide = chunk[:, pl.ds(lane, block)].astype(jnp.float32)
                stage[turn, place, pl.ds(at, 8), :] = wide

            steps(BLOCKS * rows // 8, small, widen)
        for j in range(BLOCKS):
            both = [stage[turn, place, j * rows : j * rows + 8, :] for place in range(2)]
            left[j, 16 * pair : 16 * pair + 16, :] = jnp.concatenate(both, axis=0).astype(
                jnp.bfloat16
            )
        if with_ids:
            at = BLOCKS * rows // 8 * block
            both = [chunks[2 * pair + place][:, at : at + LANES] for place in range(2)]
            both = jnp.concatenate([ids.astype(jnp.float32) for ids in both], axis=0)
            left[BLOCKS, 16 * pair : 16 * pair + 16, :LANES] = both.astype(jnp.bfloat16)


def unpack(chunks, rows, width, with_ids):
    chips = len(chunks)
    block = width // BLOCKS
    return pl.pallas_call(
        functools.partial(unpack_kernel, chips, rows, with_ids),
        out_shape=jax.ShapeDtypeStruct((BLOCKS + with_ids, chips * 8, block), jnp.bfloat16),
        in_specs=[VMEM] * chips,
        out_specs=VMEM,
        scratch_shapes=[pltpu.VMEM((2, 2, BLOCKS * rows + 8, block), jnp.float32)],
        compiler_params=params(32),
        name="unpack",
    )(*chunks)


def hold_kernel(count, *refs):
    weight, held, _, sems = refs[count:]
    block = weight.shape[0] // BLOCKS
    copies = [
        pltpu.make_async_copy(
            weight.at[pl.ds(j * block, block), :], held.at[pl.ds(j * block, block), :], sems.at[j]
        )
        for j in range(BLOCKS)
    ]
    for copy in copies:
        copy.start()
    for copy in copies:
        copy.wait()


def hold(weight, chunk, after, mib, name):
    arrays = (chunk, *after)
    return pl.pallas_call(
        functools.partial(hold_kernel, len(arrays)),
        out_shape=(
            jax.ShapeDtypeStruct(weight.shape, weight.dtype),
            jax.ShapeDtypeStruct(chunk.shape, chunk.dtype),
        ),
        in_specs=[ANY] * len(arrays) + [HBM],
        out_specs=(VMEM, ANY),
        scratch_shapes=[pltpu.SemaphoreType.DMA((BLOCKS,))],
        input_output_aliases={0: 1},
        compiler_params=params(mib),
        cost_estimate=pl.CostEstimate(flops=0, bytes_accessed=4 * weight.size, transcendentals=0),
        name=name,
    )(*arrays, weight)


def multiply(left, held, acc):
    block = left.shape[2]
    acc[...] = jnp.zeros_like(acc)
    for j in range(BLOCKS):
        acc[...] += jnp.dot(
            left[j], held[j * block : (j + 1) * block, :], preferred_element_type=jnp.float32
        )


def own_rows(left, held, name):
    rows, cols = left.shape[1], held.shape[1]
    return pl.pallas_call(
        multiply,
        out_shape=jax.ShapeDtypeStruct((rows, cols), jnp.float32),
        in_specs=[VMEM, VMEM],
        out_specs=VMEM,
        compiler_params=params(40),
        cost_estimate=pl.CostEstimate(
            flops=2 * rows * held.size, bytes_accessed=2 * held.size, transcendentals=0
        ),
        name=name,
    )(left, held)


def cache_copies(cache, kept, sems):
    return [
        pltpu.make_async_copy(cache.at[r], kept.at[r], sems.at[r]) for r in range(cache.shape[0])
    ]


def qkv_own_kernel(left, held, cache, acc, kept, sems):
    copies = cache_copies(cache, kept, sems)
    for copy in copies:
        copy.start()
    multiply(left, held, acc)
    for copy in copies:
        copy.wait()


def qkv_own(left, held, cache):
    rows, cols = left.shape[1], held.shape[1]
    return pl.pallas_call(
        qkv_own_kernel,
        out_shape=(
            jax.ShapeDtypeStruct((rows, cols), jnp.float32),
            jax.ShapeDtypeStruct(cache.shape, cache.dtype),
        ),
        in_specs=[VMEM, VMEM, HBM],
        out_specs=(VMEM, VMEM),
        scratch_shapes=[pltpu.SemaphoreType.DMA((cache.shape[0],))],
        compiler_params=params(32),
        cost_estimate=pl.CostEstimate(
            flops=2 * rows * held.size, bytes_accessed=2 * held.size, transcendentals=0
        ),
        name="qkv_own",
    )(left, held, cache)


def qkv_kernel(devices, rows, bias_ref, own_ref, left, held, cache, *refs):
    outer, inner = factors(devices // 2)
    outs, (kept, acc, stage, sems) = refs[:outer], refs[outer:]
    copies = cache_copies(cache, kept, sems)
    for copy in copies:
        copy.start()
    multiply(left, held, acc)
    bias = bias_ref[...].astype(jnp.float32)
    products = own_ref, acc
    for k in range(outer):
        for at, (m, c) in enumerate(neighbours(devices)):
            slot = m * outer + k
            mine = products[c][8 * slot : 8 * slot + rows, :]
            stage[at * rows : (at + 1) * rows, :] = mine + bias
        outs[k][...] = stage[...].astype(jnp.bfloat16)
    for copy in copies:
        copy.wait()


def qkv_project(own, left, held, bias, cache, devices, rows):
    outer, inner = factors(devices // 2)
    cols = own.shape[1]
    part = jax.ShapeDtypeStruct((2 * inner * rows, cols), jnp.bfloat16)
    *parts, kept = pl.pallas_call(
        functools.partial(qkv_kernel, devices, rows),
        out_shape=[part] * outer + [jax.ShapeDtypeStruct(cache.shape, cache.dtype)],
        in_specs=[VMEM, VMEM, VMEM, VMEM, HBM],
        out_specs=[VMEM] * (outer + 1),
        scratch_shapes=[
            pltpu.VMEM(own.shape, jnp.float32),
            pltpu.VMEM((2 * inner * rows, cols), jnp.float32),
            pltpu.SemaphoreType.DMA((cache.shape[0],)),
        ],
        compiler_params=params(24),
        name="qkv_project",
    )(bias, own, left, held, cache)
    return parts, kept


def head_of(ordered, h):
    cols = ordered.shape[2]
    pieces = []
    at, end = h * HEAD_SIZE, (h + 1) * HEAD_SIZE
    while at < end:
        d, lane = at // cols, at % cols
        width = min(end - at, cols - lane)
        pieces.append(ordered[d, :, lane : lane + width])
        at += width
    return pieces[0] if len(pieces) == 1 else jnp.concatenate(pieces, axis=1)


def in_order(devices, me, parts, wide, ordered):
    rows = ordered.shape[1]
    for at, (m, c) in enumerate(neighbours(devices)):
        wide[at] = parts[at][...].astype(jnp.float32)
        for k in range(wide.shape[1] // rows):
            ordered[place(devices, me, k, m, c)] = wide[at, k * rows : (k + 1) * rows, :]


def attend_kernel(devices, rows, me_ref, len_ref, ids_ref, cos_ref, sin_ref, keys, values, *refs):
    parts, (out_ref, wide, ordered, heads, mixed, stage) = refs[:-6], refs[-6:]
    total_heads = QUERY_HEADS + 2 * KVH
    half = HEAD_SIZE // 2
    in_order(devices, me_ref[0], parts, wide, ordered)
    for h in range(total_heads):
        heads[pl.ds(h, rows, stride=total_heads), :] = head_of(ordered, h)
    scale = 1.0 / HEAD_SIZE**0.5
    upper = lax.broadcasted_iota(jnp.int32, (2 * GROUPS, HEAD_SIZE), 0) < GROUPS
    for r in range(rows):
        base = r * total_heads
        turned = heads[base : base + QUERY_HEADS + KVH, :]
        cosine = cos_ref[r : r + 1, :]
        sine = sin_ref[r : r + 1, :]
        turned = (turned * cosine + pltpu.roll(turned, half, 1) * sine).astype(jnp.bfloat16)
        query = turned[:QUERY_HEADS]
        query_f = query.astype(jnp.float32)
        new_key = turned[QUERY_HEADS:].astype(jnp.float32)
        new_value = heads[base + QUERY_HEADS + KVH : base + total_heads, :]
        scores = []
        own = []
        for k in range(0, KVH, 2):
            mine = slice(k * GROUPS, (k + 2) * GROUPS)
            both = query_f[mine]
            wide_query = jnp.concatenate(
                [jnp.where(upper, both, 0.0), jnp.where(upper, 0.0, both)], axis=1
            ).astype(jnp.bfloat16)
            scores.append(
                lax.dot_general(
                    wide_query,
                    keys[r, :, k * HEAD_SIZE : (k + 2) * HEAD_SIZE],
                    (((1,), (1,)), ((), ())),
                    preferred_element_type=jnp.float32,
                )
            )
        for k in range(KVH):
            mine = slice(k * GROUPS, (k + 1) * GROUPS)
            own.append(jnp.sum(query_f[mine] * new_key[k : k + 1], axis=-1, keepdims=True))
        score = jnp.concatenate(scores, axis=0) * scale
        own = jnp.concatenate(own, axis=0) * scale
        valid = lax.broadcasted_iota(jnp.int32, score.shape, 1) < len_ref[r]
        top = jnp.maximum(jnp.max(jnp.where(valid, score, -1e30), axis=-1, keepdims=True), own)
        expo = jnp.where(valid, jnp.exp(score - top), 0.0)
        expo_own = jnp.exp(own - top)
        total = jnp.sum(expo, axis=-1, keepdims=True) + expo_own
        weight = (expo / total).astype(jnp.bfloat16)
        weight_own = (expo_own / total).astype(jnp.bfloat16).astype(jnp.float32)
        for k in range(0, KVH, 2):
            both = jnp.dot(
                weight[k * GROUPS : (k + 2) * GROUPS],
                values[r, :, k * HEAD_SIZE : (k + 2) * HEAD_SIZE],
                preferred_element_type=jnp.float32,
            )
            for i in range(2):
                mine = slice((k + i) * GROUPS, (k + i + 1) * GROUPS)
                part = both[i * GROUPS : (i + 1) * GROUPS, i * HEAD_SIZE : (i + 1) * HEAD_SIZE]
                part = part + weight_own[mine] * new_value[k + i : k + i + 1]
                at = r * QUERY_HEADS + (k + i) * GROUPS
                mixed[at : at + GROUPS, :] = part
    per_block = QUERY_HEADS // BLOCKS
    for h in range(QUERY_HEADS):
        j, lane = h // per_block, h % per_block
        stage[j * rows : (j + 1) * rows, lane * HEAD_SIZE : (lane + 1) * HEAD_SIZE] = mixed[
            pl.ds(h, rows, stride=QUERY_HEADS), :
        ]
    write_chunk(stage, rows, out_ref)
    write_ids(ids_ref, rows, out_ref)


def attend(me, lengths, ids, parts, cosine, sine, keys, values, devices):
    rows, capacity, width = keys.shape
    total_heads = QUERY_HEADS + 2 * KVH
    features = QUERY_HEADS * HEAD_SIZE
    return pl.pallas_call(
        functools.partial(attend_kernel, devices, rows),
        out_shape=jax.ShapeDtypeStruct((8, rows * features // 8 + LANES), jnp.bfloat16),
        in_specs=[SMEM] * 3 + [VMEM] * (4 + len(parts)),
        out_specs=VMEM,
        scratch_shapes=[
            pltpu.VMEM((len(parts), *parts[0].shape), jnp.float32),
            pltpu.VMEM((devices, rows, parts[0].shape[1]), jnp.float32),
            pltpu.VMEM((rows * total_heads, HEAD_SIZE), jnp.float32),
            pltpu.VMEM((rows * QUERY_HEADS, HEAD_SIZE), jnp.float32),
            pltpu.VMEM((BLOCKS * rows, features // BLOCKS), jnp.float32),
        ],
        compiler_params=params(24),
        name="attend",
    )(me, lengths, ids, cosine, sine, keys, values, *parts)


def times_down(down_ref, left, write):
    stored, rank, features = down_ref.shape
    block = features // BLOCKS
    for s in range(stored):
        part = jnp.zeros((rank, left.shape[1]), jnp.float32)
        for j in range(BLOCKS):
            part += lax.dot_general(
                down_ref[s, :, j * block : (j + 1) * block],
                left[j],
                (((1,), (1,)), ((), ())),
                preferred_element_type=jnp.float32,
            )
        write(slice(s * rank, (s + 1) * rank), part)


def shrink_own_kernel(down_ref, left, out_ref):
    def write(at, part):
        out_ref[at, :] = part

    times_down(down_ref, left, write)


def shrink_own(left, down):
    stored, rank, features = down.shape
    return pl.pallas_call(
        shrink_own_kernel,
        out_shape=jax.ShapeDtypeStruct((stored * rank, left.shape[1]), jnp.float32),
        in_specs=[VMEM, VMEM],
        out_specs=VMEM,
        compiler_params=params(48),
        cost_estimate=pl.CostEstimate(
            flops=2 * left.size * stored * rank, bytes_accessed=2 * left.size, transcendentals=0
        ),
        name="shrink_own",
    )(down, left)


def shrink_kernel(
    devices, me_ref, down_ref, own_part, own, other, after, coords_ref, ids, place_of, total
):
    me = me_ref[0]
    stored, rank, _ = down_ref.shape
    rows = own.shape[1]
    total[:, :rows] = own_part[...]

    def write(at, part):
        total[at, rows:] = part

    times_down(down_ref, other, write)
    for c, left in enumerate((own, other)):
        ids[c * rows : (c + 1) * rows, :] = left[BLOCKS, :, :LANES].astype(jnp.float32)
    row_ids = jnp.transpose(ids[...])[: stored * rank, :].astype(jnp.int32)
    adapter = lax.broadcasted_iota(jnp.int32, total.shape, 0) // rank + me * stored
    coords = jnp.where(row_ids == adapter, total[...], 0.0).astype(jnp.bfloat16)
    core = lax.rem(me, 2)
    sub = lax.broadcasted_iota(jnp.int32, (8, LANES), 0)
    for slot, chip in enumerate(slot_chips(devices, me)):
        for c, place in ((0, core), (1, 1 - core)):
            at = c * rows + 8 * slot
            place_of[at : at + 8, :] = sub + (2 * chip + place) * 8
    target = lax.broadcasted_iota(jnp.int32, (2 * rows, 2 * rows), 1)
    move = jnp.where(place_of[:, :1] == target, 1.0, 0.0).astype(jnp.bfloat16)
    coords = jnp.dot(coords, move, preferred_element_type=jnp.float32).astype(jnp.bfloat16)
    coords_ref[...] = coords


def shrink(me, own_part, own, other, down, after, devices):
    stored, rank, features = down.shape
    rows = devices * 8
    return pl.pallas_call(
        functools.partial(shrink_kernel, devices),
        out_shape=jax.ShapeDtypeStruct((stored * rank, rows), jnp.bfloat16),
        in_specs=[SMEM, VMEM, VMEM, VMEM, VMEM, ANY],
        out_specs=VMEM,
        scratch_shapes=[
            pltpu.VMEM((rows, LANES), jnp.float32),
            pltpu.VMEM((rows, LANES), jnp.int32),
            pltpu.VMEM((stored * rank, rows), jnp.float32),
        ],
        compiler_params=params(48),
        name="shrink",
    )(me, down, own_part, own, other, after)


def base_kernel(devices, me_ref, own_ref, left, held, out_ref, acc):
    multiply(left, held, acc)
    core = lax.rem(me_ref[0], 2)
    for slot, chip in enumerate(slot_chips(devices, me_ref[0])):
        mine = slice(8 * slot, 8 * slot + 8)
        at = pl.multiple_of((2 * chip + core) * 8, 8)
        out_ref[pl.ds(at, 8), :] = own_ref[mine, :]
        at = pl.multiple_of((2 * chip + 1 - core) * 8, 8)
        out_ref[pl.ds(at, 8), :] = acc[mine, :]


def base_project(me, own, left, held, devices):
    rows, cols = own.shape
    return pl.pallas_call(
        functools.partial(base_kernel, devices),
        out_shape=jax.ShapeDtypeStruct((2 * rows, cols), jnp.float32),
        in_specs=[SMEM, VMEM, VMEM, VMEM],
        out_specs=VMEM,
        scratch_shapes=[pltpu.VMEM(own.shape, jnp.float32)],
        compiler_params=params(40),
        cost_estimate=pl.CostEstimate(
            flops=2 * rows * held.size, bytes_accessed=2 * held.size, transcendentals=0
        ),
        name="base_project",
    )(me, own, left, held)


def add_kernel(devices, rows, me_ref, base_ref, up_ref, *refs):
    lines, (out_ref, coords) = refs[:-2], refs[-2:]
    part = coords.shape[1]
    for k, line in enumerate(lines):
        for at, (m, c) in enumerate(neighbours(devices)):
            coords[place(devices, me_ref[0], k, m, c)] = line[at * part : (at + 1) * part, :]
    delta = lax.dot_general(
        coords[...].reshape(devices * part, coords.shape[2]),
        up_ref[...],
        (((0,), (0,)), ((), ())),
        preferred_element_type=jnp.float32,
    )
    projected = base_ref[...] + delta
    for d in range(devices):
        out_ref[d] = projected[8 * d : 8 * d + rows, :].astype(jnp.bfloat16)


def add_delta(me, base, lines, up, devices, rows):
    part = up.shape[0] // devices
    return pl.pallas_call(
        functools.partial(add_kernel, devices, rows),
        out_shape=jax.ShapeDtypeStruct((devices, rows, base.shape[1]), jnp.bfloat16),
        in_specs=[SMEM, VMEM, VMEM] + [VMEM] * len(lines),
        out_specs=VMEM,
        scratch_shapes=[pltpu.VMEM((devices, part, lines[0].shape[1]), jnp.bfloat16)],
        compiler_params=params(48),
        name="add_delta",
    )(me, base, up, *lines)


def per_device(
    devices,
    hidden,
    input_norm_scale,
    query_key_value_weight,
    projection_bias,
    rotated_key_cache,
    past_value_cache,
    lengths,
    row_adapter_index,
    output_weight,
    adapter_down_weight,
    adapter_up_weight,
):
    rows = hidden.shape[0]
    me = lax.axis_index("tensor").astype(jnp.int32).reshape(1)
    half = HEAD_SIZE // 2
    inv = ROPE_BASE ** (-(jnp.arange(half, dtype=jnp.float32) * 2.0 / HEAD_SIZE))
    angle = lengths.astype(jnp.float32)[:, None] * inv[None, :]
    cosine, sine = jnp.cos(angle), jnp.sin(angle)
    cosine = jnp.concatenate([cosine, cosine], axis=1)
    sine = jnp.concatenate([-sine, sine], axis=1)
    down = jnp.transpose(adapter_down_weight, (0, 2, 1))
    up = adapter_up_weight.reshape(-1, adapter_up_weight.shape[2])

    bias = projection_bias.reshape(1, -1)
    chunks, held = gather_chunks(
        norm_chunk(hidden, input_norm_scale),
        devices,
        lambda chunk: hold(query_key_value_weight, chunk, (me,), 40, "hold_qkv"),
    )
    mine = unpack(chunks, rows, hidden.shape[1], False)
    theirs = across(mine, devices)
    own, keys = qkv_own(mine, held, rotated_key_cache)
    parts, values = qkv_project(own, theirs, held, bias, past_value_cache, devices, rows)
    parts = exchange(parts, rows, devices)
    chunk = attend(
        me, lengths, row_adapter_index, parts, cosine, sine, keys, values, devices
    )
    chunks, held = gather_chunks(
        chunk, devices, lambda chunk: hold(output_weight, chunk, (), 42, "hold_output")
    )
    mine = unpack(chunks, rows, QUERY_HEADS * HEAD_SIZE, True)
    theirs = across(mine, devices)
    own_part = shrink_own(mine, down)
    own = own_rows(mine, held, "base_own")
    coords = shrink(me, own_part, mine, theirs, down, own, devices)
    lines = gather_coords(coords, devices)
    base = base_project(me, own, theirs, held, devices)
    projected = add_delta(me, base, lines, up, devices, rows)
    projected = lax.all_to_all(projected, "tensor", split_axis=0, concat_axis=0, tiled=True)
    return jnp.transpose(projected, (1, 0, 2)).reshape(rows, -1)


def solution(mesh):
    in_specs = (
        P(("group", "tensor"), None),
        P(),
        P(None, "tensor"),
        P("tensor"),
        P(("group", "tensor"), None, None),
        P(("group", "tensor"), None, None),
        P(("group", "tensor")),
        P(("group", "tensor")),
        P(None, "tensor"),
        P("tensor", None, None),
        P(None, None, "tensor"),
    )
    out_specs = P(("group", "tensor"), None)
    return jax.shard_map(
        functools.partial(per_device, mesh.shape["tensor"]),
        mesh=mesh,
        in_specs=in_specs,
        out_specs=out_specs,
        check_vma=False,
    )
```

```python
import functools

import jax
import jax.numpy as jnp
from jax import lax
from jax.experimental import pallas as pl
from jax.experimental.pallas import tpu as pltpu
from jax.sharding import PartitionSpec as P

QUERY_HEADS = 64
KVH = 8
HEAD_SIZE = 128
ADAPTER_RANK = 16
GROUPS = QUERY_HEADS // KVH

EPS = 1e-06
ROPE_BASE = 1000000.0

BLOCKS = 8
LANES = 128
MIB = 1 << 20

VMEM = pl.BlockSpec(memory_space=pltpu.VMEM)
HBM = pl.BlockSpec(memory_space=pltpu.HBM)
ANY = pl.BlockSpec(memory_space=pl.ANY)
SMEM = pl.BlockSpec(memory_space=pltpu.SMEM)


def params(mib):
    return pltpu.CompilerParams(vmem_limit_bytes=mib * MIB)


def factors(chips):
    inner = 1
    while inner * inner * 4 <= chips and chips % (inner * 2) == 0:
        inner *= 2
    return chips // inner, inner


def slot_chips(devices, me):
    outer, inner = factors(devices // 2)
    return [lax.div(place(devices, me, k, m, 0), 2) for m in range(inner) for k in range(outer)]


def steps(count, unrolled, body):
    if unrolled:
        for i in range(count):
            body(i)
    else:
        lax.fori_loop(0, count, lambda i, _: (body(i), 0)[1], 0)


def gather_chunks(chunk, devices, meanwhile):
    outer, inner = factors(devices // 2)

    line = [chunk] + [move(chunk, devices, k, 0, 0) for k in range(1, outer)]
    held, line[outer // 4] = meanwhile(line[outer // 4])
    slots = {}
    for k in range(outer):
        for m in range(1, inner):
            slots[k, m] = move(line[k], devices, 0, m, 0)
    for k in range(outer):
        slots[k, 0] = line[k]
    return [slots[k, m] for m in range(inner) for k in range(outer)], held


def neighbours(devices):
    return [(m, c) for m in range(factors(devices // 2)[1]) for c in range(2)]


def place(devices, d, k, m, c):
    outer, inner = factors(devices // 2)
    return 2 * ((d // 2 // inner ^ k) * inner + (d // 2 % inner ^ m)) + (d % 2 ^ c)


def move(x, devices, k, m, c):
    return lax.ppermute(
        x, "tensor", [(d, place(devices, d, k, m, c)) for d in range(devices)]
    )


def join_kernel(*refs):
    parts, out_ref = refs[:-1], refs[-1]
    rows = parts[0].shape[0]
    for at, part in enumerate(parts):
        out_ref[at * rows : (at + 1) * rows, :] = part[...]


def gather_coords(coords, devices):
    around = [coords if mc == (0, 0) else move(coords, devices, 0, *mc) for mc in neighbours(devices)]
    rows, cols = coords.shape
    joined = pl.pallas_call(
        join_kernel,
        out_shape=jax.ShapeDtypeStruct((len(around) * rows, cols), coords.dtype),
        in_specs=[VMEM] * len(around),
        out_specs=VMEM,
        compiler_params=params(16),
        name="join_coords",
    )(*around)
    outer = factors(devices // 2)[0]
    return [joined] + [move(joined, devices, k, 0, 0) for k in range(1, outer)]


def turn_kernel(rows, *refs):
    wide, stage = refs[-2:]
    outer = wide.shape[0]
    parts, outs = refs[:outer], refs[outer:-2]
    for k, part in enumerate(parts):
        wide[k] = part[...].astype(jnp.float32)
    for at, out_ref in enumerate(outs):
        for k in range(outer):
            stage[k * rows : (k + 1) * rows, :] = wide[k, at * rows : (at + 1) * rows, :]
        out_ref[...] = stage[...].astype(jnp.bfloat16)


def exchange(parts, rows, devices):
    outer, _ = factors(devices // 2)
    around = neighbours(devices)
    cols = parts[0].shape[1]
    arrived = [parts[0]] + [move(parts[k], devices, k, 0, 0) for k in range(1, outer)]
    turned = pl.pallas_call(
        functools.partial(turn_kernel, rows),
        out_shape=[jax.ShapeDtypeStruct((outer * rows, cols), parts[0].dtype) for _ in around],
        in_specs=[VMEM] * outer,
        out_specs=[VMEM] * len(around),
        scratch_shapes=[
            pltpu.VMEM((outer, *parts[0].shape), jnp.float32),
            pltpu.VMEM((outer * rows, cols), jnp.float32),
        ],
        compiler_params=params(16),
        name="turn",
    )(*arrived)
    return [x if mc == (0, 0) else move(x, devices, 0, *mc) for x, mc in zip(turned, around)]


def across(x, devices):
    return move(x, devices, 0, 0, 1)


def write_chunk(stage, rows, out_ref):
    block = stage.shape[1]
    for g in range(BLOCKS * rows // 8):
        out_ref[:, g * block : (g + 1) * block] = stage[8 * g : 8 * g + 8, :].astype(jnp.bfloat16)


def write_ids(ids_ref, rows, out_ref):
    sub = lax.broadcasted_iota(jnp.int32, (8, LANES), 0)
    ids = jnp.full((8, LANES), -1.0, jnp.float32)
    for r in range(rows):
        ids = jnp.where(sub == r, ids_ref[r].astype(jnp.float32), ids)
    out_ref[:, out_ref.shape[1] - LANES :] = ids.astype(jnp.bfloat16)


def norm_kernel(x_hbm, gain_hbm, out_ref, x_ref, gain_ref, sems, stage):
    copies = [
        pltpu.make_async_copy(x_hbm, x_ref, sems.at[0]),
        pltpu.make_async_copy(gain_hbm, gain_ref, sems.at[1]),
    ]
    for copy in copies:
        copy.start()
    for copy in copies:
        copy.wait()
    rows, width = x_ref.shape
    block = width // BLOCKS
    total = jnp.zeros((rows, LANES), jnp.float32)
    for c in range(width // LANES):
        x = x_ref[:, c * LANES : (c + 1) * LANES].astype(jnp.float32)
        total = total + x * x
    factor = lax.rsqrt(jnp.sum(total, axis=-1, keepdims=True) / width + EPS)
    for c in range(width // LANES):
        x = x_ref[:, c * LANES : (c + 1) * LANES].astype(jnp.float32)
        gain = gain_ref[c : c + 1, :].astype(jnp.float32)
        j, lane = c * LANES // block, c * LANES % block
        stage[j * rows : (j + 1) * rows, lane : lane + LANES] = x * factor * gain
    write_chunk(stage, rows, out_ref)


def norm_chunk(hidden, gain):
    rows, width = hidden.shape
    return pl.pallas_call(
        norm_kernel,
        out_shape=jax.ShapeDtypeStruct((8, rows * width // 8), jnp.bfloat16),
        in_specs=[HBM, HBM],
        out_specs=VMEM,
        scratch_shapes=[
            pltpu.VMEM((rows, width), jnp.bfloat16),
            pltpu.VMEM((width // LANES, LANES), jnp.bfloat16),
            pltpu.SemaphoreType.DMA((2,)),
            pltpu.VMEM((BLOCKS * rows, width // BLOCKS), jnp.float32),
        ],
        compiler_params=params(16),
        name="norm_chunk",
    )(hidden, gain.reshape(width // LANES, LANES))


def unpack_kernel(chips, rows, with_ids, *refs):
    chunks = refs[:chips]
    left, stage = refs[chips:]
    block = stage.shape[-1]
    small = chips <= 8
    for pair in range(chips // 2):
        turn = pair % 2
        for place in range(2):
            chunk = chunks[2 * pair + place]

            def widen(g, chunk=chunk, turn=turn, place=place):
                lane = g * block if small else pl.multiple_of(g * block, block)
                at = 8 * g if small else pl.multiple_of(8 * g, 8)
                wide = chunk[:, pl.ds(lane, block)].astype(jnp.float32)
                stage[turn, place, pl.ds(at, 8), :] = wide

            steps(BLOCKS * rows // 8, small, widen)
        for j in range(BLOCKS):
            both = [stage[turn, place, j * rows : j * rows + 8, :] for place in range(2)]
            left[j, 16 * pair : 16 * pair + 16, :] = jnp.concatenate(both, axis=0).astype(
                jnp.bfloat16
            )
        if with_ids:
            at = BLOCKS * rows // 8 * block
            both = [chunks[2 * pair + place][:, at : at + LANES] for place in range(2)]
            both = jnp.concatenate([ids.astype(jnp.float32) for ids in both], axis=0)
            left[BLOCKS, 16 * pair : 16 * pair + 16, :LANES] = both.astype(jnp.bfloat16)


def unpack(chunks, rows, width, with_ids):
    chips = len(chunks)
    block = width // BLOCKS
    return pl.pallas_call(
        functools.partial(unpack_kernel, chips, rows, with_ids),
        out_shape=jax.ShapeDtypeStruct((BLOCKS + with_ids, chips * 8, block), jnp.bfloat16),
        in_specs=[VMEM] * chips,
        out_specs=VMEM,
        scratch_shapes=[pltpu.VMEM((2, 2, BLOCKS * rows + 8, block), jnp.float32)],
        compiler_params=params(32),
        name="unpack",
    )(*chunks)


def hold_kernel(count, *refs):
    weight, held, _, sems = refs[count:]
    block = weight.shape[0] // BLOCKS
    copies = [
        pltpu.make_async_copy(
            weight.at[pl.ds(j * block, block), :], held.at[pl.ds(j * block, block), :], sems.at[j]
        )
        for j in range(BLOCKS)
    ]
    for copy in copies:
        copy.start()
    for copy in copies:
        copy.wait()


def hold(weight, chunk, after, mib, name):
    arrays = (chunk, *after)
    return pl.pallas_call(
        functools.partial(hold_kernel, len(arrays)),
        out_shape=(
            jax.ShapeDtypeStruct(weight.shape, weight.dtype),
            jax.ShapeDtypeStruct(chunk.shape, chunk.dtype),
        ),
        in_specs=[ANY] * len(arrays) + [HBM],
        out_specs=(VMEM, ANY),
        scratch_shapes=[pltpu.SemaphoreType.DMA((BLOCKS,))],
        input_output_aliases={0: 1},
        compiler_params=params(mib),
        cost_estimate=pl.CostEstimate(flops=0, bytes_accessed=4 * weight.size, transcendentals=0),
        name=name,
    )(*arrays, weight)


def multiply(left, held, acc):
    block = left.shape[2]
    acc[...] = jnp.zeros_like(acc)
    for j in range(BLOCKS):
        acc[...] += jnp.dot(
            left[j], held[j * block : (j + 1) * block, :], preferred_element_type=jnp.float32
        )


def own_rows(left, held, name):
    rows, cols = left.shape[1], held.shape[1]
    return pl.pallas_call(
        multiply,
        out_shape=jax.ShapeDtypeStruct((rows, cols), jnp.float32),
        in_specs=[VMEM, VMEM],
        out_specs=VMEM,
        compiler_params=params(40),
        cost_estimate=pl.CostEstimate(
            flops=2 * rows * held.size, bytes_accessed=2 * held.size, transcendentals=0
        ),
        name=name,
    )(left, held)


def cache_copies(cache, kept, sems):
    return [
        pltpu.make_async_copy(cache.at[r], kept.at[r], sems.at[r]) for r in range(cache.shape[0])
    ]


def qkv_own_kernel(left, held, cache, acc, kept, sems):
    copies = cache_copies(cache, kept, sems)
    for copy in copies:
        copy.start()
    multiply(left, held, acc)
    for copy in copies:
        copy.wait()


def qkv_own(left, held, cache):
    rows, cols = left.shape[1], held.shape[1]
    return pl.pallas_call(
        qkv_own_kernel,
        out_shape=(
            jax.ShapeDtypeStruct((rows, cols), jnp.float32),
            jax.ShapeDtypeStruct(cache.shape, cache.dtype),
        ),
        in_specs=[VMEM, VMEM, HBM],
        out_specs=(VMEM, VMEM),
        scratch_shapes=[pltpu.SemaphoreType.DMA((cache.shape[0],))],
        compiler_params=params(32),
        cost_estimate=pl.CostEstimate(
            flops=2 * rows * held.size, bytes_accessed=2 * held.size, transcendentals=0
        ),
        name="qkv_own",
    )(left, held, cache)


def qkv_kernel(devices, rows, bias_ref, own_ref, left, held, cache, *refs):
    outer, inner = factors(devices // 2)
    outs, (kept, acc, stage, sems) = refs[:outer], refs[outer:]
    copies = cache_copies(cache, kept, sems)
    for copy in copies:
        copy.start()
    multiply(left, held, acc)
    bias = bias_ref[...].astype(jnp.float32)
    products = own_ref, acc
    for k in range(outer):
        for at, (m, c) in enumerate(neighbours(devices)):
            slot = m * outer + k
            mine = products[c][8 * slot : 8 * slot + rows, :]
            stage[at * rows : (at + 1) * rows, :] = mine + bias
        outs[k][...] = stage[...].astype(jnp.bfloat16)
    for copy in copies:
        copy.wait()


def qkv_project(own, left, held, bias, cache, devices, rows):
    outer, inner = factors(devices // 2)
    cols = own.shape[1]
    part = jax.ShapeDtypeStruct((2 * inner * rows, cols), jnp.bfloat16)
    *parts, kept = pl.pallas_call(
        functools.partial(qkv_kernel, devices, rows),
        out_shape=[part] * outer + [jax.ShapeDtypeStruct(cache.shape, cache.dtype)],
        in_specs=[VMEM, VMEM, VMEM, VMEM, HBM],
        out_specs=[VMEM] * (outer + 1),
        scratch_shapes=[
            pltpu.VMEM(own.shape, jnp.float32),
            pltpu.VMEM((2 * inner * rows, cols), jnp.float32),
            pltpu.SemaphoreType.DMA((cache.shape[0],)),
        ],
        compiler_params=params(24),
        name="qkv_project",
    )(bias, own, left, held, cache)
    return parts, kept


def head_of(ordered, h):
    cols = ordered.shape[2]
    pieces = []
    at, end = h * HEAD_SIZE, (h + 1) * HEAD_SIZE
    while at < end:
        d, lane = at // cols, at % cols
        width = min(end - at, cols - lane)
        pieces.append(ordered[d, :, lane : lane + width])
        at += width
    return pieces[0] if len(pieces) == 1 else jnp.concatenate(pieces, axis=1)


def in_order(devices, me, parts, wide, ordered):
    rows = ordered.shape[1]
    for at, (m, c) in enumerate(neighbours(devices)):
        wide[at] = parts[at][...].astype(jnp.float32)
        for k in range(wide.shape[1] // rows):
            ordered[place(devices, me, k, m, c)] = wide[at, k * rows : (k + 1) * rows, :]


def attend_kernel(devices, rows, me_ref, len_ref, ids_ref, cos_ref, sin_ref, keys, values, *refs):
    parts, (out_ref, wide, ordered, heads, mixed, stage) = refs[:-6], refs[-6:]
    total_heads = QUERY_HEADS + 2 * KVH
    half = HEAD_SIZE // 2
    in_order(devices, me_ref[0], parts, wide, ordered)
    for h in range(total_heads):
        heads[pl.ds(h, rows, stride=total_heads), :] = head_of(ordered, h)
    scale = 1.0 / HEAD_SIZE**0.5
    upper = lax.broadcasted_iota(jnp.int32, (2 * GROUPS, HEAD_SIZE), 0) < GROUPS
    for r in range(rows):
        base = r * total_heads
        turned = heads[base : base + QUERY_HEADS + KVH, :]
        cosine = cos_ref[r : r + 1, :]
        sine = sin_ref[r : r + 1, :]
        turned = (turned * cosine + pltpu.roll(turned, half, 1) * sine).astype(jnp.bfloat16)
        query = turned[:QUERY_HEADS]
        query_f = query.astype(jnp.float32)
        new_key = turned[QUERY_HEADS:].astype(jnp.float32)
        new_value = heads[base + QUERY_HEADS + KVH : base + total_heads, :]
        scores = []
        own = []
        for k in range(0, KVH, 2):
            mine = slice(k * GROUPS, (k + 2) * GROUPS)
            both = query_f[mine]
            wide_query = jnp.concatenate(
                [jnp.where(upper, both, 0.0), jnp.where(upper, 0.0, both)], axis=1
            ).astype(jnp.bfloat16)
            scores.append(
                lax.dot_general(
                    wide_query,
                    keys[r, :, k * HEAD_SIZE : (k + 2) * HEAD_SIZE],
                    (((1,), (1,)), ((), ())),
                    preferred_element_type=jnp.float32,
                )
            )
        for k in range(KVH):
            mine = slice(k * GROUPS, (k + 1) * GROUPS)
            own.append(jnp.sum(query_f[mine] * new_key[k : k + 1], axis=-1, keepdims=True))
        score = jnp.concatenate(scores, axis=0) * scale
        own = jnp.concatenate(own, axis=0) * scale
        valid = lax.broadcasted_iota(jnp.int32, score.shape, 1) < len_ref[r]
        score = jnp.where(valid, score, -1e30)
        top = jnp.maximum(jnp.max(score, axis=-1, keepdims=True), own)
        expo = jnp.exp(score - top)
        expo_own = jnp.exp(own - top)
        total = jnp.sum(expo, axis=-1, keepdims=True) + expo_own
        weight = (expo * (1.0 / total)).astype(jnp.bfloat16)
        weight_own = (expo_own / total).astype(jnp.bfloat16).astype(jnp.float32)
        for k in range(0, KVH, 2):
            both = jnp.dot(
                weight[k * GROUPS : (k + 2) * GROUPS],
                values[r, :, k * HEAD_SIZE : (k + 2) * HEAD_SIZE],
                preferred_element_type=jnp.float32,
            )
            for i in range(2):
                mine = slice((k + i) * GROUPS, (k + i + 1) * GROUPS)
                part = both[i * GROUPS : (i + 1) * GROUPS, i * HEAD_SIZE : (i + 1) * HEAD_SIZE]
                part = part + weight_own[mine] * new_value[k + i : k + i + 1]
                at = r * QUERY_HEADS + (k + i) * GROUPS
                mixed[at : at + GROUPS, :] = part
    per_block = QUERY_HEADS // BLOCKS
    for h in range(QUERY_HEADS):
        j, lane = h // per_block, h % per_block
        stage[j * rows : (j + 1) * rows, lane * HEAD_SIZE : (lane + 1) * HEAD_SIZE] = mixed[
            pl.ds(h, rows, stride=QUERY_HEADS), :
        ]
    write_chunk(stage, rows, out_ref)
    write_ids(ids_ref, rows, out_ref)


def attend(me, lengths, ids, parts, cosine, sine, keys, values, devices):
    rows, capacity, width = keys.shape
    total_heads = QUERY_HEADS + 2 * KVH
    features = QUERY_HEADS * HEAD_SIZE
    return pl.pallas_call(
        functools.partial(attend_kernel, devices, rows),
        out_shape=jax.ShapeDtypeStruct((8, rows * features // 8 + LANES), jnp.bfloat16),
        in_specs=[SMEM] * 3 + [VMEM] * (4 + len(parts)),
        out_specs=VMEM,
        scratch_shapes=[
            pltpu.VMEM((len(parts), *parts[0].shape), jnp.float32),
            pltpu.VMEM((devices, rows, parts[0].shape[1]), jnp.float32),
            pltpu.VMEM((rows * total_heads, HEAD_SIZE), jnp.float32),
            pltpu.VMEM((rows * QUERY_HEADS, HEAD_SIZE), jnp.float32),
            pltpu.VMEM((BLOCKS * rows, features // BLOCKS), jnp.float32),
        ],
        compiler_params=params(24),
        name="attend",
    )(me, lengths, ids, cosine, sine, keys, values, *parts)


def times_down(down_ref, left, write):
    stored, rank, features = down_ref.shape
    block = features // BLOCKS
    for s in range(stored):
        part = jnp.zeros((rank, left.shape[1]), jnp.float32)
        for j in range(BLOCKS):
            part += lax.dot_general(
                down_ref[s, :, j * block : (j + 1) * block],
                left[j],
                (((1,), (1,)), ((), ())),
                preferred_element_type=jnp.float32,
            )
        write(slice(s * rank, (s + 1) * rank), part)


def shrink_own_kernel(down_ref, left, out_ref):
    def write(at, part):
        out_ref[at, :] = part

    times_down(down_ref, left, write)


def shrink_own(left, down):
    stored, rank, features = down.shape
    return pl.pallas_call(
        shrink_own_kernel,
        out_shape=jax.ShapeDtypeStruct((stored * rank, left.shape[1]), jnp.float32),
        in_specs=[VMEM, VMEM],
        out_specs=VMEM,
        compiler_params=params(48),
        cost_estimate=pl.CostEstimate(
            flops=2 * left.size * stored * rank, bytes_accessed=2 * left.size, transcendentals=0
        ),
        name="shrink_own",
    )(down, left)


def shrink_kernel(
    devices, me_ref, down_ref, own_part, own, other, after, coords_ref, ids, place_of, total
):
    me = me_ref[0]
    stored, rank, _ = down_ref.shape
    rows = own.shape[1]
    total[:, :rows] = own_part[...]

    def write(at, part):
        total[at, rows:] = part

    times_down(down_ref, other, write)
    for c, left in enumerate((own, other)):
        ids[c * rows : (c + 1) * rows, :] = left[BLOCKS, :, :LANES].astype(jnp.float32)
    row_ids = jnp.transpose(ids[...])[: stored * rank, :].astype(jnp.int32)
    adapter = lax.broadcasted_iota(jnp.int32, total.shape, 0) // rank + me * stored
    coords = jnp.where(row_ids == adapter, total[...], 0.0).astype(jnp.bfloat16)
    core = lax.rem(me, 2)
    sub = lax.broadcasted_iota(jnp.int32, (8, LANES), 0)
    for slot, chip in enumerate(slot_chips(devices, me)):
        for c, place in ((0, core), (1, 1 - core)):
            at = c * rows + 8 * slot
            place_of[at : at + 8, :] = sub + (2 * chip + place) * 8
    target = lax.broadcasted_iota(jnp.int32, (2 * rows, 2 * rows), 1)
    move = jnp.where(place_of[:, :1] == target, 1.0, 0.0).astype(jnp.bfloat16)
    coords = jnp.dot(coords, move, preferred_element_type=jnp.float32).astype(jnp.bfloat16)
    coords_ref[...] = coords


def shrink(me, own_part, own, other, down, after, devices):
    stored, rank, features = down.shape
    rows = devices * 8
    return pl.pallas_call(
        functools.partial(shrink_kernel, devices),
        out_shape=jax.ShapeDtypeStruct((stored * rank, rows), jnp.bfloat16),
        in_specs=[SMEM, VMEM, VMEM, VMEM, VMEM, ANY],
        out_specs=VMEM,
        scratch_shapes=[
            pltpu.VMEM((rows, LANES), jnp.float32),
            pltpu.VMEM((rows, LANES), jnp.int32),
            pltpu.VMEM((stored * rank, rows), jnp.float32),
        ],
        compiler_params=params(48),
        name="shrink",
    )(me, down, own_part, own, other, after)


def base_kernel(devices, me_ref, own_ref, left, held, out_ref, acc):
    multiply(left, held, acc)
    core = lax.rem(me_ref[0], 2)
    for slot, chip in enumerate(slot_chips(devices, me_ref[0])):
        mine = slice(8 * slot, 8 * slot + 8)
        at = pl.multiple_of((2 * chip + core) * 8, 8)
        out_ref[pl.ds(at, 8), :] = own_ref[mine, :]
        at = pl.multiple_of((2 * chip + 1 - core) * 8, 8)
        out_ref[pl.ds(at, 8), :] = acc[mine, :]


def base_project(me, own, left, held, devices):
    rows, cols = own.shape
    return pl.pallas_call(
        functools.partial(base_kernel, devices),
        out_shape=jax.ShapeDtypeStruct((2 * rows, cols), jnp.float32),
        in_specs=[SMEM, VMEM, VMEM, VMEM],
        out_specs=VMEM,
        scratch_shapes=[pltpu.VMEM(own.shape, jnp.float32)],
        compiler_params=params(40),
        cost_estimate=pl.CostEstimate(
            flops=2 * rows * held.size, bytes_accessed=2 * held.size, transcendentals=0
        ),
        name="base_project",
    )(me, own, left, held)


def add_kernel(devices, rows, me_ref, base_ref, up_ref, *refs):
    lines, (out_ref, coords) = refs[:-2], refs[-2:]
    part = coords.shape[1]
    for k, line in enumerate(lines):
        for at, (m, c) in enumerate(neighbours(devices)):
            coords[place(devices, me_ref[0], k, m, c)] = line[at * part : (at + 1) * part, :]
    delta = lax.dot_general(
        coords[...].reshape(devices * part, coords.shape[2]),
        up_ref[...],
        (((0,), (0,)), ((), ())),
        preferred_element_type=jnp.float32,
    )
    projected = base_ref[...] + delta
    for d in range(devices):
        out_ref[d] = projected[8 * d : 8 * d + rows, :].astype(jnp.bfloat16)


def add_delta(me, base, lines, up, devices, rows):
    part = up.shape[0] // devices
    return pl.pallas_call(
        functools.partial(add_kernel, devices, rows),
        out_shape=jax.ShapeDtypeStruct((devices, rows, base.shape[1]), jnp.bfloat16),
        in_specs=[SMEM, VMEM, VMEM] + [VMEM] * len(lines),
        out_specs=VMEM,
        scratch_shapes=[pltpu.VMEM((devices, part, lines[0].shape[1]), jnp.bfloat16)],
        compiler_params=params(48),
        name="add_delta",
    )(me, base, up, *lines)


def per_device(
    devices,
    hidden,
    input_norm_scale,
    query_key_value_weight,
    projection_bias,
    rotated_key_cache,
    past_value_cache,
    lengths,
    row_adapter_index,
    output_weight,
    adapter_down_weight,
    adapter_up_weight,
):
    rows = hidden.shape[0]
    me = lax.axis_index("tensor").astype(jnp.int32).reshape(1)
    half = HEAD_SIZE // 2
    inv = ROPE_BASE ** (-(jnp.arange(half, dtype=jnp.float32) * 2.0 / HEAD_SIZE))
    angle = lengths.astype(jnp.float32)[:, None] * inv[None, :]
    cosine, sine = jnp.cos(angle), jnp.sin(angle)
    cosine = jnp.concatenate([cosine, cosine], axis=1)
    sine = jnp.concatenate([-sine, sine], axis=1)
    down = jnp.transpose(adapter_down_weight, (0, 2, 1))
    up = adapter_up_weight.reshape(-1, adapter_up_weight.shape[2])

    bias = projection_bias.reshape(1, -1)
    chunks, held = gather_chunks(
        norm_chunk(hidden, input_norm_scale),
        devices,
        lambda chunk: hold(query_key_value_weight, chunk, (me,), 40, "hold_qkv"),
    )
    mine = unpack(chunks, rows, hidden.shape[1], False)
    theirs = across(mine, devices)
    own, keys = qkv_own(mine, held, rotated_key_cache)
    parts, values = qkv_project(own, theirs, held, bias, past_value_cache, devices, rows)
    parts = exchange(parts, rows, devices)
    chunk = attend(
        me, lengths, row_adapter_index, parts, cosine, sine, keys, values, devices
    )
    chunks, held = gather_chunks(
        chunk, devices, lambda chunk: hold(output_weight, chunk, (), 42, "hold_output")
    )
    mine = unpack(chunks, rows, QUERY_HEADS * HEAD_SIZE, True)
    theirs = across(mine, devices)
    own_part = shrink_own(mine, down)
    own = own_rows(mine, held, "base_own")
    coords = shrink(me, own_part, mine, theirs, down, own, devices)
    lines = gather_coords(coords, devices)
    base = base_project(me, own, theirs, held, devices)
    projected = add_delta(me, base, lines, up, devices, rows)
    projected = lax.all_to_all(projected, "tensor", split_axis=0, concat_axis=0, tiled=True)
    return jnp.transpose(projected, (1, 0, 2)).reshape(rows, -1)


def solution(mesh):
    in_specs = (
        P(("group", "tensor"), None),
        P(),
        P(None, "tensor"),
        P("tensor"),
        P(("group", "tensor"), None, None),
        P(("group", "tensor"), None, None),
        P(("group", "tensor")),
        P(("group", "tensor")),
        P(None, "tensor"),
        P("tensor", None, None),
        P(None, None, "tensor"),
    )
    out_specs = P(("group", "tensor"), None)
    return jax.shard_map(
        functools.partial(per_device, mesh.shape["tensor"]),
        mesh=mesh,
        in_specs=in_specs,
        out_specs=out_specs,
        check_vma=False,
    )
```
